256 devices in a mesh: fsdp: 128 (over x, z_hi, y, core), tp: 2 (over z_lo).
Axes of the slice: x: 4, y: 4, z: 8 (z_hi: 4, z_lo: 2; z = z_hi * 2 + z_lo), core: 2. Of those that a mesh axis runs over, the one named last changes fastest.
Arguments:
- hidden_in: bfloat16 [49152, 4096], P('fsdp', 'tp'), may hold values from -6 to 6
- attn_first: bfloat16 [49152, 2048], P('fsdp', 'tp'), may hold values from -6 to 6
- attn_second: bfloat16 [32768, 2048], P('fsdp', 'tp'), may hold values from -6 to 6
- attn_third: bfloat16 [16384, 2048], P('fsdp', 'tp'), may hold values from -6 to 6
- out_weight: bfloat16 [4096, 2048], P('fsdp', 'tp'), may hold values from -0.125 to 0.125
- router: float32 [4096], replicated, may hold values from -0.09375 to 0.09375
- kept_second: int32 [128, 2], P('fsdp'), may hold values from -1 to 2, as said below
- kept_third: int32 [128, 1], P('fsdp'), may hold values from -1 to 2, as said below
- grad_out: bfloat16 [49152, 4096], P('fsdp', 'tp'), may hold values from -24 to 24
Outputs:
- grad_in: bfloat16 [49152, 4096], P('fsdp', 'tp')
- grad_first: bfloat16 [49152, 2048], P('fsdp', 'tp')
- grad_second: bfloat16 [32768, 2048], P('fsdp', 'tp')
- grad_third: bfloat16 [16384, 2048], P('fsdp', 'tp')
- weight_grad: bfloat16 [4096, 2048], P('fsdp', 'tp')
- router_grad: float32 [4096], replicated
The draws below stay inside these ranges and needn't reach their ends.
Inputs may be any that keep to these rules, and one draw needn't show every extreme that they name: `kept_second`: for each sequence, the blocks that take the second recursion, distinct, followed by -1 in the empty slots; every sequence keeps one or more, and the first sequence fills all 2 slots. `kept_third`: for each sequence, the first entries of its kept_second list (so its blocks take the second recursion too), followed by -1; a sequence may keep none, and the first sequence fills all 1 slots.
All inputs are finite; a program needn't handle non-finite values.
Results may differ from the reference program's by a relative error of at most 0.0053.
Values may be sent and summed in bfloat16 or wider, within the bound.
No kernel may reach another device: no remote copies, remote signals or barrier semaphores. Data moves between devices by JAX's collectives and lax.ppermute only.
A program may use at most 128 MiB of HBM per device.

```python
import jax
import jax.numpy as jnp
from jax import lax

D = 4096
HW = 2048
BLOCK = 128
NB = 3
CAP2 = 2
CAP3 = 1
SEQS = 128
TOKENS = 49152


def kept_lists(key):
    scores = jax.random.randint(jax.random.fold_in(key, 5), (SEQS, NB), 0, 2 ** 20) * NB + jnp.arange(NB, dtype=jnp.int32)[None, :]
    order = jnp.argsort(scores, axis=1).astype(jnp.int32)
    second_count = jax.random.randint(jax.random.fold_in(key, 11), (SEQS,), 1, CAP2 + 1)
    second_count = second_count.at[0].set(CAP2)
    third_count = jax.random.randint(jax.random.fold_in(key, 13), (SEQS,), 0, CAP3 + 1)
    third_count = jnp.minimum(third_count, second_count).at[0].set(CAP3)
    return (order, second_count, third_count)


def draw_kept_second(key, part):
    order, second_count, third_count = kept_lists(key)
    slots = jnp.arange(CAP2, dtype=jnp.int32)[None, :]
    return jnp.where(slots < second_count[:, None], order[:, :CAP2], -1).astype(jnp.int32)


def draw_kept_third(key, part):
    order, second_count, third_count = kept_lists(key)
    slots = jnp.arange(CAP3, dtype=jnp.int32)[None, :]
    return jnp.where(slots < third_count[:, None], order[:, :CAP3], -1).astype(jnp.int32)


def raised(array, own_key, source, target, shards_of, factor):
    def block_of(dim):
        return (jnp.arange(array.shape[dim]) // (array.shape[dim] // shards_of)).reshape((-1,) + (1,) * (array.ndim - 1 - dim))

    first = jax.random.permutation(own_key, shards_of)[block_of(target)]
    second = (block_of(target) + shards_of // 2) % shards_of
    return jnp.where((block_of(source) == first) | (block_of(source) == second), factor * array, array)


def block_levels(rng, extent, split, smallest, largest):
    level = 1.0
    for axis_at, shards_of in split:
        draws = jax.random.uniform(jax.random.fold_in(jax.random.fold_in(rng, 6), axis_at), (shards_of,), jnp.float32, smallest / len(split), largest / len(split))
        level = level * jnp.repeat(jnp.exp(draws), extent[axis_at] // shards_of).reshape((-1,) + (1,) * (len(extent) - 1 - axis_at))
    return level


def scatter_about(own_key, shape, spread, reach, shards=(), kind=jnp.bfloat16):
    drawn = spread * jax.random.normal(own_key, shape, jnp.float32)
    if shards:
        drawn = drawn * block_levels(own_key, shape, shards, -0.22, 0.18)
    return jnp.clip(drawn, -reach, reach).astype(kind)


def bell_draw_with(key, extent, width, most, cuts, heavy, kind=jnp.bfloat16):
    drawn = width * jax.random.normal(key, extent, jnp.float32)
    if cuts:
        drawn = drawn * block_levels(key, extent, cuts, -0.22, 0.18)
    return jnp.clip(raised(drawn, jax.random.fold_in(key, 3), *heavy), -most, most).astype(kind)


def setup_inputs(seed: int = 0) -> dict:
    splits = jax.random.split(jax.random.key(seed), 10)
    return {
        "hidden_in": scatter_about(splits[0], (TOKENS, D), 1.0, 6.0, ((0, 128), (1, 2))),
        "attn_first": scatter_about(splits[1], (TOKENS, HW), 1.0, 6.0, ((0, 128), (1, 2))),
        "attn_second": scatter_about(splits[2], (SEQS * CAP2 * BLOCK, HW), 1.0, 6.0, ((0, 128), (1, 2))),
        "attn_third": scatter_about(splits[3], (SEQS * CAP3 * BLOCK, HW), 1.0, 6.0, ((0, 128), (1, 2))),
        "out_weight": scatter_about(splits[4], (D, HW), HW ** -0.5, 0.125, ((0, 128), (1, 2))),
        "router": scatter_about(splits[5], (D,), D ** -0.5, 0.09375, (), jnp.float32),
        "kept_second": draw_kept_second(jax.random.fold_in(splits[9], 71), 0),
        "kept_third": draw_kept_third(jax.random.fold_in(splits[9], 71), 0),
        "grad_out": bell_draw_with(splits[8], (TOKENS, D), 1.0, 24.0, ((0, 128), (1, 2)), (0, 1, 128, 5.5)),
    }


HIGH = lax.Precision.HIGHEST


def slot_layout(kept):
    safe_ids = jnp.maximum(kept, 0)
    sequence = jnp.arange(kept.shape[0], dtype=jnp.int32)[:, None]
    first_row = (sequence * NB + safe_ids) * BLOCK
    row_ids = first_row[:, :, None] + jnp.arange(BLOCK, dtype=jnp.int32)[None, None, :]
    live = jnp.broadcast_to((kept >= 0)[:, :, None], row_ids.shape).astype(jnp.float32)
    return row_ids.reshape(-1).astype(jnp.int32), live.reshape(-1)


def to_tokens(values, row_ids, live):
    return jnp.zeros((TOKENS,), jnp.float32).at[row_ids].add(values * live)


def reference(hidden_in, attn_first, attn_second, attn_third, out_weight, router, kept_second, kept_third, grad_out):
    weight32 = out_weight.astype(jnp.float32)
    router_heads = jnp.dot(router, weight32, precision=HIGH)
    base = jnp.dot(hidden_in.astype(jnp.float32), router, precision=HIGH)
    grad_proj = jnp.dot(grad_out, out_weight, preferred_element_type=jnp.float32)
    first32 = attn_first.astype(jnp.float32)
    second32 = attn_second.astype(jnp.float32)
    third32 = attn_third.astype(jnp.float32)
    rows_one, live_one = slot_layout(kept_second)
    rows_two, live_two = slot_layout(kept_third)
    proj_one = grad_proj[rows_one]
    proj_two = grad_proj[rows_two]
    along0 = jnp.dot(first32, router_heads, precision=HIGH)
    match0 = jnp.sum(first32 * grad_proj, axis=1)
    along1 = to_tokens(jnp.dot(second32, router_heads, precision=HIGH), rows_one, live_one)
    match1 = to_tokens(jnp.sum(second32 * proj_one, axis=1), rows_one, live_one)
    match2 = to_tokens(jnp.sum(third32 * proj_two, axis=1), rows_two, live_two)
    mask1 = to_tokens(jnp.ones_like(live_one), rows_one, live_one)
    mask2 = to_tokens(jnp.ones_like(live_two), rows_two, live_two)
    gate0 = jax.nn.sigmoid(base)
    logit1 = base + gate0 * along0
    gate1 = jax.nn.sigmoid(logit1)
    logit2 = logit1 + mask1 * gate1 * along1
    gate2 = jax.nn.sigmoid(logit2)
    slope2 = mask2 * match2 * gate2 * (1.0 - gate2)
    slope1 = mask1 * (match1 + slope2 * along1) * gate1 * (1.0 - gate1)
    later0 = slope1 + slope2
    slope0 = (match0 + later0 * along0) * gate0 * (1.0 - gate0)
    total = later0 + slope0
    grad32 = grad_out.astype(jnp.float32)
    grad_in = (grad32 + total[:, None] * router[None, :]).astype(jnp.bfloat16)
    grad_first = (gate0[:, None] * (grad_proj + later0[:, None] * router_heads[None, :])).astype(jnp.bfloat16)
    gate_one = live_one * gate1[rows_one]
    later_one = slope2[rows_one]
    gate_two = live_two * gate2[rows_two]
    grad_second = (gate_one[:, None] * (proj_one + later_one[:, None] * router_heads[None, :])).astype(jnp.bfloat16)
    grad_third = (gate_two[:, None] * proj_two).astype(jnp.bfloat16)
    carry0 = (grad32 + later0[:, None] * router[None, :]).astype(jnp.bfloat16)
    carry1 = (grad32[rows_one] + later_one[:, None] * router[None, :]).astype(jnp.bfloat16)
    carry2 = grad_out[rows_two]
    scaled0 = (gate0[:, None] * first32).astype(jnp.bfloat16)
    scaled1 = (gate_one[:, None] * second32).astype(jnp.bfloat16)
    scaled2 = (gate_two[:, None] * third32).astype(jnp.bfloat16)
    weight_sum = jnp.dot(carry0.T, scaled0, preferred_element_type=jnp.float32)
    weight_sum = weight_sum + jnp.dot(carry1.T, scaled1, preferred_element_type=jnp.float32)
    weight_sum = weight_sum + jnp.dot(carry2.T, scaled2, preferred_element_type=jnp.float32)
    scale = float(TOKENS) ** -0.5
    weight_grad = (weight_sum * scale).astype(jnp.bfloat16)
    heads_sum = jnp.dot(later0 * gate0, first32, precision=HIGH) + jnp.dot(gate_one * later_one, second32, precision=HIGH)
    router_grad = (jnp.dot(total, hidden_in.astype(jnp.float32), precision=HIGH) + jnp.dot(weight32, heads_sum, precision=HIGH)) * scale
    return grad_in, grad_first, grad_second, grad_third, weight_grad, router_grad
```

```python
import jax
import jax.numpy as jnp
from jax import lax
from jax.sharding import PartitionSpec as P

NB = 3
NX, NZ, NY, NC = 4, 4, 4, 2
F32, BF16 = jnp.float32, jnp.bfloat16


def dev(x, z, y, c):
    return ((x * NZ + z) * NY + y) * NC + c


def coords(f):
    return f // (NC * NY * NZ), f // (NC * NY) % NZ, f // NC % NY, f % NC


def owner(x, y, z, c):
    return dev((x >> 1) * 2 + c, (x & 1) * 2 + (y >> 1), (y & 1) * 2 + (z >> 1), z & 1)


def shifted(x, axis, step):
    pairs = []
    for f in range(NX * NZ * NY * NC):
        at = dict(zip("xzyc", coords(f)))
        size = {"x": NX, "z": NZ, "y": NY, "c": NC}[axis]
        at[axis] = (at[axis] + step) % size
        pairs.append((f, dev(at["x"], at["z"], at["y"], at["c"])))
    return lax.ppermute(x, "fsdp", pairs)


def swap_tp(x):
    return lax.ppermute(x, "tp", [(0, 1), (1, 0)])


def ring_gather(block, axis):
    half = block.shape[0] // 2
    ahead = shifted(block, axis, -1)
    behind = shifted(block, axis, 1)
    far0 = shifted(behind[:half], axis, 1)
    far1 = shifted(ahead[half:], axis, -1)
    return [block, ahead, jnp.concatenate([far0, far1], axis=0), behind]


def ring_reduce(parts, axis):
    own, ahead, far, behind = parts
    half = far.shape[0] // 2
    got0 = shifted(far[:half].astype(BF16), axis, 1)
    got1 = shifted(far[half:].astype(BF16), axis, -1)
    send0 = jnp.concatenate([ahead[:half] + got0.astype(F32), ahead[half:]], axis=0)
    send1 = jnp.concatenate([behind[:half], behind[half:] + got1.astype(F32)], axis=0)
    return own + shifted(send0.astype(BF16), axis, 1).astype(F32) + shifted(send1.astype(BF16), axis, -1).astype(F32)


def rolled(values, axis, start):
    return lax.dynamic_slice_in_dim(
        jnp.concatenate([values, values], axis=axis), start, values.shape[axis], axis
    )


def ring_sum(v, axis):
    return v + shifted(v, axis, 1) + shifted(v, axis, 2) + shifted(v, axis, 3)


def split3(v):
    a = lax.reduce_precision(v, 8, 7)
    b = lax.reduce_precision(v - a, 8, 7)
    return a.astype(BF16), b.astype(BF16), (v - a - b).astype(BF16)


def local(
    hidden_in,
    attn_first,
    attn_second,
    attn_third,
    out_weight,
    router,
    kept_second,
    kept_third,
    grad_out,
):
    rows, width = grad_out.shape
    heads = attn_first.shape[1]
    block = rows // NB
    depth = width // 2
    f = lax.axis_index("fsdp")
    t = lax.axis_index("tp")
    x, y, c = f // (NC * NY * NZ), f // NC % NY, f % NC
    router_part = lax.dynamic_slice_in_dim(router, t * width, width, 0)

    got = []
    for z in range(NZ):
        got.append(None)
    span = out_weight.shape[0]
    for k in range(NZ):
        pairs = []
        for g in range(NX * NZ * NY * NC):
            gx, gz, gy, gc = coords(g)
            pairs.append((owner(gx, gy, (gz + k) % NZ, gc), g))
        got[k] = lax.ppermute(out_weight, "fsdp", pairs)
    z = f // (NC * NY) % NZ
    shards = rolled(jnp.stack(got), 0, (NZ - z) % NZ).reshape(NZ * span, heads)

    mine = lax.dynamic_slice_in_dim(grad_out, c * depth, depth, 1)
    other = lax.dynamic_slice_in_dim(grad_out, (1 - c) * depth, depth, 1)
    grad_here = jnp.concatenate([mine, shifted(other, "c", 1)], axis=0)
    grad_there = swap_tp(grad_here)
    low = jnp.where(t == 0, grad_here, grad_there)
    high = jnp.where(t == 0, grad_there, grad_here)
    grads = jnp.concatenate([low, high], axis=1)

    half = heads // 2
    first = jnp.concatenate(ring_gather(shards[:, :half], "x"), axis=0)
    weight_a = jnp.concatenate(ring_gather(first, "y"), axis=0)
    second = jnp.concatenate(ring_gather(shards[:, half:], "y"), axis=0)
    weight_b = jnp.concatenate(ring_gather(second, "x"), axis=0)

    router_half = jnp.concatenate(
        [
            lax.dynamic_slice_in_dim(router, c * depth, depth, 0),
            lax.dynamic_slice_in_dim(router, width + c * depth, depth, 0),
        ]
    )
    extra = jnp.stack(split3(router_half) + (jnp.zeros((2 * depth,), BF16),) * 5)
    lhs = jnp.concatenate([grads, extra], axis=0)
    count = lhs.shape[0]
    lhs = lhs.reshape(count, NX, NY, -1)
    rolled_xy = rolled(rolled(lhs, 1, x), 2, y)
    lhs_b = rolled_xy.reshape(count, -1)
    lhs_a = rolled_xy.transpose(0, 2, 1, 3).reshape(count, -1)
    proj = jnp.concatenate(
        [
            jnp.dot(lhs_a, weight_a, preferred_element_type=F32),
            jnp.dot(lhs_b, weight_b, preferred_element_type=F32),
        ],
        axis=1,
    )
    sent = shifted(proj[rows:], "c", 1)
    grad_proj = proj[:rows] + sent[:rows]
    router_heads = jnp.sum(proj[2 * rows :], axis=0) + jnp.sum(sent[rows:], axis=0)

    ids_one, ids_two = kept_second[0], kept_third[0]
    blocks = jnp.arange(NB, dtype=jnp.int32)
    zero = jnp.zeros((), BF16)

    def place(values, ids):
        shaped = values.reshape(-1, 1, block, heads)
        total = jnp.zeros((NB, block, heads), BF16)
        for j in range(ids.shape[0]):
            total = jnp.where((ids[j] == blocks)[:, None, None], shaped[j], total)
        return total.reshape(rows, heads)

    first32 = attn_first.astype(F32)
    second32 = place(attn_second, ids_one).astype(F32)
    third32 = place(attn_third, ids_two).astype(F32)
    mask1 = jnp.repeat(jnp.any(ids_one[None, :] == blocks[:, None], axis=1).astype(F32), block)
    mask2 = jnp.repeat(jnp.any(ids_two[None, :] == blocks[:, None], axis=1).astype(F32), block)
    sums = jnp.stack(
        [
            jnp.sum(hidden_in.astype(F32) * router_part, axis=1),
            jnp.sum(first32 * router_heads, axis=1),
            jnp.sum(first32 * grad_proj, axis=1),
            jnp.sum(second32 * router_heads, axis=1),
            jnp.sum(second32 * grad_proj, axis=1),
            jnp.sum(third32 * grad_proj, axis=1),
        ]
    )
    base, along0, match0, along1, match1, match2 = sums + swap_tp(sums)
    gate0 = jax.nn.sigmoid(base)
    logit1 = base + gate0 * along0
    gate1 = jax.nn.sigmoid(logit1)
    logit2 = logit1 + mask1 * gate1 * along1
    gate2 = jax.nn.sigmoid(logit2)
    slope2 = mask2 * match2 * gate2 * (1.0 - gate2)
    slope1 = mask1 * (match1 + slope2 * along1) * gate1 * (1.0 - gate1)
    later0 = slope1 + slope2
    slope0 = (match0 + later0 * along0) * gate0 * (1.0 - gate0)
    total = later0 + slope0

    scaled = (
        (gate0[:, None] * first32).astype(BF16).astype(F32)
        + (gate1[:, None] * second32).astype(BF16).astype(F32)
        + (gate2[:, None] * third32).astype(BF16).astype(F32)
    ).astype(BF16)
    scaled = jnp.concatenate([scaled, shifted(scaled, "c", 1)], axis=0)
    token = (((0,), (0,)), ((), ()))

    def terms(lhs, rhs):
        whole = lax.dot_general(lhs, rhs, token, preferred_element_type=F32)
        return [whole[k * (2 * depth // 4) : (k + 1) * (2 * depth // 4)] for k in range(4)]

    def parts(whole):
        span = whole.shape[0] // 4
        return [whole[k * span : (k + 1) * span] for k in range(4)]

    red_a = ring_reduce(terms(lhs_a[: 2 * rows], scaled[:, :half]), "y")
    red_b = ring_reduce(terms(lhs_b[: 2 * rows], scaled[:, half:]), "x")
    red_a = ring_reduce(parts(red_a), "x")
    red_b = ring_reduce(parts(red_b), "y")
    red = jnp.concatenate([red_a, red_b], axis=1).astype(BF16).reshape(NZ, span, heads)
    weight_sum = 0.0
    ordered = rolled(red, 0, z)
    for k in range(NZ):
        pairs = []
        for g in range(NX * NZ * NY * NC):
            gx, gz, gy, gc = coords(g)
            pairs.append((g, owner(gx, gy, (gz + k) % NZ, gc)))
        weight_sum = weight_sum + lax.ppermute(ordered[k], "fsdp", pairs).astype(F32)

    heads_part = jnp.sum(
        (later0 * gate0)[:, None] * first32 + (gate1 * slope2)[:, None] * second32, axis=0
    )
    hidden_part = jnp.sum(total[:, None] * hidden_in.astype(F32), axis=0)
    both = jnp.concatenate([heads_part, hidden_part])
    both = both + shifted(both, "c", 1)
    heads_chip, hidden_chip = both[:heads], both[heads:]

    def back(weight, part):
        cut = jnp.stack(split3(part) + (jnp.zeros(part.shape, BF16),) * 5)
        return jnp.sum(
            lax.dot_general(cut, weight, (((1,), (1,)), ((), ())), preferred_element_type=F32), axis=0
        )

    term_a = back(weight_a, heads_chip[:half]).reshape(NY, NX, -1).transpose(1, 0, 2)
    term_b = back(weight_b, heads_chip[half:]).reshape(NX, NY, -1)
    term = term_a + term_b
    term = rolled(rolled(term, 0, (NX - x) % NX), 1, (NY - y) % NY).reshape(-1)
    vector = jnp.concatenate([heads_chip, hidden_chip, term])
    vector = ring_sum(ring_sum(ring_sum(vector, "x"), "y"), "z")
    heads_total, hidden_total, term = vector[:heads], vector[heads : heads + width], vector[heads + width :]
    term_other = shifted(term, "c", 1)
    core0 = jnp.where(c == 0, term, term_other)
    core1 = jnp.where(c == 0, term_other, term)
    term = jnp.concatenate([core0[:depth], core1[:depth], core0[depth:], core1[depth:]])
    full = lax.dynamic_update_slice_in_dim(
        term, lax.dynamic_slice_in_dim(term, t * width, width, 0) + hidden_total, t * width, 0
    )
    scale = float(rows * NX * NZ * NY * NC) ** (-0.5)
    router_grad = (full + swap_tp(full)) * scale

    own_router = lax.dynamic_slice_in_dim(router, f * span, span, 0)
    weight_grad = ((weight_sum + own_router[:, None] * heads_total[None, :]) * scale).astype(BF16)

    grad_in = (grad_out.astype(F32) + total[:, None] * router_part[None, :]).astype(BF16)
    grad_first = (gate0[:, None] * (grad_proj + later0[:, None] * router_heads)).astype(BF16)
    at_one = (gate1[:, None] * (grad_proj + slope2[:, None] * router_heads)).astype(BF16)
    at_two = (gate2[:, None] * grad_proj).astype(BF16)

    def pick(values, ids):
        shaped = values.reshape(NB, block, heads)
        out = []
        for j in range(ids.shape[0]):
            one = lax.dynamic_index_in_dim(shaped, jnp.maximum(ids[j], 0), 0, keepdims=False)
            out.append(jnp.where(ids[j] >= 0, one, zero))
        return jnp.concatenate(out, axis=0)

    return (grad_in, grad_first, pick(at_one, ids_one), pick(at_two, ids_two), weight_grad, router_grad)


def solution(mesh):
    return jax.shard_map(
        local,
        mesh=mesh,
        in_specs=(
            P("fsdp", "tp"),
            P("fsdp", "tp"),
            P("fsdp", "tp"),
            P("fsdp", "tp"),
            P("fsdp", "tp"),
            P(),
            P("fsdp", None),
            P("fsdp", None),
            P("fsdp", "tp"),
        ),
        out_specs=(
            P("fsdp", "tp"),
            P("fsdp", "tp"),
            P("fsdp", "tp"),
            P("fsdp", "tp"),
            P("fsdp", "tp"),
            P(),
        ),
        check_vma=False,
    )
```

```python
import jax
import jax.numpy as jnp
from jax import lax
from jax.experimental import pallas as pl
from jax.experimental.pallas import tpu as pltpu
from jax.sharding import PartitionSpec as P

NB = 3
NX, NZ, NY, NC = 4, 4, 4, 2
NF = NX * NZ * NY * NC
F32, BF16 = jnp.float32, jnp.bfloat16
ROWS, WIDTH, HEADS = 384, 2048, 1024
BLOCK = ROWS // NB
DEPTH = WIDTH // 2
HALF = HEADS // 2
SPAN = 32
CHUNK = 4 * 4 * SPAN
SIZES = {"x": NX, "z": NZ, "y": NY, "c": NC}
VMEM = pl.BlockSpec(memory_space=pltpu.VMEM)
SMEM = pl.BlockSpec(memory_space=pltpu.SMEM)


def dev(x, z, y, c):
    return ((x * NZ + z) * NY + y) * NC + c


def shifted(v, axis, step):
    pairs = []
    for f in range(NF):
        at = {"x": f // (NC * NY * NZ), "z": f // (NC * NY) % NZ, "y": f // NC % NY, "c": f % NC}
        here = dev(**at)
        at[axis] = (at[axis] + step) % SIZES[axis]
        pairs.append((dev(**at), here))
    return lax.ppermute(v, "fsdp", pairs)


def swap_tp(v):
    return lax.ppermute(v, "tp", [(0, 1), (1, 0)])


def around(v, axis):
    return [v] + [shifted(v, axis, k) for k in (1, 2, 3)]


def ring_sum(v, axis):
    a, b, c, d = around(v, axis)
    return (a + b) + (c + d)


def call(kernel, outs, scratch, flops, moved, *args):
    specs = [SMEM if a.dtype == jnp.int32 else VMEM for a in args]
    single = not isinstance(outs, list)
    shapes = [jax.ShapeDtypeStruct(s, d) for s, d in ([outs] if single else outs)]
    got = pl.pallas_call(
        kernel,
        out_shape=shapes,
        in_specs=specs,
        out_specs=[VMEM] * len(shapes),
        scratch_shapes=[pltpu.VMEM(s, d) for s, d in scratch],
        compiler_params=pltpu.CompilerParams(vmem_limit_bytes=40 * 2**20),
        cost_estimate=pl.CostEstimate(flops=flops, bytes_accessed=moved, transcendentals=0),
    )(*args)
    return got[0] if single else got


def split_kernel(pos, grad, mine, other):
    c = pos[3]
    row = lax.broadcasted_iota(jnp.int32, (256, 128), 0)
    col = lax.broadcasted_iota(jnp.int32, (256, 128), 1)
    source = (col >> 5) * 64 + (col & 31)
    take = (row == source + c * 32).astype(F32).astype(BF16)
    leave = (row == source + (1 - c) * 32).astype(F32).astype(BF16)
    for k in range(WIDTH // 256):
        piece = grad[:, k * 256 : (k + 1) * 256]
        at = slice(k * 128, (k + 1) * 128)
        mine[:, at] = jnp.dot(piece, take, preferred_element_type=F32).astype(BF16)
        other[:, at] = jnp.dot(piece, leave, preferred_element_type=F32).astype(BF16)


def to_rows(columns):
    lane = lax.broadcasted_iota(jnp.int32, (ROWS, 128), 1)
    wide = jnp.zeros((ROWS, 128), F32)
    for k, column in enumerate(columns):
        wide = jnp.where(lane == k, column, wide)
    return wide.T[:8]


def to_columns(rows):
    wide = jnp.concatenate([rows, jnp.zeros((128 - rows.shape[0], ROWS), F32)], axis=0)
    return wide.T


def chosen(kept, j, b):
    return (kept[0, j] == b).astype(F32)


def placed(kept, columns):
    out = []
    for b in range(NB):
        out.append(sum(chosen(kept, j, b) * column for j, column in enumerate(columns)))
    return jnp.concatenate(out, axis=0)


def slots(ref, count):
    return [ref[j * BLOCK : (j + 1) * BLOCK, :].astype(F32) for j in range(count)]


def along_kernel(kept2, hidden, router, a1, a2, heads, out):
    r = heads[...]
    base = jnp.sum(hidden[...].astype(F32) * router[...], axis=1, keepdims=True)
    along0 = jnp.sum(a1[...].astype(F32) * r, axis=1, keepdims=True)
    along1 = placed(kept2, [jnp.sum(v * r, axis=1, keepdims=True) for v in slots(a2, 2)])
    out[...] = to_rows([base, along0, along1])


def mask_row(kept, count):
    b = lax.broadcasted_iota(jnp.int32, (1, ROWS), 1) >> 7
    mask = jnp.zeros((1, ROWS), F32)
    for j in range(count):
        mask = jnp.where(b == kept[0, j], 1.0, mask)
    return mask


def sigmoid(v):
    return jax.nn.sigmoid(v)


def scaled_kernel(kept2, kept3, sums, sent, a1, a2, a3, gates, scaled):
    both = sums[...] + sent[...]
    base, along0, along1 = both[0:1], both[1:2], both[2:3]
    gate0 = sigmoid(base)
    logit1 = base + gate0 * along0
    gate1 = sigmoid(logit1)
    gate2 = sigmoid(logit1 + mask_row(kept2, 2) * gate1 * along1)
    rows = jnp.concatenate([gate0, gate1, gate2, along0, along1, jnp.zeros((3, ROWS), F32)], axis=0)
    gates[...] = rows
    columns = to_columns(rows)
    for b in range(NB):
        at = slice(b * BLOCK, (b + 1) * BLOCK)
        g = columns[at]
        total = (g[:, 0:1] * a1[at, :].astype(F32)).astype(BF16).astype(F32)
        for j in range(2):
            v = (g[:, 1:2] * a2[j * BLOCK : (j + 1) * BLOCK, :].astype(F32)).astype(BF16)
            total = total + chosen(kept2, j, b) * v.astype(F32)
        v = (g[:, 2:3] * a3[...].astype(F32)).astype(BF16)
        total = total + chosen(kept3, 0, b) * v.astype(F32)
        scaled[at, :] = total.astype(BF16)


def term_kernel(pos, gm, gr, gmt, grt, s0, s1, *refs):
    outs, (gt, st, lhs) = refs[:8], refs[8:]
    x, z, y, t = pos[0], pos[1], pos[2], pos[4]
    here = pl.multiple_of(t * DEPTH, DEPTH)
    there = pl.multiple_of((1 - t) * DEPTH, DEPTH)
    for k in range(DEPTH // 256):
        at = slice(k * 256, (k + 1) * 256)
        gt[pl.ds(here + k * 256, 256), :ROWS] = gm[:, at].T
        gt[pl.ds(here + k * 256, 256), ROWS:] = gr[:, at].T
        gt[pl.ds(there + k * 256, 256), :ROWS] = gmt[:, at].T
        gt[pl.ds(there + k * 256, 256), ROWS:] = grt[:, at].T
    st[:ROWS, :] = s0[...]
    st[ROWS:, :] = s1[...]
    for k in (2, 1, 3, 0):
        for side in range(2):
            for i in range(4):
                for j in range(4):
                    xx, yy = ((x + i) & 3, (y + k) & 3) if side == 0 else ((x + k) & 3, (y + i) & 3)
                    row = pl.multiple_of(xx * 512 + ((z + j) & 3) * 128 + yy * 32, 32)
                    lhs[(i * 4 + j) * SPAN : (i * 4 + j + 1) * SPAN, :] = gt[pl.ds(row, SPAN), :]
            cols = slice(side * HALF, (side + 1) * HALF)
            got = jnp.dot(lhs[...], st[:, cols], preferred_element_type=F32)
            out = outs[side * 4 + k]
            out[...] = got.astype(out.dtype)


def proj_kernel(pos, gm, gr, gmt, grt, *refs):
    pieces, (weight, keep, send) = refs[:8], refs[8:]
    x, z, y, t = pos[0], pos[1], pos[2], pos[4]
    for k in range(4):
        for side in range(2):
            for i in range(4):
                for j in range(4):
                    xx, yy = ((x + i) & 3, (y + k) & 3) if side == 0 else ((x + k) & 3, (y + i) & 3)
                    row = pl.multiple_of(xx * 512 + ((z + j) & 3) * 128 + yy * 32, 32)
                    weight[pl.ds(row, SPAN), side * HALF : (side + 1) * HALF] = pieces[side * 4 + k][
                        (i * 4 + j) * SPAN : (i * 4 + j + 1) * SPAN, :
                    ]
    here = pl.multiple_of(t * DEPTH, DEPTH)
    there = pl.multiple_of((1 - t) * DEPTH, DEPTH)
    for out, a, b in ((send, gr, grt), (keep, gm, gmt)):
        for n in range(2):
            at = slice(n * HALF, (n + 1) * HALF)
            out[:, at] = jnp.dot(
                a[...], weight[pl.ds(here, DEPTH), at], preferred_element_type=F32
            ) + jnp.dot(b[...], weight[pl.ds(there, DEPTH), at], preferred_element_type=F32)


def match_kernel(kept2, kept3, keep, sent, a1, a2, a3, out):
    proj = keep[...] + sent[...]
    match0 = jnp.sum(a1[...].astype(F32) * proj, axis=1, keepdims=True)

    def slot(kept, ref, count):
        parts = []
        for b in range(NB):
            value = 0.0
            for j in range(count):
                value = value + chosen(kept, j, b) * ref[j * BLOCK : (j + 1) * BLOCK, :].astype(F32)
            parts.append(jnp.sum(value * proj[b * BLOCK : (b + 1) * BLOCK], axis=1, keepdims=True))
        return jnp.concatenate(parts, axis=0)

    out[...] = to_rows([match0, slot(kept2, a2, 2), slot(kept3, a3, 1)])


def slope_kernel(kept2, kept3, sums, sent, gates, a1, a2, hidden, out, vector):
    both = sums[...] + sent[...]
    match0, match1, match2 = both[0:1], both[1:2], both[2:3]
    g = gates[...]
    gate0, gate1, gate2, along0, along1 = g[0:1], g[1:2], g[2:3], g[3:4], g[4:5]
    slope2 = mask_row(kept3, 1) * match2 * gate2 * (1.0 - gate2)
    slope1 = mask_row(kept2, 2) * (match1 + slope2 * along1) * gate1 * (1.0 - gate1)
    later0 = slope1 + slope2
    slope0 = (match0 + later0 * along0) * gate0 * (1.0 - gate0)
    total = later0 + slope0
    rows = jnp.concatenate(
        [gate0, gate1, gate2, later0, slope2, total, later0 * gate0, gate1 * slope2], axis=0
    )
    out[...] = rows
    columns = to_columns(rows)
    heads = jnp.sum(columns[:, 6:7] * a1[...].astype(F32), axis=0, keepdims=True)
    for b in range(NB):
        weight = columns[b * BLOCK : (b + 1) * BLOCK, 7:8]
        for j in range(2):
            v = a2[j * BLOCK : (j + 1) * BLOCK, :].astype(F32)
            heads = heads + chosen(kept2, j, b) * jnp.sum(weight * v, axis=0, keepdims=True)
    hid = jnp.sum(columns[:, 5:6] * hidden[...].astype(F32), axis=0, keepdims=True)
    vector[...] = jnp.concatenate([heads, hid], axis=1)


def grads_kernel(kept2, kept3, rows, keep, sent, heads, grad, router, gin, g1, g2, g3, proj):
    columns = to_columns(rows[...])
    gin[...] = (grad[...].astype(F32) + columns[:, 5:6] * router[...]).astype(BF16)
    proj[...] = keep[...] + sent[...]
    r = heads[...]
    g1[...] = (columns[:, 0:1] * (proj[...] + columns[:, 3:4] * r)).astype(BF16)

    def slot(kept, j):
        safe = jnp.maximum(kept[0, j], 0)
        live = (kept[0, j] >= 0).astype(F32)
        col = jnp.zeros((BLOCK, 128), F32)
        for b in range(NB):
            col = jnp.where(safe == b, columns[b * BLOCK : (b + 1) * BLOCK], col)
        return proj[pl.ds(pl.multiple_of(safe * BLOCK, BLOCK), BLOCK), :], col, live

    for j in range(2):
        p, col, live = slot(kept2, j)
        v = live * col[:, 1:2] * (p + col[:, 4:5] * r)
        g2[j * BLOCK : (j + 1) * BLOCK, :] = v.astype(BF16)
    p, col, live = slot(kept3, 0)
    g3[...] = (live * col[:, 2:3] * p).astype(BF16)


def back_kernel(mine, sent, weight, heads_hidden, term):
    both = mine[...] + sent[...]
    heads_hidden[...] = both
    v = both[:, :HEADS]
    a = v.astype(BF16)
    rest = v - a.astype(F32)
    b = rest.astype(BF16)
    d = (rest - b.astype(F32)).astype(BF16)
    lhs = jnp.concatenate([a, b, d, jnp.zeros((13, HEADS), BF16)], axis=0)
    got = lax.dot_general(lhs, weight[...], (((1,), (1,)), ((), ())), preferred_element_type=F32)
    term[...] = jnp.sum(got, axis=0, keepdims=True)


def local(
    hidden_in,
    attn_first,
    attn_second,
    attn_third,
    out_weight,
    router,
    kept_second,
    kept_third,
    grad_out,
):
    f = lax.axis_index("fsdp")
    t = lax.axis_index("tp")
    x, z, y, c = f // (NC * NY * NZ), f // (NC * NY) % NZ, f // NC % NY, f % NC
    pos = jnp.stack([x, z, y, c, t, t, t, t]).astype(jnp.int32)
    router_part = lax.dynamic_slice_in_dim(router, t * WIDTH, WIDTH, 0).reshape(1, WIDTH)

    block = jnp.concatenate(around(out_weight, "z"), axis=0)
    mine, other = call(
        split_kernel, [((ROWS, DEPTH), BF16)] * 2, [], 2 * ROWS * WIDTH * 256, 3 * 2**20, pos, grad_out
    )
    received = shifted(other, "c", 1)
    first = jnp.concatenate(around(block[:, :HALF], "x"), axis=0)
    second = jnp.concatenate(around(block[:, HALF:], "y"), axis=0)

    by_owner = router.reshape(NX, NZ, NY, NC, SPAN)
    by_owner = lax.dynamic_index_in_dim(by_owner, c, 3, keepdims=False)
    by_owner = jnp.concatenate([by_owner] * 2, axis=1)
    by_owner = lax.dynamic_slice_in_dim(by_owner, z, NZ, 1)
    double_x = jnp.concatenate([by_owner] * 2, axis=0)
    double_y = jnp.concatenate([by_owner] * 2, axis=2)
    router_a = lax.dynamic_index_in_dim(lax.dynamic_slice_in_dim(double_x, x, NX, 0), y, 2, keepdims=False)
    router_b = lax.dynamic_index_in_dim(lax.dynamic_slice_in_dim(double_y, y, NY, 2), x, 0, keepdims=False)
    router_a = router_a.reshape(CHUNK, 1)
    router_b = router_b.transpose(1, 0, 2).reshape(CHUNK, 1)
    heads_a = jnp.sum(first.astype(F32) * router_a, axis=0)
    heads_b = jnp.sum(second.astype(F32) * router_b, axis=0)
    heads_a = ring_sum(heads_a, "y")
    heads_b = ring_sum(heads_b, "x")
    router_heads = jnp.concatenate([heads_a, heads_b])
    router_heads = (router_heads + shifted(router_heads, "c", 1)).reshape(1, HEADS)

    pieces = around(first, "y") + around(second, "x")
    mine_t = swap_tp(mine)
    received_t = swap_tp(received)
    grads = (mine, received, mine_t, received_t)

    sums = call(
        along_kernel, ((8, ROWS), F32), [], 10**7, 3 * 2**20,
        kept_second, hidden_in, router_part, attn_first, attn_second, router_heads,
    )
    gates, scaled = call(
        scaled_kernel, [((8, ROWS), F32), ((ROWS, HEADS), BF16)], [], 10**7, 2 * 2**20,
        kept_second, kept_third, sums, swap_tp(sums), attn_first, attn_second, attn_third,
    )
    scaled_other = shifted(scaled, "c", 1)

    kinds = [F32, BF16, BF16, BF16]
    terms = call(
        term_kernel,
        [((CHUNK, HALF), k) for k in kinds * 2],
        [((WIDTH, 2 * ROWS), BF16), ((2 * ROWS, HEADS), BF16), ((CHUNK, 2 * ROWS), BF16)],
        2 * 2 * ROWS * WIDTH * HEADS, 10 * 2**20,
        pos, *grads, scaled, scaled_other,
    )

    def gathered(parts, axis):
        total = parts[0]
        for k in (1, 2, 3):
            total = total + shifted(parts[k], axis, -k).astype(F32)
        return total

    def cut(total):
        n = total.shape[0] // 4
        return [total[:n]] + [total[k * n : (k + 1) * n].astype(BF16) for k in (1, 2, 3)]

    red_a = gathered(cut(gathered(terms[:4], "y")), "x")
    red_b = gathered(cut(gathered(terms[4:], "x")), "y")
    weight_sum = gathered(cut(jnp.concatenate([red_a, red_b], axis=1)), "z")

    weight, keep, send = call(
        proj_kernel,
        [((WIDTH, HEADS), BF16), ((ROWS, HEADS), F32), ((ROWS, HEADS), F32)],
        [], 2 * 2 * ROWS * WIDTH * HEADS, 14 * 2**20,
        pos, *grads, *pieces,
    )
    sent = shifted(send, "c", 1)
    sums = call(
        match_kernel, ((8, ROWS), F32), [], 10**7, 5 * 2**20,
        kept_second, kept_third, keep, sent, attn_first, attn_second, attn_third,
    )
    rows, vector = call(
        slope_kernel, [((8, ROWS), F32), ((1, HEADS + WIDTH), F32)], [], 10**7, 3 * 2**20,
        kept_second, kept_third, sums, swap_tp(sums), gates, attn_first, attn_second, hidden_in,
    )
    vector, term = call(
        back_kernel, [((1, HEADS + WIDTH), F32), ((1, WIDTH), F32)], [], 2 * 16 * WIDTH * HEADS, 4 * 2**20,
        vector, shifted(vector, "c", 1), weight,
    )
    grad_in, grad_first, grad_second, grad_third = call(
        grads_kernel,
        [((ROWS, WIDTH), BF16), ((ROWS, HEADS), BF16), ((2 * BLOCK, HEADS), BF16), ((BLOCK, HEADS), BF16)],
        [((ROWS, HEADS), F32)], 10**7, 10 * 2**20,
        kept_second, kept_third, rows, keep, sent, router_heads, grad_out, router_part,
    )
    vector = jnp.concatenate([vector, term], axis=1).reshape(-1)
    vector = ring_sum(ring_sum(ring_sum(vector, "x"), "y"), "z")
    heads_total, hidden_total, term = vector[:HEADS], vector[HEADS : HEADS + WIDTH], vector[HEADS + WIDTH :]
    term_other = shifted(term, "c", 1)
    low = jnp.where(c == 0, term, term_other).reshape(-1, 1, SPAN)
    high = jnp.where(c == 0, term_other, term).reshape(-1, 1, SPAN)
    full = jnp.concatenate([low, high], axis=1).reshape(2, WIDTH)
    own = jnp.arange(2, dtype=jnp.int32)[:, None] == t
    full = (full + jnp.where(own, hidden_total[None, :], 0.0)).reshape(-1)
    scale = float(ROWS * NF) ** (-0.5)
    router_grad = (full + swap_tp(full)) * scale
    own_router = lax.dynamic_slice_in_dim(router, f * SPAN, SPAN, 0)
    weight_grad = ((weight_sum + own_router[:, None] * heads_total[None, :]) * scale).astype(BF16)
    return (grad_in, grad_first, grad_second, grad_third, weight_grad, router_grad)


def solution(mesh):
    return jax.shard_map(
        local,
        mesh=mesh,
        in_specs=(
            P("fsdp", "tp"),
            P("fsdp", "tp"),
            P("fsdp", "tp"),
            P("fsdp", "tp"),
            P("fsdp", "tp"),
            P(),
            P("fsdp", None),
            P("fsdp", None),
            P("fsdp", "tp"),
        ),
        out_specs=(
            P("fsdp", "tp"),
            P("fsdp", "tp"),
            P("fsdp", "tp"),
            P("fsdp", "tp"),
            P("fsdp", "tp"),
            P(),
        ),
        check_vma=False,
    )
```

```python
import jax
import jax.numpy as jnp
from jax import lax
from jax.experimental import pallas as pl
from jax.experimental.pallas import tpu as pltpu
from jax.sharding import PartitionSpec as P

NB = 3
NX, NZ, NY, NC = 4, 4, 4, 2
NF = NX * NZ * NY * NC
F32, BF16 = jnp.float32, jnp.bfloat16
ROWS, WIDTH, HEADS = 384, 2048, 1024
BLOCK = ROWS // NB
DEPTH = WIDTH // 2
HALF = HEADS // 2
SPAN = 32
CHUNK = 4 * 4 * SPAN
SIZES = {"x": NX, "z": NZ, "y": NY, "c": NC}
VMEM = pl.BlockSpec(memory_space=pltpu.VMEM)
SMEM = pl.BlockSpec(memory_space=pltpu.SMEM)


def dev(x, z, y, c):
    return ((x * NZ + z) * NY + y) * NC + c


def shifted(v, axis, step):
    pairs = []
    for f in range(NF):
        at = {"x": f // (NC * NY * NZ), "z": f // (NC * NY) % NZ, "y": f // NC % NY, "c": f % NC}
        here = dev(**at)
        at[axis] = (at[axis] + step) % SIZES[axis]
        pairs.append((dev(**at), here))
    return lax.ppermute(v, "fsdp", pairs)


def swap_tp(v):
    return lax.ppermute(v, "tp", [(0, 1), (1, 0)])


def around(v, axis):
    return [v] + [shifted(v, axis, k) for k in (1, 2, 3)]


def ring_sum(v, axis):
    a, b, c, d = around(v, axis)
    return (a + b) + (c + d)


def quad(v):
    pairs = [(2 * f + t, 2 * (f ^ 1) + 1 - t) for f in range(NF) for t in range(2)]
    return swap_tp(v), shifted(v, "c", 1), lax.ppermute(v, ("fsdp", "tp"), pairs)


def call(kernel, outs, scratch, *args):
    def spec(dtype):
        return SMEM if dtype == jnp.int32 else VMEM

    single = not isinstance(outs, list)
    shapes = [jax.ShapeDtypeStruct(s, d) for s, d in ([outs] if single else outs)]
    got = pl.pallas_call(
        kernel,
        out_shape=shapes,
        in_specs=[spec(a.dtype) for a in args],
        out_specs=[spec(s.dtype) for s in shapes],
        scratch_shapes=[pltpu.VMEM(s, d) for s, d in scratch],
        compiler_params=pltpu.CompilerParams(vmem_limit_bytes=40 * 2**20),
        cost_estimate=pl.CostEstimate(flops=1, bytes_accessed=1, transcendentals=0),
    )(*args)
    return got[0] if single else got


def split_kernel(pos, kept2, kept3, grad, hidden, router, mine, other, info):
    c = pos[3]
    row = lax.broadcasted_iota(jnp.int32, (128, 256), 0)
    col = lax.broadcasted_iota(jnp.int32, (128, 256), 1)
    source = (row >> 5) * 64 + (row & 31)
    take = (col == source + c * 32).astype(F32).astype(BF16)
    leave = (col == source + (1 - c) * 32).astype(F32).astype(BF16)
    both = (((1,), (1,)), ((), ()))
    for k in range(WIDTH // 256):
        piece = grad[:, k * 256 : (k + 1) * 256]
        at = slice(k * 128, (k + 1) * 128)
        mine[at, :] = lax.dot_general(take, piece, both, preferred_element_type=F32).astype(BF16)
        other[at, :] = lax.dot_general(leave, piece, both, preferred_element_type=F32).astype(BF16)
    base = jnp.sum(hidden[...].astype(F32) * router[...], axis=1, keepdims=True)
    rows = to_rows([base])
    at = lax.broadcasted_iota(jnp.int32, (8, ROWS), 0)
    for k, value in enumerate((kept2[0, 0], kept2[0, 1], kept3[0, 0])):
        rows = jnp.where(at == k + 1, value.astype(F32), rows)
    info[...] = rows


def to_rows(columns):
    lane = lax.broadcasted_iota(jnp.int32, (ROWS, 128), 1)
    wide = jnp.zeros((ROWS, 128), F32)
    for k, column in enumerate(columns):
        wide = jnp.where(lane == k, column, wide)
    return wide.T[:8]


def to_columns(rows):
    wide = jnp.concatenate([rows, jnp.zeros((128 - rows.shape[0], ROWS), F32)], axis=0)
    return wide.T


def chosen(info, j, b):
    return (info[j + 1 : j + 2, 0:1] == float(b)).astype(F32)


def mask_row(info, slots):
    b = (lax.broadcasted_iota(jnp.int32, (1, ROWS), 1) >> 7).astype(F32)
    mask = jnp.zeros((1, ROWS), F32)
    for j in slots:
        mask = jnp.where(info[j + 1 : j + 2, :] == b, 1.0, mask)
    return mask


def slot(attn, j):
    return attn[ROWS + j * BLOCK : ROWS + (j + 1) * BLOCK, :].astype(F32)


def along_kernel(info, info_o, attn, attn_o, heads, out):
    r = heads[...]
    for n, (i, a) in enumerate(((info, attn), (info_o, attn_o))):
        along0 = jnp.sum(a[:ROWS, :].astype(F32) * r, axis=1, keepdims=True)
        parts = [jnp.sum(slot(a, j) * r, axis=1, keepdims=True) for j in range(2)]
        along1 = jnp.concatenate(
            [chosen(i, 0, b) * parts[0] + chosen(i, 1, b) * parts[1] for b in range(NB)], axis=0
        )
        rows = to_rows([along0, along1])
        base = jnp.concatenate([jnp.zeros((2, ROWS), F32), i[0:1, :], jnp.zeros((5, ROWS), F32)], axis=0)
        out[:, n * ROWS : (n + 1) * ROWS] = rows + base


def scaled_kernel(info, info_o, attn, attn_o, sums, sent, gates, scaled):
    for n, (i, a) in enumerate(((info, attn), (info_o, attn_o))):
        cols = slice(n * ROWS, (n + 1) * ROWS)
        both = sums[:, cols] + sent[:, cols]
        along0, along1, base = both[0:1], both[1:2], both[2:3]
        gate0 = jax.nn.sigmoid(base)
        logit1 = base + gate0 * along0
        gate1 = jax.nn.sigmoid(logit1)
        gate2 = jax.nn.sigmoid(logit1 + mask_row(i, (0, 1)) * gate1 * along1)
        rows = jnp.concatenate([gate0, gate1, gate2, along0, along1, jnp.zeros((3, ROWS), F32)], axis=0)
        gates[:, cols] = rows
        columns = to_columns(rows)
        for b in range(NB):
            at = slice(b * BLOCK, (b + 1) * BLOCK)
            g = columns[at]
            total = (g[:, 0:1] * a[at, :].astype(F32)).astype(BF16).astype(F32)
            for j in range(3):
                w = g[:, 1:2] if j < 2 else g[:, 2:3]
                total = total + chosen(i, j, b) * (w * slot(a, j)).astype(BF16).astype(F32)
            scaled[n * ROWS + b * BLOCK : n * ROWS + (b + 1) * BLOCK, :] = total.astype(BF16)


def term_kernel(pos, gm, gr, gmt, grt, scaled, *outs):
    outs, later = outs[:8], outs[8]
    x, y, t = pos[0], pos[2], pos[4]
    for k in range(8):
        later[k] = pos[k]

    def product(a, b, cols):
        return jnp.dot(a, scaled[:ROWS, cols], preferred_element_type=F32) + jnp.dot(
            b, scaled[ROWS:, cols], preferred_element_type=F32
        )

    left, right = slice(0, HALF), slice(HALF, HEADS)
    for k in (2, 1, 3, 0):
        at = pl.ds(pl.multiple_of(((y + k) & 3) * SPAN, SPAN), SPAN)
        for n, (a, b) in enumerate(((gm, gr), (gmt, grt))):
            a = a.reshape(8, 128, ROWS)[:, at, :].reshape(256, ROWS)
            b = b.reshape(8, 128, ROWS)[:, at, :].reshape(256, ROWS)
            outs[k][n * 256 : (n + 1) * 256, :] = product(a, b, left).astype(BF16)
        xx = (x + k) & 3
        at = pl.ds(pl.multiple_of((xx & 1) * CHUNK, CHUNK), CHUNK)
        out = outs[4 + k]

        @pl.when((xx >> 1) == t)
        def _():
            out[...] = product(gm[at, :], gr[at, :], right).astype(BF16)

        @pl.when((xx >> 1) != t)
        def _():
            out[...] = product(gmt[at, :], grt[at, :], right).astype(BF16)


def cut_kernel(pos, *refs):
    a, b, outs = refs[:4], refs[4:8], refs[8:16]
    tmp = refs[16]
    x, y, t = pos[0], pos[2], pos[4]
    for n, parts in enumerate((a, b)):
        total = parts[0][...].astype(F32)
        for part in parts[1:]:
            total = total + part[...].astype(F32)
        tmp[...] = total
        for k in range(4):
            out = outs[4 * n + k]
            if n == 0:
                xx = (x + k) & 3
                row = pl.multiple_of(((xx >> 1) ^ t) * 256 + (xx & 1) * 128, 128)
                out[...] = tmp[pl.ds(row, 128), :].astype(out.dtype)
            else:
                for j in range(4):
                    row = pl.multiple_of(j * 128 + ((y + k) & 3) * SPAN, SPAN)
                    out[j * SPAN : (j + 1) * SPAN, :] = tmp[pl.ds(row, SPAN), :].astype(out.dtype)


def cut_last_kernel(pos, *refs):
    parts, outs, tmp = refs[:8], refs[8:12], refs[12]
    z = pos[1]
    for n in range(2):
        total = parts[4 * n][...]
        for part in parts[4 * n + 1 : 4 * n + 4]:
            total = total + part[...].astype(F32)
        tmp[:, n * HALF : (n + 1) * HALF] = total
    for k in range(4):
        row = pl.multiple_of(((z + k) & 3) * SPAN, SPAN)
        outs[k][...] = tmp[pl.ds(row, SPAN), :].astype(outs[k].dtype)


def proj_kernel(pos, gm, gr, gmt, grt, *refs):
    pieces, (weight, keep, send) = refs[:8], refs[8:]
    x, z, y, t = pos[0], pos[1], pos[2], pos[4]
    for k in range(4):
        for side in range(2):
            for i in range(4):
                for j in range(4):
                    xx, yy = ((x + i) & 3, (y + k) & 3) if side == 0 else ((x + k) & 3, (y + i) & 3)
                    row = pl.multiple_of(xx * 512 + ((z + j) & 3) * 128 + yy * 32, 32)
                    weight[pl.ds(row, SPAN), side * HALF : (side + 1) * HALF] = pieces[side * 4 + k][
                        (i * 4 + j) * SPAN : (i * 4 + j + 1) * SPAN, :
                    ]
    here = pl.ds(pl.multiple_of(t * DEPTH, DEPTH), DEPTH)
    there = pl.ds(pl.multiple_of((1 - t) * DEPTH, DEPTH), DEPTH)
    token = (((0,), (0,)), ((), ()))
    for out, a, b in ((send, gr, grt), (keep, gm, gmt)):
        out[...] = lax.dot_general(
            a[...], weight[here, :], token, preferred_element_type=F32
        ) + lax.dot_general(b[...], weight[there, :], token, preferred_element_type=F32)


def match_kernel(info, info_o, attn, attn_o, keep, send, out):
    for n, (i, a, p) in enumerate(((info, attn, keep), (info_o, attn_o, send))):
        columns = [jnp.sum(a[:ROWS, :].astype(F32) * p[...], axis=1, keepdims=True)]
        for slots in ((0, 1), (2,)):
            parts = []
            for b in range(NB):
                value = sum(chosen(i, j, b) * slot(a, j) for j in slots)
                parts.append(jnp.sum(value * p[b * BLOCK : (b + 1) * BLOCK, :], axis=1, keepdims=True))
            columns.append(jnp.concatenate(parts, axis=0))
        out[:, n * ROWS : (n + 1) * ROWS] = to_rows(columns)


def slope_kernel(info, info_o, attn, attn_o, gates, sums, sums_t, sums_c, sums_ct, hidden, weight, out, vector):
    heads = 0.0
    for n, (i, a) in enumerate(((info, attn), (info_o, attn_o))):
        cols = slice(n * ROWS, (n + 1) * ROWS)
        swapped = slice((1 - n) * ROWS, (2 - n) * ROWS)
        both = (sums[:, cols] + sums_t[:, cols]) + (sums_c[:, swapped] + sums_ct[:, swapped])
        match0, match1, match2 = both[0:1], both[1:2], both[2:3]
        g = gates[:, cols]
        gate0, gate1, gate2, along0, along1 = g[0:1], g[1:2], g[2:3], g[3:4], g[4:5]
        slope2 = mask_row(i, (2,)) * match2 * gate2 * (1.0 - gate2)
        slope1 = mask_row(i, (0, 1)) * (match1 + slope2 * along1) * gate1 * (1.0 - gate1)
        later0 = slope1 + slope2
        slope0 = (match0 + later0 * along0) * gate0 * (1.0 - gate0)
        total = later0 + slope0
        rows = jnp.concatenate(
            [gate0, gate1, gate2, later0, slope2, total, later0 * gate0, gate1 * slope2], axis=0
        )
        columns = to_columns(rows)
        heads = heads + jnp.sum(columns[:, 6:7] * a[:ROWS, :].astype(F32), axis=0, keepdims=True)
        for j in range(2):
            w = sum(chosen(i, j, b) * columns[b * BLOCK : (b + 1) * BLOCK, 7:8] for b in range(NB))
            heads = heads + jnp.sum(w * slot(a, j), axis=0, keepdims=True)
        if n == 0:
            out[...] = rows
            vector[:, HEADS : HEADS + WIDTH] = jnp.sum(
                columns[:, 5:6] * hidden[...].astype(F32), axis=0, keepdims=True
            )
    vector[:, :HEADS] = heads
    a = heads.astype(BF16)
    rest = heads - a.astype(F32)
    b = rest.astype(BF16)
    d = (rest - b.astype(F32)).astype(BF16)
    lhs = jnp.concatenate([a, b, d, jnp.zeros((13, HEADS), BF16)], axis=0)
    got = lax.dot_general(lhs, weight[...], (((1,), (1,)), ((), ())), preferred_element_type=F32)
    vector[:, HEADS + WIDTH :] = jnp.sum(got, axis=0, keepdims=True)


def grads_kernel(kept2, kept3, rows, keep, sent, heads, grad, router, gin, g1, g2, g3, proj):
    columns = to_columns(rows[...])
    gin[...] = (grad[...].astype(F32) + columns[:, 5:6] * router[...]).astype(BF16)
    proj[...] = keep[...] + sent[...]
    r = heads[...]
    g1[...] = (columns[:, 0:1] * (proj[...] + columns[:, 3:4] * r)).astype(BF16)

    def at_slot(kept, j):
        safe = jnp.maximum(kept[0, j], 0)
        live = (kept[0, j] >= 0).astype(F32)
        col = jnp.zeros((BLOCK, 128), F32)
        for b in range(NB):
            col = jnp.where(safe == b, columns[b * BLOCK : (b + 1) * BLOCK], col)
        return proj[pl.ds(pl.multiple_of(safe * BLOCK, BLOCK), BLOCK), :], col, live

    for j in range(2):
        p, col, live = at_slot(kept2, j)
        v = live * col[:, 1:2] * (p + col[:, 4:5] * r)
        g2[j * BLOCK : (j + 1) * BLOCK, :] = v.astype(BF16)
    p, col, live = at_slot(kept3, 0)
    g3[...] = (live * col[:, 2:3] * p).astype(BF16)


def local(
    hidden_in,
    attn_first,
    attn_second,
    attn_third,
    out_weight,
    router,
    kept_second,
    kept_third,
    grad_out,
):
    f = lax.axis_index("fsdp")
    t = lax.axis_index("tp")
    x, z, y, c = f // (NC * NY * NZ), f // (NC * NY) % NZ, f // NC % NY, f % NC
    pos = jnp.stack([x, z, y, c, t, t, t, t]).astype(jnp.int32)
    router_part = lax.dynamic_slice_in_dim(router, t * WIDTH, WIDTH, 0).reshape(1, WIDTH)

    block = jnp.concatenate(around(out_weight, "z"), axis=0)
    mine, other, info = call(
        split_kernel, [((DEPTH, ROWS), BF16)] * 2 + [((8, ROWS), F32)], [],
        pos, kept_second, kept_third, grad_out, hidden_in, router_part,
    )
    attn = jnp.concatenate([attn_first, attn_second, attn_third], axis=0)
    received, info_o, attn_o = shifted(other, "c", 1), shifted(info, "c", 1), shifted(attn, "c", 1)
    side = (info, info_o, attn, attn_o)
    grads = (mine, received, swap_tp(mine), swap_tp(received))
    first = jnp.concatenate(around(block[:, :HALF], "x"), axis=0)
    second = jnp.concatenate(around(block[:, HALF:], "y"), axis=0)
    pieces = around(first, "y") + around(second, "x")

    by_owner = router.reshape(NX, NZ, NY, NC, SPAN)
    by_owner = lax.dynamic_index_in_dim(by_owner, c, 3, keepdims=False)
    by_owner = jnp.concatenate([by_owner] * 2, axis=1)
    by_owner = lax.dynamic_slice_in_dim(by_owner, z, NZ, 1)
    double_x = jnp.concatenate([by_owner] * 2, axis=0)
    double_y = jnp.concatenate([by_owner] * 2, axis=2)
    router_a = lax.dynamic_index_in_dim(lax.dynamic_slice_in_dim(double_x, x, NX, 0), y, 2, keepdims=False)
    router_b = lax.dynamic_index_in_dim(lax.dynamic_slice_in_dim(double_y, y, NY, 2), x, 0, keepdims=False)
    router_a = router_a.reshape(CHUNK, 1)
    router_b = router_b.transpose(1, 0, 2).reshape(CHUNK, 1)
    heads_a = ring_sum(jnp.sum(first.astype(F32) * router_a, axis=0), "y")
    heads_b = ring_sum(jnp.sum(second.astype(F32) * router_b, axis=0), "x")
    router_heads = jnp.concatenate([heads_a, heads_b])
    router_heads = (router_heads + shifted(router_heads, "c", 1)).reshape(1, HEADS)

    sums = call(along_kernel, ((8, 2 * ROWS), F32), [], *side, router_heads)
    gates, scaled = call(
        scaled_kernel, [((8, 2 * ROWS), F32), ((2 * ROWS, HEADS), BF16)], [], *side, sums, swap_tp(sums)
    )

    *terms, later = call(
        term_kernel, [((CHUNK, HALF), BF16)] * 8 + [((8,), jnp.int32)], [], pos, *grads, scaled
    )

    def sent_round(parts, axis):
        return [parts[0]] + [shifted(parts[k], axis, -k) for k in (1, 2, 3)]

    quarter = [((CHUNK // 4, HALF), k) for k in (F32, BF16, BF16, BF16)]
    cuts = call(
        cut_kernel, quarter * 2, [((CHUNK, HALF), F32)],
        pos, *sent_round(terms[:4], "y"), *sent_round(terms[4:], "x"),
    )
    last = [((SPAN, HEADS), k) for k in (F32, BF16, BF16, BF16)]
    cuts = call(
        cut_last_kernel, last, [((4 * SPAN, HEADS), F32)],
        pos, *sent_round(cuts[:4], "x"), *sent_round(cuts[4:], "y"),
    )
    cuts = sent_round(cuts, "z")
    weight_sum = cuts[0] + (cuts[1].astype(F32) + cuts[2].astype(F32) + cuts[3].astype(F32))

    weight, keep, send = call(
        proj_kernel,
        [((WIDTH, HEADS), BF16), ((ROWS, HEADS), F32), ((ROWS, HEADS), F32)], [],
        later, *grads, *pieces,
    )
    sums = call(match_kernel, ((8, 2 * ROWS), F32), [], *side, keep, send)
    rows, vector = call(
        slope_kernel, [((8, ROWS), F32), ((1, HEADS + 2 * WIDTH), F32)], [],
        *side, gates, sums, *quad(sums), hidden_in, weight,
    )
    grad_in, grad_first, grad_second, grad_third = call(
        grads_kernel,
        [((ROWS, WIDTH), BF16), ((ROWS, HEADS), BF16), ((2 * BLOCK, HEADS), BF16), ((BLOCK, HEADS), BF16)],
        [((ROWS, HEADS), F32)],
        kept_second, kept_third, rows, keep, shifted(send, "c", 1), router_heads, grad_out, router_part,
    )
    vector = ring_sum(ring_sum(ring_sum(vector.reshape(-1), "x"), "y"), "z")
    heads_total, vector = vector[:HEADS], vector[HEADS:]
    by_t, by_c, by_ct = quad(vector)
    hidden_here = vector[:WIDTH] + by_c[:WIDTH]
    hidden_there = by_t[:WIDTH] + by_ct[:WIDTH]
    term = vector[WIDTH:] + by_t[WIDTH:]
    term_other = by_c[WIDTH:] + by_ct[WIDTH:]
    low = jnp.where(c == 0, term, term_other).reshape(-1, 1, SPAN)
    high = jnp.where(c == 0, term_other, term).reshape(-1, 1, SPAN)
    full = jnp.concatenate([low, high], axis=1).reshape(2, WIDTH)
    own = jnp.arange(2, dtype=jnp.int32)[:, None] == t
    full = (full + jnp.where(own, hidden_here[None, :], hidden_there[None, :])).reshape(-1)
    scale = float(ROWS * NF) ** (-0.5)
    router_grad = full * scale
    own_router = lax.dynamic_slice_in_dim(router, f * SPAN, SPAN, 0)
    weight_grad = ((weight_sum + own_router[:, None] * heads_total[None, :]) * scale).astype(BF16)
    return (grad_in, grad_first, grad_second, grad_third, weight_grad, router_grad)


def solution(mesh):
    return jax.shard_map(
        local,
        mesh=mesh,
        in_specs=(
            P("fsdp", "tp"),
            P("fsdp", "tp"),
            P("fsdp", "tp"),
            P("fsdp", "tp"),
            P("fsdp", "tp"),
            P(),
            P("fsdp", None),
            P("fsdp", None),
            P("fsdp", "tp"),
        ),
        out_specs=(
            P("fsdp", "tp"),
            P("fsdp", "tp"),
            P("fsdp", "tp"),
            P("fsdp", "tp"),
            P("fsdp", "tp"),
            P(),
        ),
        check_vma=False,
    )
```

```python
import jax
import jax.numpy as jnp
from jax import lax
from jax.experimental import pallas as pl
from jax.experimental.pallas import tpu as pltpu
from jax.sharding import PartitionSpec as P

NB = 3
NX, NZ, NY, NC = 4, 4, 4, 2
NF = NX * NZ * NY * NC
F32, BF16 = jnp.float32, jnp.bfloat16
ROWS, WIDTH, HEADS = 384, 2048, 1024
BLOCK = ROWS // NB
DEPTH = WIDTH // 2
HALF = HEADS // 2
SPAN = 32
CHUNK = 4 * 4 * SPAN
SIZES = {"x": NX, "z": NZ, "y": NY, "c": NC, "t": 2}
VMEM = pl.BlockSpec(memory_space=pltpu.VMEM)
SMEM = pl.BlockSpec(memory_space=pltpu.SMEM)


def shifted(v, axis, step):
    n = SIZES[axis]
    return lax.ppermute(v, axis, [((i + step) % n, i) for i in range(n)])


def paired(v, axis, bit):
    return lax.ppermute(v, axis, [(i ^ bit, i) for i in range(SIZES[axis])])


def swap_tp(v):
    return shifted(v, "t", 1)


def around(v, axis):
    return [v] + [shifted(v, axis, k) for k in (1, 2, 3)]


def ring_gather(v, axis):
    n = v.shape[0] // 2
    ahead, behind = shifted(v, axis, 1), shifted(v, axis, -1)
    return [v, ahead, behind, shifted(behind[:n], axis, -1), shifted(ahead[n:], axis, 1)]


def fly_sum(v, axis):
    v = v + paired(v, axis, 1)
    return v + paired(v, axis, 2)


def quad(v):
    return swap_tp(v), shifted(v, "c", 1), lax.ppermute(v, ("c", "t"), [(3 - i, i) for i in range(4)])


def call(kernel, outs, scratch, *args):
    def spec(dtype):
        return SMEM if dtype == jnp.int32 else VMEM

    single = not isinstance(outs, list)
    shapes = [jax.ShapeDtypeStruct(s, d) for s, d in ([outs] if single else outs)]
    got = pl.pallas_call(
        kernel,
        out_shape=shapes,
        in_specs=[spec(a.dtype) for a in args],
        out_specs=[spec(s.dtype) for s in shapes],
        scratch_shapes=[pltpu.VMEM(s, d) for s, d in scratch],
        compiler_params=pltpu.CompilerParams(vmem_limit_bytes=40 * 2**20),
        cost_estimate=pl.CostEstimate(flops=1, bytes_accessed=1, transcendentals=0),
    )(*args)
    return got[0] if single else got


def split_kernel(pos, kept2, kept3, grad, hidden, router, mine, other, info):
    c = pos[3]
    row = lax.broadcasted_iota(jnp.int32, (128, 256), 0)
    col = lax.broadcasted_iota(jnp.int32, (128, 256), 1)
    source = (row >> 5) * 64 + (row & 31)
    take = (col == source + c * 32).astype(F32).astype(BF16)
    leave = (col == source + (1 - c) * 32).astype(F32).astype(BF16)
    both = (((1,), (1,)), ((), ()))
    for k in range(WIDTH // 256):
        piece = grad[:, k * 256 : (k + 1) * 256]
        at = slice(k * 128, (k + 1) * 128)
        mine[at, :] = lax.dot_general(take, piece, both, preferred_element_type=F32).astype(BF16)
        other[at, :] = lax.dot_general(leave, piece, both, preferred_element_type=F32).astype(BF16)
    base = jnp.sum(hidden[...].astype(F32) * router[...], axis=1, keepdims=True)
    rows = to_rows([base])
    at = lax.broadcasted_iota(jnp.int32, (8, ROWS), 0)
    for k, value in enumerate((kept2[0, 0], kept2[0, 1], kept3[0, 0])):
        rows = jnp.where(at == k + 1, value.astype(F32), rows)
    info[:, :ROWS] = jnp.where(c == 0, rows, 0.0)
    info[:, ROWS:] = jnp.where(c == 0, 0.0, rows)


def to_rows(columns):
    lane = lax.broadcasted_iota(jnp.int32, (ROWS, 128), 1)
    wide = jnp.zeros((ROWS, 128), F32)
    for k, column in enumerate(columns):
        wide = jnp.where(lane == k, column, wide)
    return wide.T[:8]


def to_columns(rows):
    wide = jnp.concatenate([rows, jnp.zeros((128 - rows.shape[0], ROWS), F32)], axis=0)
    return wide.T


def chosen(info, j, b):
    return (info[j + 1 : j + 2, 0:1] == float(b)).astype(F32)


def mask_row(info, slots):
    b = (lax.broadcasted_iota(jnp.int32, (1, ROWS), 1) >> 7).astype(F32)
    mask = jnp.zeros((1, ROWS), F32)
    for j in slots:
        mask = jnp.where(info[j + 1 : j + 2, :] == b, 1.0, mask)
    return mask


def slot(attn, j):
    return attn[ROWS + j * BLOCK : ROWS + (j + 1) * BLOCK, :].astype(F32)


def along_kernel(info, info_o, attn, attn_o, heads, out):
    r = heads[...]
    for n, (i, a) in enumerate(((info, attn), (info_o, attn_o))):
        along0 = jnp.sum(a[:ROWS, :].astype(F32) * r, axis=1, keepdims=True)
        parts = [jnp.sum(slot(a, j) * r, axis=1, keepdims=True) for j in range(2)]
        along1 = jnp.concatenate(
            [chosen(i, 0, b) * parts[0] + chosen(i, 1, b) * parts[1] for b in range(NB)], axis=0
        )
        rows = to_rows([along0, along1])
        base = jnp.concatenate([jnp.zeros((2, ROWS), F32), i[0:1, :], jnp.zeros((5, ROWS), F32)], axis=0)
        out[:, n * ROWS : (n + 1) * ROWS] = rows + base


def scaled_kernel(info, info_o, attn, attn_o, sums, sent, gates, scaled):
    for n, (i, a) in enumerate(((info, attn), (info_o, attn_o))):
        cols = slice(n * ROWS, (n + 1) * ROWS)
        both = sums[:, cols] + sent[:, cols]
        along0, along1, base = both[0:1], both[1:2], both[2:3]
        gate0 = jax.nn.sigmoid(base)
        logit1 = base + gate0 * along0
        gate1 = jax.nn.sigmoid(logit1)
        gate2 = jax.nn.sigmoid(logit1 + mask_row(i, (0, 1)) * gate1 * along1)
        rows = jnp.concatenate([gate0, gate1, gate2, along0, along1, jnp.zeros((3, ROWS), F32)], axis=0)
        gates[:, cols] = rows
        columns = to_columns(rows)
        for b in range(NB):
            at = slice(b * BLOCK, (b + 1) * BLOCK)
            g = columns[at]
            total = (g[:, 0:1] * a[at, :].astype(F32)).astype(BF16).astype(F32)
            for j in range(3):
                w = g[:, 1:2] if j < 2 else g[:, 2:3]
                total = total + chosen(i, j, b) * (w * slot(a, j)).astype(BF16).astype(F32)
            scaled[n * ROWS + b * BLOCK : n * ROWS + (b + 1) * BLOCK, :] = total.astype(BF16)


def term_kernel(pos, gm, gr, gmt, grt, scaled, *refs):
    outs, later, lhs = refs[:10], refs[10], refs[11]
    x, y, t = pos[0], pos[2], pos[4]
    for k in range(8):
        later[k] = pos[k]
    half = CHUNK // 2
    for k in (2, 1, 3, 0):
        for side in range(2):
            if side == 0:
                for n, (a, b) in enumerate(((gm, gr), (gmt, grt))):
                    for g in range(8):
                        row = pl.multiple_of(g * 128 + ((y + k) & 3) * SPAN, SPAN)
                        at = slice(n * half + g * SPAN, n * half + (g + 1) * SPAN)
                        lhs[at, :ROWS] = a[pl.ds(row, SPAN), :]
                        lhs[at, ROWS:] = b[pl.ds(row, SPAN), :]
            else:
                xx = (x + k) & 3
                at = pl.ds(pl.multiple_of((xx & 1) * CHUNK, CHUNK), CHUNK)

                @pl.when((xx >> 1) == t)
                def _():
                    lhs[:, :ROWS] = gm[at, :]
                    lhs[:, ROWS:] = gr[at, :]

                @pl.when((xx >> 1) != t)
                def _():
                    lhs[:, :ROWS] = gmt[at, :]
                    lhs[:, ROWS:] = grt[at, :]

            plus, minus, add_plus, add_minus, own = outs[5 * side : 5 * side + 5]
            for h in range(2):
                rows = slice(h * half, (h + 1) * half)
                got = jnp.dot(
                    lhs[rows, :], scaled[:, side * HALF : (side + 1) * HALF], preferred_element_type=F32
                )
                if k == 0:
                    own[rows, :] = got
                elif (k, h) == (1, 0):
                    add_plus[...] = got
                elif (k, h) == (3, 1):
                    add_minus[...] = got
                else:
                    out = plus if (k, h) in ((2, 0), (1, 1)) else minus
                    out[rows, :] = got.astype(BF16)


def middle_kernel(*refs):
    half = CHUNK // 2
    for side in range(2):
        add_plus, got_plus, add_minus, got_minus = refs[4 * side : 4 * side + 4]
        refs[8 + 2 * side][...] = (add_plus[...] + got_plus[:half, :].astype(F32)).astype(BF16)
        refs[9 + 2 * side][...] = (add_minus[...] + got_minus[half:, :].astype(F32)).astype(BF16)


def cut_kernel(pos, *refs):
    outs, tmp = refs[10:18], refs[18]
    x, y, t = pos[0], pos[2], pos[4]
    half = CHUNK // 2
    for n in range(2):
        own, got_plus, got_minus, late_plus, late_minus = refs[5 * n : 5 * n + 5]
        tmp[:half, :] = own[:half, :] + got_minus[:half, :].astype(F32) + late_plus[...].astype(F32)
        tmp[half:, :] = own[half:, :] + got_plus[half:, :].astype(F32) + late_minus[...].astype(F32)
        for k in range(4):
            out = outs[4 * n + k]
            if n == 0:
                xx = (x + k) & 3
                row = pl.multiple_of(((xx >> 1) ^ t) * 256 + (xx & 1) * 128, 128)
                out[...] = tmp[pl.ds(row, 128), :].astype(out.dtype)
            else:
                for j in range(4):
                    row = pl.multiple_of(j * 128 + ((y + k) & 3) * SPAN, SPAN)
                    out[j * SPAN : (j + 1) * SPAN, :] = tmp[pl.ds(row, SPAN), :].astype(out.dtype)


def cut_last_kernel(pos, *refs):
    parts, outs, tmp = refs[:8], refs[8:12], refs[12]
    z = pos[1]
    for n in range(2):
        total = parts[4 * n][...]
        for part in parts[4 * n + 1 : 4 * n + 4]:
            total = total + part[...].astype(F32)
        tmp[:, n * HALF : (n + 1) * HALF] = total
    for k in range(4):
        row = pl.multiple_of(((z + k) & 3) * SPAN, SPAN)
        outs[k][...] = tmp[pl.ds(row, SPAN), :].astype(outs[k].dtype)


def proj_kernel(pos, gm, gr, gmt, grt, *refs):
    pieces, (weight, keep, send) = refs[:10], refs[10:]
    x, z, y, t = pos[0], pos[1], pos[2], pos[4]
    for k in range(4):
        for side in range(2):
            for i in range(4):
                for j in range(4):
                    xx, yy = ((x + i) & 3, (y + k) & 3) if side == 0 else ((x + k) & 3, (y + i) & 3)
                    row = pl.multiple_of(xx * 512 + ((z + j) & 3) * 128 + yy * 32, 32)
                    at = (i * 4 + j) * SPAN
                    piece = pieces[side * 5 + (0, 1, 3, 2)[k]]
                    if k == 2 and at >= CHUNK // 2:
                        piece, at = pieces[side * 5 + 4], at - CHUNK // 2
                    weight[pl.ds(row, SPAN), side * HALF : (side + 1) * HALF] = piece[at : at + SPAN, :]
    here = pl.ds(pl.multiple_of(t * DEPTH, DEPTH), DEPTH)
    there = pl.ds(pl.multiple_of((1 - t) * DEPTH, DEPTH), DEPTH)
    token = (((0,), (0,)), ((), ()))
    for out, a, b in ((send, gr, grt), (keep, gm, gmt)):
        out[...] = lax.dot_general(
            a[...], weight[here, :], token, preferred_element_type=F32
        ) + lax.dot_general(b[...], weight[there, :], token, preferred_element_type=F32)


def match_kernel(info, info_o, attn, attn_o, keep, send, out):
    for n, (i, a, p) in enumerate(((info, attn, keep), (info_o, attn_o, send))):
        columns = [jnp.sum(a[:ROWS, :].astype(F32) * p[...], axis=1, keepdims=True)]
        for slots in ((0, 1), (2,)):
            parts = []
            for b in range(NB):
                value = sum(chosen(i, j, b) * slot(a, j) for j in slots)
                parts.append(jnp.sum(value * p[b * BLOCK : (b + 1) * BLOCK, :], axis=1, keepdims=True))
            columns.append(jnp.concatenate(parts, axis=0))
        out[:, n * ROWS : (n + 1) * ROWS] = to_rows(columns)


def slope_kernel(info, info_o, attn, attn_o, gates, sums, sums_c, hidden, weight, out, vector):
    heads = 0.0
    for n, (i, a) in enumerate(((info, attn), (info_o, attn_o))):
        cols = slice(n * ROWS, (n + 1) * ROWS)
        swapped = slice((1 - n) * ROWS, (2 - n) * ROWS)
        both = sums[:, cols] + sums_c[:, swapped]
        match0, match1, match2 = both[0:1], both[1:2], both[2:3]
        g = gates[:, cols]
        gate0, gate1, gate2, along0, along1 = g[0:1], g[1:2], g[2:3], g[3:4], g[4:5]
        slope2 = mask_row(i, (2,)) * match2 * gate2 * (1.0 - gate2)
        slope1 = mask_row(i, (0, 1)) * (match1 + slope2 * along1) * gate1 * (1.0 - gate1)
        later0 = slope1 + slope2
        slope0 = (match0 + later0 * along0) * gate0 * (1.0 - gate0)
        total = later0 + slope0
        rows = jnp.concatenate(
            [gate0, gate1, gate2, later0, slope2, total, later0 * gate0, gate1 * slope2], axis=0
        )
        columns = to_columns(rows)
        heads = heads + jnp.sum(columns[:, 6:7] * a[:ROWS, :].astype(F32), axis=0, keepdims=True)
        for j in range(2):
            w = sum(chosen(i, j, b) * columns[b * BLOCK : (b + 1) * BLOCK, 7:8] for b in range(NB))
            heads = heads + jnp.sum(w * slot(a, j), axis=0, keepdims=True)
        if n == 0:
            out[...] = rows
            vector[:, HEADS : HEADS + WIDTH] = jnp.sum(
                columns[:, 5:6] * hidden[...].astype(F32), axis=0, keepdims=True
            )
    vector[:, :HEADS] = heads
    a = heads.astype(BF16)
    rest = heads - a.astype(F32)
    b = rest.astype(BF16)
    d = (rest - b.astype(F32)).astype(BF16)
    lhs = jnp.concatenate([a, b, d, jnp.zeros((13, HEADS), BF16)], axis=0)
    got = lax.dot_general(lhs, weight[...], (((1,), (1,)), ((), ())), preferred_element_type=F32)
    vector[:, HEADS + WIDTH :] = jnp.sum(got, axis=0, keepdims=True)


def grads_kernel(kept2, kept3, rows, keep, sent, heads, grad, router, gin, g1, g2, g3, proj):
    columns = to_columns(rows[...])
    gin[...] = (grad[...].astype(F32) + columns[:, 5:6] * router[...]).astype(BF16)
    proj[...] = keep[...] + sent[...]
    r = heads[...]
    g1[...] = (columns[:, 0:1] * (proj[...] + columns[:, 3:4] * r)).astype(BF16)

    def at_slot(kept, j):
        safe = jnp.maximum(kept[0, j], 0)
        live = (kept[0, j] >= 0).astype(F32)
        col = jnp.zeros((BLOCK, 128), F32)
        for b in range(NB):
            col = jnp.where(safe == b, columns[b * BLOCK : (b + 1) * BLOCK], col)
        return proj[pl.ds(pl.multiple_of(safe * BLOCK, BLOCK), BLOCK), :], col, live

    for j in range(2):
        p, col, live = at_slot(kept2, j)
        v = live * col[:, 1:2] * (p + col[:, 4:5] * r)
        g2[j * BLOCK : (j + 1) * BLOCK, :] = v.astype(BF16)
    p, col, live = at_slot(kept3, 0)
    g3[...] = (live * col[:, 2:3] * p).astype(BF16)


def local(
    hidden_in,
    attn_first,
    attn_second,
    attn_third,
    out_weight,
    router,
    kept_second,
    kept_third,
    grad_out,
):
    x, z, y, c, t = (lax.axis_index(a) for a in "xzyct")
    f = ((x * NZ + z) * NY + y) * NC + c
    pos = jnp.stack([x, z, y, c, t, t, t, t]).astype(jnp.int32)
    router_part = lax.dynamic_slice_in_dim(router, t * WIDTH, WIDTH, 0).reshape(1, WIDTH)

    block = jnp.concatenate(around(out_weight, "z"), axis=0)
    mine, other, info = call(
        split_kernel, [((DEPTH, ROWS), BF16)] * 2 + [((8, 2 * ROWS), F32)], [],
        pos, kept_second, kept_third, grad_out, hidden_in, router_part,
    )
    attn = jnp.concatenate([attn_first, attn_second, attn_third], axis=0)
    received, attn_o = shifted(other, "c", 1), shifted(attn, "c", 1)
    info = lax.psum(info, "c")
    info_o = jnp.where(c == 0, info[:, ROWS:], info[:, :ROWS])
    info = jnp.where(c == 0, info[:, :ROWS], info[:, ROWS:])
    side = (info, info_o, attn, attn_o)
    grads = (mine, received, swap_tp(mine), swap_tp(received))
    first = jnp.concatenate(around(block[:, :HALF], "x"), axis=0)
    second = jnp.concatenate(around(block[:, HALF:], "y"), axis=0)
    pieces = ring_gather(first, "y") + ring_gather(second, "x")

    by_owner = router.reshape(NX, NZ, NY, NC, SPAN)
    by_owner = lax.dynamic_index_in_dim(by_owner, c, 3, keepdims=False)
    by_owner = jnp.concatenate([by_owner] * 2, axis=1)
    by_owner = lax.dynamic_slice_in_dim(by_owner, z, NZ, 1)
    double_x = jnp.concatenate([by_owner] * 2, axis=0)
    double_y = jnp.concatenate([by_owner] * 2, axis=2)
    router_a = lax.dynamic_index_in_dim(lax.dynamic_slice_in_dim(double_x, x, NX, 0), y, 2, keepdims=False)
    router_b = lax.dynamic_index_in_dim(lax.dynamic_slice_in_dim(double_y, y, NY, 2), x, 0, keepdims=False)
    router_a = router_a.reshape(CHUNK, 1)
    router_b = router_b.transpose(1, 0, 2).reshape(CHUNK, 1)
    heads_a = lax.psum(jnp.sum(first.astype(F32) * router_a, axis=0), "y")
    heads_b = lax.psum(jnp.sum(second.astype(F32) * router_b, axis=0), "x")
    router_heads = lax.psum(jnp.concatenate([heads_a, heads_b]), "c").reshape(1, HEADS)

    sums = call(along_kernel, ((8, 2 * ROWS), F32), [], *side, router_heads)
    gates, scaled = call(
        scaled_kernel, [((8, 2 * ROWS), F32), ((2 * ROWS, HEADS), BF16)], [], *side, sums, swap_tp(sums)
    )

    full, part = (CHUNK, HALF), (CHUNK // 2, HALF)
    *terms, later = call(
        term_kernel,
        [(full, BF16), (full, BF16), (part, F32), (part, F32), (full, F32)] * 2 + [((8,), jnp.int32)],
        [((CHUNK, 2 * ROWS), BF16)], pos, *grads, scaled,
    )
    got = [[shifted(terms[5 * n], a, -1), shifted(terms[5 * n + 1], a, 1)] for n, a in enumerate("yx")]
    middle = call(
        middle_kernel, [(part, BF16)] * 4, [],
        *[v for n in range(2) for v in (terms[5 * n + 2], got[n][0], terms[5 * n + 3], got[n][1])],
    )
    late = [[shifted(middle[2 * n], a, -1), shifted(middle[2 * n + 1], a, 1)] for n, a in enumerate("yx")]

    def sent_round(parts, axis):
        return [parts[0]] + [shifted(parts[k], axis, -k) for k in (1, 2, 3)]

    quarter = [((CHUNK // 4, HALF), k) for k in (F32, BF16, BF16, BF16)]
    cuts = call(
        cut_kernel, quarter * 2, [((CHUNK, HALF), F32)],
        pos, *[v for n in range(2) for v in (terms[5 * n + 4], *got[n], *late[n])],
    )
    last = [((SPAN, HEADS), k) for k in (F32, BF16, BF16, BF16)]
    cuts = call(
        cut_last_kernel, last, [((4 * SPAN, HEADS), F32)],
        pos, *sent_round(cuts[:4], "x"), *sent_round(cuts[4:], "y"),
    )
    cuts = sent_round(cuts, "z")
    weight_sum = cuts[0] + (cuts[1].astype(F32) + cuts[2].astype(F32) + cuts[3].astype(F32))

    weight, keep, send = call(
        proj_kernel,
        [((WIDTH, HEADS), BF16), ((ROWS, HEADS), F32), ((ROWS, HEADS), F32)], [],
        later, *grads, *pieces,
    )
    sums = call(match_kernel, ((8, 2 * ROWS), F32), [], *side, keep, send)
    sums = sums + swap_tp(sums)
    rows, vector = call(
        slope_kernel, [((8, ROWS), F32), ((1, HEADS + 2 * WIDTH), F32)], [],
        *side, gates, sums, shifted(sums, "c", 1), hidden_in, weight,
    )
    grad_in, grad_first, grad_second, grad_third = call(
        grads_kernel,
        [((ROWS, WIDTH), BF16), ((ROWS, HEADS), BF16), ((2 * BLOCK, HEADS), BF16), ((BLOCK, HEADS), BF16)],
        [((ROWS, HEADS), F32)],
        kept_second, kept_third, rows, keep, shifted(send, "c", 1), router_heads, grad_out, router_part,
    )
    vector = fly_sum(fly_sum(fly_sum(vector.reshape(-1), "x"), "y"), "z")
    heads_total, vector = vector[:HEADS], vector[HEADS:]
    by_t, by_c, by_ct = quad(vector)
    hidden_here = vector[:WIDTH] + by_c[:WIDTH]
    hidden_there = by_t[:WIDTH] + by_ct[:WIDTH]
    term = vector[WIDTH:] + by_t[WIDTH:]
    term_other = by_c[WIDTH:] + by_ct[WIDTH:]
    low = jnp.where(c == 0, term, term_other).reshape(-1, 1, SPAN)
    high = jnp.where(c == 0, term_other, term).reshape(-1, 1, SPAN)
    full = jnp.concatenate([low, high], axis=1).reshape(2, WIDTH)
    own = jnp.arange(2, dtype=jnp.int32)[:, None] == t
    full = (full + jnp.where(own, hidden_here[None, :], hidden_there[None, :])).reshape(-1)
    scale = float(ROWS * NF) ** (-0.5)
    router_grad = full * scale
    own_router = lax.dynamic_slice_in_dim(router, f * SPAN, SPAN, 0)
    weight_grad = ((weight_sum + own_router[:, None] * heads_total[None, :]) * scale).astype(BF16)
    return (grad_in, grad_first, grad_second, grad_third, weight_grad, router_grad)


def solution(mesh):
    fine = jax.sharding.Mesh(mesh.devices.reshape(NX, NZ, NY, NC, 2), ("x", "z", "y", "c", "t"))
    rows = ("x", "z", "y", "c")
    both, lists = P(rows, "t"), P(rows, None)
    return jax.shard_map(
        local,
        mesh=fine,
        in_specs=(both, both, both, both, both, P(), lists, lists, both),
        out_specs=(both, both, both, both, both, P()),
        check_vma=False,
    )
```

```python
import jax
import jax.numpy as jnp
from jax import lax
from jax.experimental import pallas as pl
from jax.experimental.pallas import tpu as pltpu
from jax.sharding import PartitionSpec as P

NB = 3
NX, NZ, NY, NC = 4, 4, 4, 2
NF = NX * NZ * NY * NC
F32, BF16 = jnp.float32, jnp.bfloat16
ROWS, WIDTH, HEADS = 384, 2048, 1024
BLOCK = ROWS // NB
DEPTH = WIDTH // 2
HALF = HEADS // 2
SPAN = 32
CHUNK = 4 * 4 * SPAN
SIZES = {"x": NX, "z": NZ, "y": NY, "c": NC, "t": 2}
VMEM = pl.BlockSpec(memory_space=pltpu.VMEM)
SMEM = pl.BlockSpec(memory_space=pltpu.SMEM)


def shifted(v, axis, step):
    n = SIZES[axis]
    return lax.ppermute(v, axis, [((i + step) % n, i) for i in range(n)])


def paired(v, axis, bit):
    return lax.ppermute(v, axis, [(i ^ bit, i) for i in range(SIZES[axis])])


def swap_tp(v):
    return shifted(v, "t", 1)


def tie(*groups):
    return lax.optimization_barrier(groups)


def fly_sum(v, axis):
    v = v + paired(v, axis, 1)
    return v + paired(v, axis, 2)


def quad(v):
    return swap_tp(v), shifted(v, "c", 1), lax.ppermute(v, ("c", "t"), [(3 - i, i) for i in range(4)])


def call(kernel, outs, scratch, *args):
    def spec(dtype):
        return SMEM if dtype == jnp.int32 else VMEM

    single = not isinstance(outs, list)
    shapes = [jax.ShapeDtypeStruct(s, d) for s, d in ([outs] if single else outs)]
    got = pl.pallas_call(
        kernel,
        out_shape=shapes,
        in_specs=[spec(a.dtype) for a in args],
        out_specs=[spec(s.dtype) for s in shapes],
        scratch_shapes=[pltpu.VMEM(s, d) for s, d in scratch],
        compiler_params=pltpu.CompilerParams(vmem_limit_bytes=20 * 2**20),
        cost_estimate=pl.CostEstimate(flops=1, bytes_accessed=1, transcendentals=0),
    )(*args)
    return got[0] if single else got


def split_kernel(pos, kept2, kept3, grad, hidden, router, mine, other, info):
    c = pos[3]
    row = lax.broadcasted_iota(jnp.int32, (128, 256), 0)
    col = lax.broadcasted_iota(jnp.int32, (128, 256), 1)
    source = (row >> 5) * 64 + (row & 31)
    take = (col == source + c * 32).astype(F32).astype(BF16)
    leave = (col == source + (1 - c) * 32).astype(F32).astype(BF16)
    both = (((1,), (1,)), ((), ()))
    for k in range(WIDTH // 256):
        piece = grad[:, k * 256 : (k + 1) * 256]
        at = slice(k * 128, (k + 1) * 128)
        mine[at, :] = lax.dot_general(take, piece, both, preferred_element_type=F32).astype(BF16)
        other[at, :] = lax.dot_general(leave, piece, both, preferred_element_type=F32).astype(BF16)
    base = jnp.sum(hidden[...].astype(F32) * router[...], axis=1, keepdims=True)
    rows = to_rows([base])
    at = lax.broadcasted_iota(jnp.int32, (8, ROWS), 0)
    for k, value in enumerate((kept2[0, 0], kept2[0, 1], kept3[0, 0])):
        rows = jnp.where(at == k + 1, value.astype(F32), rows)
    info[:, :ROWS] = jnp.where(c == 0, rows, 0.0)
    info[:, ROWS:] = jnp.where(c == 0, 0.0, rows)


def to_rows(columns):
    lane = lax.broadcasted_iota(jnp.int32, (ROWS, 128), 1)
    wide = jnp.zeros((ROWS, 128), F32)
    for k, column in enumerate(columns):
        wide = jnp.where(lane == k, column, wide)
    return wide.T[:8]


def to_columns(rows):
    wide = jnp.concatenate([rows, jnp.zeros((128 - rows.shape[0], ROWS), F32)], axis=0)
    return wide.T


def chosen(info, j, b):
    return (info[j + 1 : j + 2, 0:1] == float(b)).astype(F32)


def mask_row(info, slots):
    b = (lax.broadcasted_iota(jnp.int32, (1, ROWS), 1) >> 7).astype(F32)
    mask = jnp.zeros((1, ROWS), F32)
    for j in slots:
        mask = jnp.where(info[j + 1 : j + 2, :] == b, 1.0, mask)
    return mask


def slot(attn, j):
    return attn[ROWS + j * BLOCK : ROWS + (j + 1) * BLOCK, :].astype(F32)


def along_kernel(info, info_o, attn, attn_o, heads, out):
    r = heads[...]
    for n, (i, a) in enumerate(((info, attn), (info_o, attn_o))):
        along0 = jnp.sum(a[:ROWS, :].astype(F32) * r, axis=1, keepdims=True)
        parts = [jnp.sum(slot(a, j) * r, axis=1, keepdims=True) for j in range(2)]
        along1 = jnp.concatenate(
            [chosen(i, 0, b) * parts[0] + chosen(i, 1, b) * parts[1] for b in range(NB)], axis=0
        )
        rows = to_rows([along0, along1])
        base = jnp.concatenate([jnp.zeros((2, ROWS), F32), i[0:1, :], jnp.zeros((5, ROWS), F32)], axis=0)
        out[:, n * ROWS : (n + 1) * ROWS] = rows + base


def scaled_kernel(info, info_o, attn, attn_o, sums, sent, gates, scaled):
    for n, (i, a) in enumerate(((info, attn), (info_o, attn_o))):
        cols = slice(n * ROWS, (n + 1) * ROWS)
        both = sums[:, cols] + sent[:, cols]
        along0, along1, base = both[0:1], both[1:2], both[2:3]
        gate0 = jax.nn.sigmoid(base)
        logit1 = base + gate0 * along0
        gate1 = jax.nn.sigmoid(logit1)
        gate2 = jax.nn.sigmoid(logit1 + mask_row(i, (0, 1)) * gate1 * along1)
        rows = jnp.concatenate([gate0, gate1, gate2, along0, along1, jnp.zeros((3, ROWS), F32)], axis=0)
        gates[:, cols] = rows
        columns = to_columns(rows)
        for b in range(NB):
            at = slice(b * BLOCK, (b + 1) * BLOCK)
            g = columns[at]
            total = (g[:, 0:1] * a[at, :].astype(F32)).astype(BF16).astype(F32)
            for j in range(3):
                w = g[:, 1:2] if j < 2 else g[:, 2:3]
                total = total + chosen(i, j, b) * (w * slot(a, j)).astype(BF16).astype(F32)
            scaled[n * ROWS + b * BLOCK : n * ROWS + (b + 1) * BLOCK, :] = total.astype(BF16)


def term_kernel(pos, gm, gr, gmt, grt, scaled, *refs):
    outs, later, lhs = refs[:10], refs[10], refs[11]
    x, y, t = pos[0], pos[2], pos[4]
    for k in range(8):
        later[k] = pos[k]
    half = CHUNK // 2
    for k in (2, 1, 3, 0):
        for side in range(2):
            if side == 0:
                for n, (a, b) in enumerate(((gm, gr), (gmt, grt))):
                    for g in range(8):
                        row = pl.multiple_of(g * 128 + ((y + k) & 3) * SPAN, SPAN)
                        at = slice(n * half + g * SPAN, n * half + (g + 1) * SPAN)
                        lhs[at, :ROWS] = a[pl.ds(row, SPAN), :]
                        lhs[at, ROWS:] = b[pl.ds(row, SPAN), :]
            else:
                xx = (x + k) & 3
                at = pl.ds(pl.multiple_of((xx & 1) * CHUNK, CHUNK), CHUNK)

                @pl.when((xx >> 1) == t)
                def _():
                    lhs[:, :ROWS] = gm[at, :]
                    lhs[:, ROWS:] = gr[at, :]

                @pl.when((xx >> 1) != t)
                def _():
                    lhs[:, :ROWS] = gmt[at, :]
                    lhs[:, ROWS:] = grt[at, :]

            plus, minus, add_plus, add_minus, own = outs[5 * side : 5 * side + 5]
            for h in range(2):
                rows = slice(h * half, (h + 1) * half)
                got = jnp.dot(
                    lhs[rows, :], scaled[:, side * HALF : (side + 1) * HALF], preferred_element_type=F32
                )
                if k == 0:
                    own[rows, :] = got
                elif (k, h) == (1, 0):
                    add_plus[...] = got
                elif (k, h) == (3, 1):
                    add_minus[...] = got
                else:
                    out = plus if (k, h) in ((2, 0), (1, 1)) else minus
                    out[rows, :] = got.astype(BF16)


def middle_kernel(*refs):
    half = CHUNK // 2
    for side in range(2):
        add_plus, got_plus, add_minus, got_minus = refs[4 * side : 4 * side + 4]
        refs[8 + 2 * side][...] = (add_plus[...] + got_plus[:half, :].astype(F32)).astype(BF16)
        refs[9 + 2 * side][...] = (add_minus[...] + got_minus[half:, :].astype(F32)).astype(BF16)


def cut_kernel(pos, *refs):
    outs, tmp = refs[10:18], refs[18]
    x, y, t = pos[0], pos[2], pos[4]
    half = CHUNK // 2
    for n in range(2):
        own, got_plus, got_minus, late_plus, late_minus = refs[5 * n : 5 * n + 5]
        tmp[:half, :] = own[:half, :] + got_minus[:half, :].astype(F32) + late_plus[...].astype(F32)
        tmp[half:, :] = own[half:, :] + got_plus[half:, :].astype(F32) + late_minus[...].astype(F32)
        for k in range(4):
            out = outs[4 * n + k]
            if n == 0:
                xx = (x + k) & 3
                row = pl.multiple_of(((xx >> 1) ^ t) * 256 + (xx & 1) * 128, 128)
                out[...] = tmp[pl.ds(row, 128), :].astype(out.dtype)
            else:
                for j in range(4):
                    row = pl.multiple_of(j * 128 + ((y + k) & 3) * SPAN, SPAN)
                    out[j * SPAN : (j + 1) * SPAN, :] = tmp[pl.ds(row, SPAN), :].astype(out.dtype)


def cut_last_kernel(pos, *refs):
    parts, outs, tmp = refs[:8], refs[8:12], refs[12]
    z = pos[1]
    for n in range(2):
        total = parts[4 * n][...]
        for part in parts[4 * n + 1 : 4 * n + 4]:
            total = total + part[...].astype(F32)
        tmp[:, n * HALF : (n + 1) * HALF] = total
    for k in range(4):
        row = pl.multiple_of(((z + k) & 3) * SPAN, SPAN)
        outs[k][...] = tmp[pl.ds(row, SPAN), :].astype(outs[k].dtype)


def proj_kernel(pos, gm, gr, gmt, grt, *refs):
    pieces, (weight, keep, send) = refs[:10], refs[10:]
    x, z, y, t = pos[0], pos[1], pos[2], pos[4]
    half = CHUNK // 2
    for n, k in enumerate((0, 1, 3, 2, 2)):
        piece = pieces[n]
        for g in range(piece.shape[0] // SPAN):
            row = (g + 8 * (n == 4)) * 128 + ((y + k) & 3) * SPAN
            weight[pl.ds(pl.multiple_of(row, SPAN), SPAN), :HALF] = piece[g * SPAN : (g + 1) * SPAN, :]
        piece = pieces[5 + n]
        row = pl.multiple_of(((x + k) & 3) * CHUNK + half * (n == 4), half)
        weight[pl.ds(row, piece.shape[0]), HALF:] = piece[...]
    here = pl.ds(pl.multiple_of(t * DEPTH, DEPTH), DEPTH)
    there = pl.ds(pl.multiple_of((1 - t) * DEPTH, DEPTH), DEPTH)
    token = (((0,), (0,)), ((), ()))
    for out, a, b in ((send, gr, grt), (keep, gm, gmt)):
        out[...] = lax.dot_general(
            a[...], weight[here, :], token, preferred_element_type=F32
        ) + lax.dot_general(b[...], weight[there, :], token, preferred_element_type=F32)


def match_kernel(info, info_o, attn, attn_o, keep, send, out):
    for n, (i, a, p) in enumerate(((info, attn, keep), (info_o, attn_o, send))):
        columns = [jnp.sum(a[:ROWS, :].astype(F32) * p[...], axis=1, keepdims=True)]
        for slots in ((0, 1), (2,)):
            parts = []
            for b in range(NB):
                value = sum(chosen(i, j, b) * slot(a, j) for j in slots)
                parts.append(jnp.sum(value * p[b * BLOCK : (b + 1) * BLOCK, :], axis=1, keepdims=True))
            columns.append(jnp.concatenate(parts, axis=0))
        out[:, n * ROWS : (n + 1) * ROWS] = to_rows(columns)


def slope_kernel(pos, info, info_o, attn, attn_o, gates, sums, sums_c, hidden, weight, out, vector):
    heads = 0.0
    for n, (i, a) in enumerate(((info, attn), (info_o, attn_o))):
        cols = slice(n * ROWS, (n + 1) * ROWS)
        swapped = slice((1 - n) * ROWS, (2 - n) * ROWS)
        both = sums[:, cols] + sums_c[:, swapped]
        match0, match1, match2 = both[0:1], both[1:2], both[2:3]
        g = gates[:, cols]
        gate0, gate1, gate2, along0, along1 = g[0:1], g[1:2], g[2:3], g[3:4], g[4:5]
        slope2 = mask_row(i, (2,)) * match2 * gate2 * (1.0 - gate2)
        slope1 = mask_row(i, (0, 1)) * (match1 + slope2 * along1) * gate1 * (1.0 - gate1)
        later0 = slope1 + slope2
        slope0 = (match0 + later0 * along0) * gate0 * (1.0 - gate0)
        total = later0 + slope0
        rows = jnp.concatenate(
            [gate0, gate1, gate2, later0, slope2, total, later0 * gate0, gate1 * slope2], axis=0
        )
        columns = to_columns(rows)
        heads = heads + jnp.sum(columns[:, 6:7] * a[:ROWS, :].astype(F32), axis=0, keepdims=True)
        for j in range(2):
            w = sum(chosen(i, j, b) * columns[b * BLOCK : (b + 1) * BLOCK, 7:8] for b in range(NB))
            heads = heads + jnp.sum(w * slot(a, j), axis=0, keepdims=True)
        if n == 0:
            out[...] = rows
            hid = jnp.sum(columns[:, 5:6] * hidden[...].astype(F32), axis=0, keepdims=True)
    vector[:, :HEADS] = heads
    lhs = split3(heads)
    got = lax.dot_general(lhs, weight[...], (((1,), (1,)), ((), ())), preferred_element_type=F32)
    term = jnp.sum(got, axis=0, keepdims=True)
    row = lax.broadcasted_iota(jnp.int32, (128, 256), 0)
    col = lax.broadcasted_iota(jnp.int32, (128, 256), 1)
    spread = (col == (row >> 5) * 64 + (row & 31) + pos[3] * SPAN).astype(F32).astype(BF16)
    for k in range(WIDTH // 128):
        piece = jnp.dot(split3(term[:, k * 128 : (k + 1) * 128]), spread, preferred_element_type=F32)
        piece = jnp.sum(piece, axis=0, keepdims=True)
        at = (k % 8) * 256
        here = hid[:, at : at + 256]
        vector[:, HEADS + k * 256 : HEADS + (k + 1) * 256] = piece + jnp.where(pos[4] == k // 8, here, 0.0)


def split3(v):
    a = v.astype(BF16)
    rest = v - a.astype(F32)
    b = rest.astype(BF16)
    d = (rest - b.astype(F32)).astype(BF16)
    return jnp.concatenate([a, b, d, jnp.zeros((13, v.shape[1]), BF16)], axis=0)


def block_kernel(pos, own, ahead, far, behind, router, left, right, heads):
    z = pos[1]
    for k, part in enumerate((own, ahead, far, behind)):
        row = pl.multiple_of(((z + k) & 3) * SPAN, SPAN)
        left[pl.ds(row, SPAN), :] = part[:, :HALF]
        right[pl.ds(row, SPAN), :] = part[:, HALF:]
    r = split3(router[...])
    for n, block in enumerate((left, right)):
        got = jnp.dot(r, block[...], preferred_element_type=F32)
        heads[:, n * HALF : (n + 1) * HALF] = jnp.sum(got, axis=0, keepdims=True)


def plane_kernel(pos, *refs):
    a, b, (left, right) = refs[:4], refs[4:8], refs[8:]
    x, y = pos[0], pos[2]
    for k in range(4):
        left[pl.ds(pl.multiple_of(((x + k) & 3) * 128, 128), 128), :] = a[k][...]
        for j in range(4):
            row = pl.multiple_of(j * 128 + ((y + k) & 3) * SPAN, SPAN)
            right[pl.ds(row, SPAN), :] = b[k][j * SPAN : (j + 1) * SPAN, :]


def final_kernel(own, ahead, far, behind, router, heads, out):
    total = own[...] + (ahead[...].astype(F32) + far[...].astype(F32) + behind[...].astype(F32))
    scale = float(ROWS * NF) ** (-0.5)
    out[...] = ((total + router[...] * heads[...]) * scale).astype(BF16)


def grads_kernel(kept2, kept3, rows, keep, sent, heads, grad, router, gin, g1, g2, g3, proj):
    columns = to_columns(rows[...])
    gin[...] = (grad[...].astype(F32) + columns[:, 5:6] * router[...]).astype(BF16)
    proj[...] = keep[...] + sent[...]
    r = heads[...]
    g1[...] = (columns[:, 0:1] * (proj[...] + columns[:, 3:4] * r)).astype(BF16)

    def at_slot(kept, j):
        safe = jnp.maximum(kept[0, j], 0)
        live = (kept[0, j] >= 0).astype(F32)
        col = jnp.zeros((BLOCK, 128), F32)
        for b in range(NB):
            col = jnp.where(safe == b, columns[b * BLOCK : (b + 1) * BLOCK], col)
        return proj[pl.ds(pl.multiple_of(safe * BLOCK, BLOCK), BLOCK), :], col, live

    for j in range(2):
        p, col, live = at_slot(kept2, j)
        v = live * col[:, 1:2] * (p + col[:, 4:5] * r)
        g2[j * BLOCK : (j + 1) * BLOCK, :] = v.astype(BF16)
    p, col, live = at_slot(kept3, 0)
    g3[...] = (live * col[:, 2:3] * p).astype(BF16)


def local(
    hidden_in,
    attn_first,
    attn_second,
    attn_third,
    out_weight,
    router,
    kept_second,
    kept_third,
    grad_out,
):
    x, z, y, c, t = (lax.axis_index(a) for a in "xzyct")
    f = ((x * NZ + z) * NY + y) * NC + c
    pos = jnp.stack([x, z, y, c, t, t, t, t]).astype(jnp.int32)
    router_part = lax.dynamic_slice_in_dim(router, t * WIDTH, WIDTH, 0).reshape(1, WIDTH)

    router_rows = lax.dynamic_slice(
        router.reshape(NX, NZ, NY, NC, SPAN), (x, 0, y, c, 0), (1, NZ, 1, 1, SPAN)
    ).reshape(1, NZ * SPAN)
    own_router = lax.dynamic_slice_in_dim(router, f * SPAN, SPAN, 0).reshape(SPAN, 1)
    half = CHUNK // 2

    zs = [shifted(out_weight, "z", k) for k in (1, 2, 3)]
    mine, other, info = call(
        split_kernel, [((DEPTH, ROWS), BF16)] * 2 + [((8, 2 * ROWS), F32)], [],
        pos, kept_second, kept_third, grad_out, hidden_in, router_part,
    )
    received = shifted(other, "c", 1)
    mine_t = swap_tp(mine)
    zs, received, mine = tie(zs, received, mine)
    left, right, heads = call(
        block_kernel, [((128, HALF), BF16)] * 2 + [((1, HEADS), F32)], [], pos, out_weight, *zs, router_rows
    )

    lefts = [shifted(left, "x", k) for k in (1, 2, 3)]
    rights = [shifted(right, "y", k) for k in (1, 2, 3)]
    attn = jnp.concatenate([attn_first, attn_second, attn_third], axis=0)
    heads = lax.psum(heads, "y")
    lefts, rights, heads, received, attn = tie(lefts, rights, heads, received, attn)
    left, right = call(plane_kernel, [((CHUNK, HALF), BF16)] * 2, [], pos, left, *lefts, right, *rights)

    pieces = [[left, shifted(left, "y", 1), shifted(left, "y", -1)]]
    pieces += [[right, shifted(right, "x", 1), shifted(right, "x", -1)]]
    heads = lax.psum(lax.psum(heads, "x"), "c")
    info = lax.psum(info, "c")
    pieces, heads, info, mine_t, received, attn = tie(pieces, heads, info, mine_t, received, attn)
    router_heads = heads
    info_o = jnp.where(c == 0, info[:, ROWS:], info[:, :ROWS])
    info = jnp.where(c == 0, info[:, :ROWS], info[:, ROWS:])
    for n, a in enumerate("yx"):
        pieces[n].append(shifted(pieces[n][2][:half], a, -1))
        pieces[n].append(shifted(pieces[n][1][half:], a, 1))
    received_t = swap_tp(received)
    attn_o = lax.optimization_barrier(shifted(attn, "c", 1))
    side = (info, info_o, attn, attn_o)

    sums = call(along_kernel, ((8, 2 * ROWS), F32), [], *side, router_heads)
    sent = lax.psum(sums, "t") - sums
    gates, scaled = call(
        scaled_kernel, [((8, 2 * ROWS), F32), ((2 * ROWS, HEADS), BF16)], [], *side, sums, sent
    )
    pieces, scaled, received_t = tie(pieces, scaled, received_t)
    grads = (mine, received, mine_t, received_t)

    full, part = (CHUNK, HALF), (CHUNK // 2, HALF)
    *terms, later = call(
        term_kernel,
        [(full, BF16), (full, BF16), (part, F32), (part, F32), (full, F32)] * 2 + [((8,), jnp.int32)],
        [((CHUNK, 2 * ROWS), BF16)], pos, *grads, scaled,
    )
    got = [[shifted(terms[5 * n], a, -1), shifted(terms[5 * n + 1], a, 1)] for n, a in enumerate("yx")]
    weight, keep, send = call(
        proj_kernel,
        [((WIDTH, HEADS), BF16), ((ROWS, HEADS), F32), ((ROWS, HEADS), F32)], [],
        later, *grads, *pieces[0], *pieces[1],
    )
    sums = call(match_kernel, ((8, 2 * ROWS), F32), [], *side, keep, send)
    sums = sums + swap_tp(sums)
    got, sums, keep, send, weight = tie(got, sums, keep, send, weight)
    middle = call(
        middle_kernel, [(part, BF16)] * 4, [],
        *[v for n in range(2) for v in (terms[5 * n + 2], got[n][0], terms[5 * n + 3], got[n][1])],
    )
    late = [[shifted(middle[2 * n], a, -1), shifted(middle[2 * n + 1], a, 1)] for n, a in enumerate("yx")]
    rows, vector = call(
        slope_kernel, [((8, ROWS), F32), ((1, HEADS + 2 * WIDTH), F32)], [],
        pos, *side, gates, sums, shifted(sums, "c", 1), hidden_in, weight,
    )
    late, rows, vector, send = tie(late, rows, vector, send)
    quarter = [((CHUNK // 4, HALF), k) for k in (F32, BF16, BF16, BF16)]
    cuts = call(
        cut_kernel, quarter * 2, [((CHUNK, HALF), F32)],
        pos, *[v for n in range(2) for v in (terms[5 * n + 4], *got[n], *late[n])],
    )

    def sent_round(parts, axis):
        return [parts[0]] + [shifted(parts[k], axis, -k) for k in (1, 2, 3)]

    cuts = sent_round(cuts[:4], "x") + sent_round(cuts[4:], "y")
    vector = fly_sum(vector.reshape(-1), "x")
    sent = shifted(send, "c", 1)
    cuts, vector, sent = tie(cuts, vector, sent)
    last = [((SPAN, HEADS), k) for k in (F32, BF16, BF16, BF16)]
    cuts = call(cut_last_kernel, last, [((4 * SPAN, HEADS), F32)], pos, *cuts)
    cuts = sent_round(cuts, "z")
    grad_in, grad_first, grad_second, grad_third = call(
        grads_kernel,
        [((ROWS, WIDTH), BF16), ((ROWS, HEADS), BF16), ((2 * BLOCK, HEADS), BF16), ((BLOCK, HEADS), BF16)],
        [((ROWS, HEADS), F32)],
        kept_second, kept_third, rows, keep, sent, router_heads, grad_out, router_part,
    )
    vector = fly_sum(vector, "y")
    cuts, vector = tie(cuts, vector)
    vector = fly_sum(vector, "z")
    weight_grad = call(
        final_kernel, ((SPAN, HEADS), BF16), [], *cuts, own_router, vector[:HEADS].reshape(1, HEADS)
    )
    vector = vector[HEADS:]
    by_t, by_c, by_ct = quad(vector)
    router_grad = ((vector + by_t) + (by_c + by_ct)) * float(ROWS * NF) ** (-0.5)
    return (grad_in, grad_first, grad_second, grad_third, weight_grad, router_grad)


def solution(mesh):
    fine = jax.sharding.Mesh(mesh.devices.reshape(NX, NZ, NY, NC, 2), ("x", "z", "y", "c", "t"))
    rows = ("x", "z", "y", "c")
    both, lists = P(rows, "t"), P(rows, None)
    return jax.shard_map(
        local,
        mesh=fine,
        in_specs=(both, both, both, both, both, P(), lists, lists, both),
        out_specs=(both, both, both, both, both, P()),
        check_vma=False,
    )
```

```python
import jax
import jax.numpy as jnp
from jax import lax
from jax.experimental import pallas as pl
from jax.experimental.pallas import tpu as pltpu
from jax.sharding import PartitionSpec as P

NB = 3
NX, NZ, NY, NC = 4, 4, 4, 2
NF = NX * NZ * NY * NC
F32, BF16 = jnp.float32, jnp.bfloat16
ROWS, WIDTH, HEADS = 384, 2048, 1024
BLOCK = ROWS // NB
DEPTH = WIDTH // 2
HALF = HEADS // 2
SPAN = 32
CHUNK = 4 * 4 * SPAN
SIZES = {"x": NX, "z": NZ, "y": NY, "c": NC, "t": 2}
VMEM = pl.BlockSpec(memory_space=pltpu.VMEM)
SMEM = pl.BlockSpec(memory_space=pltpu.SMEM)


def shifted(v, axis, step):
    n = SIZES[axis]
    return lax.ppermute(v, axis, [((i + step) % n, i) for i in range(n)])


def paired(v, axis, bit):
    return lax.ppermute(v, axis, [(i ^ bit, i) for i in range(SIZES[axis])])


def swap_tp(v):
    return shifted(v, "t", 1)


def tie(*groups):
    return lax.optimization_barrier(groups)


def fly_sum(v, axis):
    v = v + paired(v, axis, 1)
    return v + paired(v, axis, 2)


def quad(v):
    return swap_tp(v), shifted(v, "c", 1), lax.ppermute(v, ("c", "t"), [(3 - i, i) for i in range(4)])


def call(kernel, outs, scratch, *args, alias=None):
    def spec(dtype):
        return SMEM if dtype == jnp.int32 else VMEM

    single = not isinstance(outs, list)
    shapes = [jax.ShapeDtypeStruct(s, d) for s, d in ([outs] if single else outs)]
    got = pl.pallas_call(
        kernel,
        out_shape=shapes,
        in_specs=[spec(a.dtype) for a in args],
        out_specs=[spec(s.dtype) for s in shapes],
        scratch_shapes=[pltpu.VMEM(s, d) for s, d in scratch],
        input_output_aliases=alias or {},
        compiler_params=pltpu.CompilerParams(vmem_limit_bytes=20 * 2**20),
        cost_estimate=pl.CostEstimate(flops=1, bytes_accessed=1, transcendentals=0),
    )(*args)
    return got[0] if single else got


def split_kernel(pos, kept2, kept3, grad, hidden, router, mine, other, info, base_out):
    c = pos[3]
    row = lax.broadcasted_iota(jnp.int32, (128, 256), 0)
    col = lax.broadcasted_iota(jnp.int32, (128, 256), 1)
    source = (row >> 5) * 64 + (row & 31)
    take = (col == source + c * 32).astype(F32).astype(BF16)
    leave = (col == source + (1 - c) * 32).astype(F32).astype(BF16)
    both = (((1,), (1,)), ((), ()))
    for k in range(WIDTH // 256):
        piece = grad[:, k * 256 : (k + 1) * 256]
        at = slice(k * 128, (k + 1) * 128)
        mine[at, :] = lax.dot_general(take, piece, both, preferred_element_type=F32).astype(BF16)
        other[at, :] = lax.dot_general(leave, piece, both, preferred_element_type=F32).astype(BF16)
    base = jnp.sum(hidden[...].astype(F32) * router[...], axis=1, keepdims=True)
    rows = to_rows([base])
    base_out[...] = rows
    at = lax.broadcasted_iota(jnp.int32, (8, ROWS), 0)
    for k, value in enumerate((kept2[0, 0], kept2[0, 1], kept3[0, 0])):
        rows = jnp.where(at == k + 1, value.astype(F32), rows)
    info[:, :ROWS] = jnp.where(c == 0, rows, 0.0)
    info[:, ROWS:] = jnp.where(c == 0, 0.0, rows)


def to_rows(columns):
    lane = lax.broadcasted_iota(jnp.int32, (ROWS, 128), 1)
    wide = jnp.zeros((ROWS, 128), F32)
    for k, column in enumerate(columns):
        wide = jnp.where(lane == k, column, wide)
    return wide.T[:8]


def to_columns(rows):
    wide = jnp.concatenate([rows, jnp.zeros((128 - rows.shape[0], ROWS), F32)], axis=0)
    return wide.T


def chosen(info, j, b):
    return (info[j + 1 : j + 2, 0:1] == float(b)).astype(F32)


def mask_row(info, slots):
    b = (lax.broadcasted_iota(jnp.int32, (1, ROWS), 1) >> 7).astype(F32)
    mask = jnp.zeros((1, ROWS), F32)
    for j in slots:
        mask = jnp.where(info[j + 1 : j + 2, :] == b, 1.0, mask)
    return mask


def slot(attn, j):
    return attn[ROWS + j * BLOCK : ROWS + (j + 1) * BLOCK, :].astype(F32)


def halves_kernel(*refs):
    half = CHUNK // 2
    for n in range(2):
        ahead, behind = refs[2 * n], refs[2 * n + 1]
        refs[4 + 2 * n][...] = behind[:half, :]
        refs[5 + 2 * n][...] = ahead[half:, :]


def put_pieces(pos, pieces, which, weight):
    x, y = pos[0], pos[2]
    half = CHUNK // 2
    for n, k in which:
        piece = pieces[n]
        for g in range(piece.shape[0] // SPAN):
            row = (g + 8 * (n == 4)) * 128 + ((y + k) & 3) * SPAN
            weight[pl.ds(pl.multiple_of(row, SPAN), SPAN), :HALF] = piece[g * SPAN : (g + 1) * SPAN, :]
        piece = pieces[5 + n]
        row = pl.multiple_of(((x + k) & 3) * CHUNK + half * (n == 4), half)
        weight[pl.ds(row, piece.shape[0]), HALF:] = piece[...]


def near_kernel(pos, a0, a1, a2, b0, b1, b2, weight):
    put_pieces(pos, [a0, a1, a2, None, None, b0, b1, b2], ((0, 0), (1, 1), (2, 3)), weight)


def along_kernel(pos, info, info_o, attn, attn_o, base, router, a3, a4, b3, b4, weight_in, weight, heads, out):
    put_pieces(pos, [None] * 3 + [a3, a4] + [None] * 3 + [b3, b4], ((3, 2), (4, 2)), weight)
    r = jnp.sum(jnp.dot(split3(router[...]), weight[...], preferred_element_type=F32), axis=0, keepdims=True)
    heads[...] = r
    for n, (i, a) in enumerate(((info, attn), (info_o, attn_o))):
        along0 = jnp.sum(a[:ROWS, :].astype(F32) * r, axis=1, keepdims=True)
        parts = [jnp.sum(slot(a, j) * r, axis=1, keepdims=True) for j in range(2)]
        along1 = jnp.concatenate(
            [chosen(i, 0, b) * parts[0] + chosen(i, 1, b) * parts[1] for b in range(NB)], axis=0
        )
        rows = to_rows([along0, along1])
        if n == 0:
            first = jnp.concatenate([jnp.zeros((2, ROWS), F32), base[0:1, :], jnp.zeros((5, ROWS), F32)], axis=0)
            rows = rows + first
        out[:, n * ROWS : (n + 1) * ROWS] = rows


def quad_sum(n, sums, by_t, by_c, by_ct):
    cols = slice(n * ROWS, (n + 1) * ROWS)
    swapped = slice((1 - n) * ROWS, (2 - n) * ROWS)
    return (sums[:, cols] + by_t[:, cols]) + (by_c[:, swapped] + by_ct[:, swapped])


def scaled_kernel(info, info_o, attn, attn_o, sums, by_t, by_c, by_ct, gates, scaled):
    for n, (i, a) in enumerate(((info, attn), (info_o, attn_o))):
        cols = slice(n * ROWS, (n + 1) * ROWS)
        both = quad_sum(n, sums, by_t, by_c, by_ct)
        along0, along1, base = both[0:1], both[1:2], both[2:3]
        gate0 = jax.nn.sigmoid(base)
        logit1 = base + gate0 * along0
        gate1 = jax.nn.sigmoid(logit1)
        gate2 = jax.nn.sigmoid(logit1 + mask_row(i, (0, 1)) * gate1 * along1)
        rows = jnp.concatenate([gate0, gate1, gate2, along0, along1, jnp.zeros((3, ROWS), F32)], axis=0)
        gates[:, cols] = rows
        columns = to_columns(rows)
        for b in range(NB):
            at = slice(b * BLOCK, (b + 1) * BLOCK)
            g = columns[at]
            total = (g[:, 0:1] * a[at, :].astype(F32)).astype(BF16).astype(F32)
            for j in range(3):
                w = g[:, 1:2] if j < 2 else g[:, 2:3]
                total = total + chosen(i, j, b) * (w * slot(a, j)).astype(BF16).astype(F32)
            scaled[n * ROWS + b * BLOCK : n * ROWS + (b + 1) * BLOCK, :] = total.astype(BF16)


def term_kernel(pos, here, there, scaled, *refs):
    outs, later, lhs = refs[:10], refs[10], refs[11]
    x, y, t = pos[0], pos[2], pos[4]
    for k in range(8):
        later[k] = pos[k]
    half = CHUNK // 2
    for k in (2, 1, 3, 0):
        for side in range(2):
            if side == 0:
                for n, grads in enumerate((here, there)):
                    for g in range(8):
                        row = pl.multiple_of(g * 128 + ((y + k) & 3) * SPAN, SPAN)
                        at = slice(n * half + g * SPAN, n * half + (g + 1) * SPAN)
                        lhs[at, :] = grads[pl.ds(row, SPAN), :]
            else:
                xx = (x + k) & 3
                at = pl.ds(pl.multiple_of((xx & 1) * CHUNK, CHUNK), CHUNK)

                @pl.when((xx >> 1) == t)
                def _():
                    lhs[...] = here[at, :]

                @pl.when((xx >> 1) != t)
                def _():
                    lhs[...] = there[at, :]

            plus, minus, add_plus, add_minus, own = outs[5 * side : 5 * side + 5]
            for h in range(2):
                rows = slice(h * half, (h + 1) * half)
                got = jnp.dot(
                    lhs[rows, :], scaled[:, side * HALF : (side + 1) * HALF], preferred_element_type=F32
                )
                if k == 0:
                    own[rows, :] = got
                elif (k, h) == (1, 0):
                    add_plus[...] = got
                elif (k, h) == (3, 1):
                    add_minus[...] = got
                else:
                    out = plus if (k, h) in ((2, 0), (1, 1)) else minus
                    out[rows, :] = got.astype(BF16)


def middle_kernel(*refs):
    half = CHUNK // 2
    for side in range(2):
        add_plus, got_plus, add_minus, got_minus = refs[4 * side : 4 * side + 4]
        refs[8 + 2 * side][...] = (add_plus[...] + got_plus[:half, :].astype(F32)).astype(BF16)
        refs[9 + 2 * side][...] = (add_minus[...] + got_minus[half:, :].astype(F32)).astype(BF16)


def cut_kernel(pos, *refs):
    outs, tmp = refs[10:18], refs[18]
    x, y, t = pos[0], pos[2], pos[4]
    half = CHUNK // 2
    for n in range(2):
        own, got_plus, got_minus, late_plus, late_minus = refs[5 * n : 5 * n + 5]
        tmp[:half, :] = own[:half, :] + got_minus[:half, :].astype(F32) + late_plus[...].astype(F32)
        tmp[half:, :] = own[half:, :] + got_plus[half:, :].astype(F32) + late_minus[...].astype(F32)
        for k in range(4):
            out = outs[4 * n + k]
            if n == 0:
                xx = (x + k) & 3
                row = pl.multiple_of(((xx >> 1) ^ t) * 256 + (xx & 1) * 128, 128)
                out[...] = tmp[pl.ds(row, 128), :].astype(out.dtype)
            else:
                for j in range(4):
                    row = pl.multiple_of(j * 128 + ((y + k) & 3) * SPAN, SPAN)
                    out[j * SPAN : (j + 1) * SPAN, :] = tmp[pl.ds(row, SPAN), :].astype(out.dtype)


def cut_last_kernel(pos, *refs):
    parts, outs, tmp = refs[:8], refs[8:12], refs[12]
    z = pos[1]
    for n in range(2):
        total = parts[4 * n][...]
        for part in parts[4 * n + 1 : 4 * n + 4]:
            total = total + part[...].astype(F32)
        tmp[:, n * HALF : (n + 1) * HALF] = total
    for k in range(4):
        row = pl.multiple_of(((z + k) & 3) * SPAN, SPAN)
        outs[k][...] = tmp[pl.ds(row, SPAN), :].astype(outs[k].dtype)


def proj_kernel(pos, here, there, weight, keep, send):
    t = pos[4]
    own = pl.ds(pl.multiple_of(t * DEPTH, DEPTH), DEPTH)
    partner = pl.ds(pl.multiple_of((1 - t) * DEPTH, DEPTH), DEPTH)
    token = (((0,), (0,)), ((), ()))
    for out, at in ((send, slice(ROWS, 2 * ROWS)), (keep, slice(0, ROWS))):
        out[...] = lax.dot_general(
            here[:, at], weight[own, :], token, preferred_element_type=F32
        ) + lax.dot_general(there[:, at], weight[partner, :], token, preferred_element_type=F32)


def match_kernel(info, info_o, attn, attn_o, keep, send, out):
    for n, (i, a, p) in enumerate(((info, attn, keep), (info_o, attn_o, send))):
        columns = [jnp.sum(a[:ROWS, :].astype(F32) * p[...], axis=1, keepdims=True)]
        for slots in ((0, 1), (2,)):
            parts = []
            for b in range(NB):
                value = sum(chosen(i, j, b) * slot(a, j) for j in slots)
                parts.append(jnp.sum(value * p[b * BLOCK : (b + 1) * BLOCK, :], axis=1, keepdims=True))
            columns.append(jnp.concatenate(parts, axis=0))
        out[:, n * ROWS : (n + 1) * ROWS] = to_rows(columns)


def slope_kernel(pos, info, info_o, attn, attn_o, gates, sums, by_t, by_c, by_ct, hidden, weight, out, vector):
    heads = 0.0
    for n, (i, a) in enumerate(((info, attn), (info_o, attn_o))):
        cols = slice(n * ROWS, (n + 1) * ROWS)
        both = quad_sum(n, sums, by_t, by_c, by_ct)
        match0, match1, match2 = both[0:1], both[1:2], both[2:3]
        g = gates[:, cols]
        gate0, gate1, gate2, along0, along1 = g[0:1], g[1:2], g[2:3], g[3:4], g[4:5]
        slope2 = mask_row(i, (2,)) * match2 * gate2 * (1.0 - gate2)
        slope1 = mask_row(i, (0, 1)) * (match1 + slope2 * along1) * gate1 * (1.0 - gate1)
        later0 = slope1 + slope2
        slope0 = (match0 + later0 * along0) * gate0 * (1.0 - gate0)
        total = later0 + slope0
        rows = jnp.concatenate(
            [gate0, gate1, gate2, later0, slope2, total, later0 * gate0, gate1 * slope2], axis=0
        )
        columns = to_columns(rows)
        heads = heads + jnp.sum(columns[:, 6:7] * a[:ROWS, :].astype(F32), axis=0, keepdims=True)
        for j in range(2):
            w = sum(chosen(i, j, b) * columns[b * BLOCK : (b + 1) * BLOCK, 7:8] for b in range(NB))
            heads = heads + jnp.sum(w * slot(a, j), axis=0, keepdims=True)
        if n == 0:
            out[...] = rows
            hid = jnp.sum(columns[:, 5:6] * hidden[...].astype(F32), axis=0, keepdims=True)
    vector[:, :HEADS] = heads
    lhs = split3(heads)
    got = lax.dot_general(lhs, weight[...], (((1,), (1,)), ((), ())), preferred_element_type=F32)
    term = jnp.sum(got, axis=0, keepdims=True)
    row = lax.broadcasted_iota(jnp.int32, (128, 256), 0)
    col = lax.broadcasted_iota(jnp.int32, (128, 256), 1)
    spread = (col == (row >> 5) * 64 + (row & 31) + pos[3] * SPAN).astype(F32).astype(BF16)
    for k in range(WIDTH // 128):
        piece = jnp.dot(split3(term[:, k * 128 : (k + 1) * 128]), spread, preferred_element_type=F32)
        piece = jnp.sum(piece, axis=0, keepdims=True)
        at = (k % 8) * 256
        here = hid[:, at : at + 256]
        vector[:, HEADS + k * 256 : HEADS + (k + 1) * 256] = piece + jnp.where(pos[4] == k // 8, here, 0.0)


def split3(v):
    a = v.astype(BF16)
    rest = v - a.astype(F32)
    b = rest.astype(BF16)
    d = (rest - b.astype(F32)).astype(BF16)
    return jnp.concatenate([a, b, d, jnp.zeros((13, v.shape[1]), BF16)], axis=0)


def block_kernel(pos, own, ahead, far, behind, mine, received, left, right, here, later):
    z = pos[1]
    for k, part in enumerate((own, ahead, far, behind)):
        row = pl.multiple_of(((z + k) & 3) * SPAN, SPAN)
        left[pl.ds(row, SPAN), :] = part[:, :HALF]
        right[pl.ds(row, SPAN), :] = part[:, HALF:]
    here[:, :ROWS] = mine[...]
    here[:, ROWS:] = received[...]
    for k in range(8):
        later[k] = pos[k]


def attn_kernel(pos, first, second, third, attn):
    attn[:ROWS, :] = first[...]
    attn[ROWS : ROWS + 2 * BLOCK, :] = second[...]
    attn[ROWS + 2 * BLOCK :, :] = third[...]


def plane_kernel(pos, *refs):
    a, b, (left, right) = refs[:4], refs[4:8], refs[8:]
    x, y = pos[0], pos[2]
    for k in range(4):
        left[pl.ds(pl.multiple_of(((x + k) & 3) * 128, 128), 128), :] = a[k][...]
        for j in range(4):
            row = pl.multiple_of(j * 128 + ((y + k) & 3) * SPAN, SPAN)
            right[pl.ds(row, SPAN), :] = b[k][j * SPAN : (j + 1) * SPAN, :]


def final_kernel(own, ahead, far, behind, router, heads, out):
    total = own[...] + (ahead[...].astype(F32) + far[...].astype(F32) + behind[...].astype(F32))
    scale = float(ROWS * NF) ** (-0.5)
    out[...] = ((total + router[...] * heads[...]) * scale).astype(BF16)


def grads_kernel(kept2, kept3, rows, keep, sent, heads, heads_o, grad, router, gin, g1, g2, g3, proj):
    columns = to_columns(rows[...])
    gin[...] = (grad[...].astype(F32) + columns[:, 5:6] * router[...]).astype(BF16)
    proj[...] = keep[...] + sent[...]
    r = heads[...] + heads_o[...]
    g1[...] = (columns[:, 0:1] * (proj[...] + columns[:, 3:4] * r)).astype(BF16)

    def at_slot(kept, j):
        safe = jnp.maximum(kept[0, j], 0)
        live = (kept[0, j] >= 0).astype(F32)
        col = jnp.zeros((BLOCK, 128), F32)
        for b in range(NB):
            col = jnp.where(safe == b, columns[b * BLOCK : (b + 1) * BLOCK], col)
        return proj[pl.ds(pl.multiple_of(safe * BLOCK, BLOCK), BLOCK), :], col, live

    for j in range(2):
        p, col, live = at_slot(kept2, j)
        v = live * col[:, 1:2] * (p + col[:, 4:5] * r)
        g2[j * BLOCK : (j + 1) * BLOCK, :] = v.astype(BF16)
    p, col, live = at_slot(kept3, 0)
    g3[...] = (live * col[:, 2:3] * p).astype(BF16)


def local(
    hidden_in,
    attn_first,
    attn_second,
    attn_third,
    out_weight,
    router,
    kept_second,
    kept_third,
    grad_out,
):
    x, z, y, c, t = (lax.axis_index(a) for a in "xzyct")
    f = ((x * NZ + z) * NY + y) * NC + c
    pos = jnp.stack([x, z, y, c, t, t, t, t]).astype(jnp.int32)
    router_part = lax.dynamic_slice_in_dim(router, t * WIDTH, WIDTH, 0).reshape(1, WIDTH)

    router_half = lax.dynamic_index_in_dim(
        router.reshape(NX * NZ * NY, NC, SPAN), c, 1, keepdims=False
    ).reshape(1, WIDTH)
    own_router = lax.dynamic_slice_in_dim(router, f * SPAN, SPAN, 0).reshape(SPAN, 1)

    zs = [shifted(out_weight, "z", k) for k in (1, 2, 3)]
    mine, other, info, base = call(
        split_kernel, [((DEPTH, ROWS), BF16)] * 2 + [((8, 2 * ROWS), F32), ((8, ROWS), F32)], [],
        pos, kept_second, kept_third, grad_out, hidden_in, router_part,
    )
    received = shifted(other, "c", 1)
    info = lax.psum(info, "c")
    zs, received, info = tie(zs, received, info)
    left, right, here, later = call(
        block_kernel, [((128, HALF), BF16)] * 2 + [((DEPTH, 2 * ROWS), BF16), ((8,), jnp.int32)], [],
        pos, out_weight, *zs, mine, received,
    )

    lefts = [shifted(left, "x", k) for k in (1, 2, 3)]
    rights = [shifted(right, "y", k) for k in (1, 2, 3)]
    there = swap_tp(here)
    attn = call(
        attn_kernel, ((2 * ROWS, HEADS), BF16), [], later, attn_first, attn_second, attn_third
    )
    attn_o = shifted(attn, "c", 1)
    lefts, rights, attn_o = tie(lefts, rights, attn_o)
    left, right = call(plane_kernel, [((CHUNK, HALF), BF16)] * 2, [], pos, left, *lefts, right, *rights)
    info_o = jnp.where(c == 0, info[:, ROWS:], info[:, :ROWS])
    info = jnp.where(c == 0, info[:, :ROWS], info[:, ROWS:])
    side = (info, info_o, attn, attn_o)

    near = [shifted(left, "y", 1), shifted(left, "y", -1), shifted(right, "x", 1), shifted(right, "x", -1)]
    near = tie(*near)
    full, part = (CHUNK, HALF), (CHUNK // 2, HALF)
    cut = call(halves_kernel, [(part, BF16)] * 4, [], *near)
    far = [shifted(cut[0], "y", -1), shifted(cut[1], "y", 1), shifted(cut[2], "x", -1), shifted(cut[3], "x", 1)]
    weight = call(
        near_kernel, ((WIDTH, HEADS), BF16), [], pos, left, near[0], near[1], right, near[2], near[3]
    )
    far, weight, there = tie(far, weight, there)

    weight, heads, sums = call(
        along_kernel, [((WIDTH, HEADS), BF16), ((1, HEADS), F32), ((8, 2 * ROWS), F32)], [],
        pos, *side, base, router_half, *far, weight, alias={11: 0},
    )
    others, heads_o = quad(sums), shifted(heads, "c", 1)
    keep, send = call(proj_kernel, [((ROWS, HEADS), F32)] * 2, [], pos, here, there, weight)
    others, heads_o, keep, send = tie(others, heads_o, keep, send)
    gates, scaled = call(
        scaled_kernel, [((8, 2 * ROWS), F32), ((2 * ROWS, HEADS), BF16)], [], *side, sums, *others
    )
    sums = call(match_kernel, ((8, 2 * ROWS), F32), [], *side, keep, send)
    sums, scaled = tie(sums, scaled)
    others = quad(sums)

    *terms, later = call(
        term_kernel,
        [(full, BF16), (full, BF16), (part, F32), (part, F32), (full, F32)] * 2 + [((8,), jnp.int32)],
        [((CHUNK, 2 * ROWS), BF16)], pos, here, there, scaled,
    )
    terms, others, send, later = tie(terms, others, send, later)
    got = [[shifted(terms[5 * n], a, -1), shifted(terms[5 * n + 1], a, 1)] for n, a in enumerate("yx")]
    sent = shifted(send, "c", 1)
    rows, vector = call(
        slope_kernel, [((8, ROWS), F32), ((1, HEADS + 2 * WIDTH), F32)], [],
        later, *side, gates, sums, *others, hidden_in, weight,
    )
    got, sent, vector = tie(got, sent, vector)
    middle = call(
        middle_kernel, [(part, BF16)] * 4, [],
        *[v for n in range(2) for v in (terms[5 * n + 2], got[n][0], terms[5 * n + 3], got[n][1])],
    )
    late = [[shifted(middle[2 * n], a, -1), shifted(middle[2 * n + 1], a, 1)] for n, a in enumerate("yx")]
    vector = fly_sum(vector.reshape(-1), "x")
    late, vector = tie(late, vector)
    quarter = [((CHUNK // 4, HALF), k) for k in (F32, BF16, BF16, BF16)]
    cuts = call(
        cut_kernel, quarter * 2, [((CHUNK, HALF), F32)],
        pos, *[v for n in range(2) for v in (terms[5 * n + 4], *got[n], *late[n])],
    )

    def sent_round(parts, axis):
        return [parts[0]] + [shifted(parts[k], axis, -k) for k in (1, 2, 3)]

    cuts = sent_round(cuts[:4], "x") + sent_round(cuts[4:], "y")
    vector = fly_sum(vector, "y")
    cuts, rows, vector = tie(cuts, rows, vector)
    last = [((SPAN, HEADS), k) for k in (F32, BF16, BF16, BF16)]
    cuts = call(cut_last_kernel, last, [((4 * SPAN, HEADS), F32)], pos, *cuts)
    cuts = sent_round(cuts, "z")
    grads = call(
        grads_kernel,
        [((ROWS, WIDTH), BF16), ((ROWS, HEADS), BF16), ((2 * BLOCK, HEADS), BF16), ((BLOCK, HEADS), BF16)],
        [((ROWS, HEADS), F32)],
        kept_second, kept_third, rows, keep, sent, heads, heads_o, grad_out, router_part,
    )
    vector = fly_sum(vector, "z")
    cuts, grads, vector = tie(cuts, grads, vector)
    weight_grad = call(
        final_kernel, ((SPAN, HEADS), BF16), [], *cuts, own_router, vector[:HEADS].reshape(1, HEADS)
    )
    vector = vector[HEADS:]
    by_t, by_c, by_ct = quad(vector)
    router_grad = ((vector + by_t) + (by_c + by_ct)) * float(ROWS * NF) ** (-0.5)
    return (*grads, weight_grad, router_grad)


def solution(mesh):
    fine = jax.sharding.Mesh(mesh.devices.reshape(NX, NZ, NY, NC, 2), ("x", "z", "y", "c", "t"))
    rows = ("x", "z", "y", "c")
    both, lists = P(rows, "t"), P(rows, None)
    return jax.shard_map(
        local,
        mesh=fine,
        in_specs=(both, both, both, both, both, P(), lists, lists, both),
        out_specs=(both, both, both, both, both, P()),
        check_vma=False,
    )
```

```python
import jax
import jax.numpy as jnp
from jax import lax
from jax.experimental import pallas as pl
from jax.experimental.pallas import tpu as pltpu
from jax.sharding import PartitionSpec as P

NB = 3
NX, NZ, NY, NC = 4, 4, 4, 2
NF = NX * NZ * NY * NC
F32, BF16 = jnp.float32, jnp.bfloat16
ROWS, WIDTH, HEADS = 384, 2048, 1024
BLOCK = ROWS // NB
DEPTH = WIDTH // 2
HALF = HEADS // 2
SPAN = 32
CHUNK = 4 * 4 * SPAN
SIZES = {"x": NX, "z": NZ, "y": NY, "c": NC, "t": 2}
VMEM = pl.BlockSpec(memory_space=pltpu.VMEM)
SMEM = pl.BlockSpec(memory_space=pltpu.SMEM)


def shifted(v, axis, step):
    n = SIZES[axis]
    return lax.ppermute(v, axis, [((i + step) % n, i) for i in range(n)])


def paired(v, axis, bit):
    return lax.ppermute(v, axis, [(i ^ bit, i) for i in range(SIZES[axis])])


def swap_tp(v):
    return shifted(v, "t", 1)


def tie(*groups):
    return lax.optimization_barrier(groups)


def ring_sum(v, axis):
    a, b, c = (shifted(v, axis, k) for k in (1, 2, 3))
    return (v + a) + (b + c)


def fly_sum(v, axis):
    v = v + paired(v, axis, 1)
    return v + paired(v, axis, 2)


def quad(v):
    return swap_tp(v), shifted(v, "c", 1), lax.ppermute(v, ("c", "t"), [(3 - i, i) for i in range(4)])


def call(kernel, outs, scratch, *args, alias=None):
    def spec(dtype):
        return SMEM if dtype == jnp.int32 else VMEM

    single = not isinstance(outs, list)
    shapes = [jax.ShapeDtypeStruct(s, d) for s, d in ([outs] if single else outs)]
    got = pl.pallas_call(
        kernel,
        out_shape=shapes,
        in_specs=[spec(a.dtype) for a in args],
        out_specs=[spec(s.dtype) for s in shapes],
        scratch_shapes=[pltpu.VMEM(s, d) for s, d in scratch],
        input_output_aliases=alias or {},
        compiler_params=pltpu.CompilerParams(vmem_limit_bytes=20 * 2**20),
        cost_estimate=pl.CostEstimate(flops=1, bytes_accessed=1, transcendentals=0),
    )(*args)
    return got[0] if single else got


def split_kernel(pos, kept2, kept3, grad, mine, other, info):
    c = pos[3]
    row = lax.broadcasted_iota(jnp.int32, (128, 256), 0)
    col = lax.broadcasted_iota(jnp.int32, (128, 256), 1)
    source = (row >> 5) * 64 + (row & 31)
    take = (col == source + c * 32).astype(F32).astype(BF16)
    leave = (col == source + (1 - c) * 32).astype(F32).astype(BF16)
    both = (((1,), (1,)), ((), ()))
    for k in range(WIDTH // 256):
        piece = grad[:, k * 256 : (k + 1) * 256]
        at = slice(k * 128, (k + 1) * 128)
        mine[at, :] = lax.dot_general(take, piece, both, preferred_element_type=F32).astype(BF16)
        other[at, :] = lax.dot_general(leave, piece, both, preferred_element_type=F32).astype(BF16)
    rows = jnp.zeros((8, ROWS), F32)
    at = lax.broadcasted_iota(jnp.int32, (8, ROWS), 0)
    for k, value in enumerate((kept2[0, 0], kept2[0, 1], kept3[0, 0])):
        rows = jnp.where(at == k + 1, value.astype(F32), rows)
    info[:, :ROWS] = jnp.where(c == 0, rows, 0.0)
    info[:, ROWS:] = jnp.where(c == 0, 0.0, rows)


def to_rows(columns):
    lane = lax.broadcasted_iota(jnp.int32, (ROWS, 128), 1)
    wide = jnp.zeros((ROWS, 128), F32)
    for k, column in enumerate(columns):
        wide = jnp.where(lane == k, column, wide)
    return wide.T[:8]


def to_columns(rows):
    wide = jnp.concatenate([rows, jnp.zeros((128 - rows.shape[0], ROWS), F32)], axis=0)
    return wide.T


def chosen(info, j, b):
    return (info[j + 1 : j + 2, 0:1] == float(b)).astype(F32)


def mask_row(info, slots):
    b = (lax.broadcasted_iota(jnp.int32, (1, ROWS), 1) >> 7).astype(F32)
    mask = jnp.zeros((1, ROWS), F32)
    for j in slots:
        mask = jnp.where(info[j + 1 : j + 2, :] == b, 1.0, mask)
    return mask


def slot(attn, j):
    return attn[ROWS + j * BLOCK : ROWS + (j + 1) * BLOCK, :].astype(F32)


def put_pieces(pos, pieces, which, weight):
    x, y = pos[0], pos[2]
    for n, k in enumerate(which):
        left, right = pieces[2 * n], pieces[2 * n + 1]
        for g in range(16):
            row = pl.multiple_of(g * 128 + ((y + k) & 3) * SPAN, SPAN)
            weight[pl.ds(row, SPAN), :HALF] = left[g * SPAN : (g + 1) * SPAN, :]
        weight[pl.ds(pl.multiple_of(((x + k) & 3) * CHUNK, CHUNK), CHUNK), HALF:] = right[...]


def near_kernel(pos, *refs):
    put_pieces(pos, refs[:6], (0, 1, 3), refs[6])


def along_kernel(pos, info, info_o, attn, attn_o, base, router, left, right, weight_in, weight, heads, out):
    put_pieces(pos, (left, right), (2,), weight)
    r = jnp.sum(jnp.dot(split3(router[...]), weight[...], preferred_element_type=F32), axis=0, keepdims=True)
    heads[...] = r
    for n, (i, a) in enumerate(((info, attn), (info_o, attn_o))):
        along0 = jnp.sum(a[:ROWS, :].astype(F32) * r, axis=1, keepdims=True)
        parts = [jnp.sum(slot(a, j) * r, axis=1, keepdims=True) for j in range(2)]
        along1 = jnp.concatenate(
            [chosen(i, 0, b) * parts[0] + chosen(i, 1, b) * parts[1] for b in range(NB)], axis=0
        )
        rows = to_rows([along0, along1])
        if n == 0:
            first = jnp.concatenate([jnp.zeros((2, ROWS), F32), base[0:1, :], jnp.zeros((5, ROWS), F32)], axis=0)
            rows = rows + first
        out[:, n * ROWS : (n + 1) * ROWS] = rows


def quad_sum(n, sums, by_t, by_c, by_ct):
    cols = slice(n * ROWS, (n + 1) * ROWS)
    swapped = slice((1 - n) * ROWS, (2 - n) * ROWS)
    return (sums[:, cols] + by_t[:, cols]) + (by_c[:, swapped] + by_ct[:, swapped])


def scaled_kernel(info, info_o, attn, attn_o, sums, by_t, by_c, by_ct, gates, scaled):
    for n, (i, a) in enumerate(((info, attn), (info_o, attn_o))):
        cols = slice(n * ROWS, (n + 1) * ROWS)
        both = quad_sum(n, sums, by_t, by_c, by_ct)
        along0, along1, base = both[0:1], both[1:2], both[2:3]
        gate0 = jax.nn.sigmoid(base)
        logit1 = base + gate0 * along0
        gate1 = jax.nn.sigmoid(logit1)
        gate2 = jax.nn.sigmoid(logit1 + mask_row(i, (0, 1)) * gate1 * along1)
        rows = jnp.concatenate([gate0, gate1, gate2, along0, along1, jnp.zeros((3, ROWS), F32)], axis=0)
        gates[:, cols] = rows
        columns = to_columns(rows)
        for b in range(NB):
            at = slice(b * BLOCK, (b + 1) * BLOCK)
            g = columns[at]
            total = (g[:, 0:1] * a[at, :].astype(F32)).astype(BF16).astype(F32)
            for j in range(3):
                w = g[:, 1:2] if j < 2 else g[:, 2:3]
                total = total + chosen(i, j, b) * (w * slot(a, j)).astype(BF16).astype(F32)
            scaled[n * ROWS + b * BLOCK : n * ROWS + (b + 1) * BLOCK, :] = total.astype(BF16)


def term_kernel(pos, here0, here1, there0, there1, scaled, *refs):
    outs, later, lhs = refs[:8], refs[8], refs[9]
    x, y, t = pos[0], pos[2], pos[4]
    for k in range(8):
        later[k] = pos[k]
    for k in (1, 3, 2, 0):
        out = outs[k]
        for n, grads in enumerate((here0, here1, there0, there1)):
            for g in range(4):
                row = pl.multiple_of(g * 128 + ((y + k) & 3) * SPAN, SPAN)
                at = slice(n * 128 + g * SPAN, n * 128 + (g + 1) * SPAN)
                lhs[at, :] = grads[pl.ds(row, SPAN), :]
        out[...] = jnp.dot(lhs[...], scaled[:, :HALF], preferred_element_type=F32).astype(out.dtype)
        xx = (x + k) & 3
        for n, grads in enumerate((here0, here1, there0, there1)):
            half = t if n < 2 else 1 - t

            @pl.when(xx == 2 * half + n % 2)
            def _():
                got = jnp.dot(grads[...], scaled[:, HALF:], preferred_element_type=F32)
                outs[4 + k][...] = got.astype(outs[4 + k].dtype)


def cut_kernel(pos, *refs):
    outs, tmp = refs[8:16], refs[16]
    x, y, t = pos[0], pos[2], pos[4]
    for n in range(2):
        total = refs[4 * n][...]
        for part in refs[4 * n + 1 : 4 * n + 4]:
            total = total + part[...].astype(F32)
        tmp[...] = total
        for k in range(4):
            out = outs[4 * n + k]
            if n == 0:
                xx = (x + k) & 3
                row = pl.multiple_of(((xx >> 1) ^ t) * 256 + (xx & 1) * 128, 128)
                out[...] = tmp[pl.ds(row, 128), :].astype(out.dtype)
            else:
                for j in range(4):
                    row = pl.multiple_of(j * 128 + ((y + k) & 3) * SPAN, SPAN)
                    out[j * SPAN : (j + 1) * SPAN, :] = tmp[pl.ds(row, SPAN), :].astype(out.dtype)


def cut_last_kernel(pos, *refs):
    parts, outs, tmp = refs[:8], refs[8:12], refs[12]
    z = pos[1]
    for n in range(2):
        total = parts[4 * n][...]
        for part in parts[4 * n + 1 : 4 * n + 4]:
            total = total + part[...].astype(F32)
        tmp[:, n * HALF : (n + 1) * HALF] = total
    for k in range(4):
        row = pl.multiple_of(((z + k) & 3) * SPAN, SPAN)
        outs[k][...] = tmp[pl.ds(row, SPAN), :].astype(outs[k].dtype)


def proj_kernel(pos, here0, here1, there0, there1, weight, keep, send):
    t = pos[4]
    token = (((0,), (0,)), ((), ()))
    for out, at in ((send, slice(ROWS, 2 * ROWS)), (keep, slice(0, ROWS))):
        total = 0.0
        for n, grads in enumerate((here0, here1, there0, there1)):
            half = t if n < 2 else 1 - t
            rows = pl.ds(pl.multiple_of((2 * half + n % 2) * CHUNK, CHUNK), CHUNK)
            total = total + lax.dot_general(
                grads[:, at], weight[rows, :], token, preferred_element_type=F32
            )
        out[...] = total


def match_kernel(info, info_o, attn, attn_o, keep, send, out):
    for n, (i, a, p) in enumerate(((info, attn, keep), (info_o, attn_o, send))):
        columns = [jnp.sum(a[:ROWS, :].astype(F32) * p[...], axis=1, keepdims=True)]
        for slots in ((0, 1), (2,)):
            parts = []
            for b in range(NB):
                value = sum(chosen(i, j, b) * slot(a, j) for j in slots)
                parts.append(jnp.sum(value * p[b * BLOCK : (b + 1) * BLOCK, :], axis=1, keepdims=True))
            columns.append(jnp.concatenate(parts, axis=0))
        out[:, n * ROWS : (n + 1) * ROWS] = to_rows(columns)


def slope_kernel(pos, info, info_o, attn, attn_o, gates, sums, by_t, by_c, by_ct, hidden, weight, out, vector):
    heads = 0.0
    for n, (i, a) in enumerate(((info, attn), (info_o, attn_o))):
        cols = slice(n * ROWS, (n + 1) * ROWS)
        both = quad_sum(n, sums, by_t, by_c, by_ct)
        match0, match1, match2 = both[0:1], both[1:2], both[2:3]
        g = gates[:, cols]
        gate0, gate1, gate2, along0, along1 = g[0:1], g[1:2], g[2:3], g[3:4], g[4:5]
        slope2 = mask_row(i, (2,)) * match2 * gate2 * (1.0 - gate2)
        slope1 = mask_row(i, (0, 1)) * (match1 + slope2 * along1) * gate1 * (1.0 - gate1)
        later0 = slope1 + slope2
        slope0 = (match0 + later0 * along0) * gate0 * (1.0 - gate0)
        total = later0 + slope0
        rows = jnp.concatenate(
            [gate0, gate1, gate2, later0, slope2, total, later0 * gate0, gate1 * slope2], axis=0
        )
        columns = to_columns(rows)
        heads = heads + jnp.sum(columns[:, 6:7] * a[:ROWS, :].astype(F32), axis=0, keepdims=True)
        for j in range(2):
            w = sum(chosen(i, j, b) * columns[b * BLOCK : (b + 1) * BLOCK, 7:8] for b in range(NB))
            heads = heads + jnp.sum(w * slot(a, j), axis=0, keepdims=True)
        if n == 0:
            out[...] = rows
            hid = jnp.sum(columns[:, 5:6] * hidden[...].astype(F32), axis=0, keepdims=True)
    vector[:, :HEADS] = heads
    lhs = split3(heads)
    got = lax.dot_general(lhs, weight[...], (((1,), (1,)), ((), ())), preferred_element_type=F32)
    term = jnp.sum(got, axis=0, keepdims=True)
    row = lax.broadcasted_iota(jnp.int32, (128, 256), 0)
    col = lax.broadcasted_iota(jnp.int32, (128, 256), 1)
    spread = (col == (row >> 5) * 64 + (row & 31) + pos[3] * SPAN).astype(F32).astype(BF16)
    for k in range(WIDTH // 128):
        piece = jnp.dot(split3(term[:, k * 128 : (k + 1) * 128]), spread, preferred_element_type=F32)
        piece = jnp.sum(piece, axis=0, keepdims=True)
        at = (k % 8) * 256
        here = hid[:, at : at + 256]
        vector[:, HEADS + k * 256 : HEADS + (k + 1) * 256] = piece + jnp.where(pos[4] == k // 8, here, 0.0)


def split3(v):
    a = v.astype(BF16)
    rest = v - a.astype(F32)
    b = rest.astype(BF16)
    d = (rest - b.astype(F32)).astype(BF16)
    return jnp.concatenate([a, b, d, jnp.zeros((13, v.shape[1]), BF16)], axis=0)


def block_kernel(pos, own, ahead, far, behind, mine, received, left, right, here0, here1, later):
    z = pos[1]
    for k, part in enumerate((own, ahead, far, behind)):
        row = pl.multiple_of(((z + k) & 3) * SPAN, SPAN)
        left[pl.ds(row, SPAN), :] = part[:, :HALF]
        right[pl.ds(row, SPAN), :] = part[:, HALF:]
    for n, here in enumerate((here0, here1)):
        here[:, :ROWS] = mine[n * CHUNK : (n + 1) * CHUNK, :]
        here[:, ROWS:] = received[n * CHUNK : (n + 1) * CHUNK, :]
    for k in range(8):
        later[k] = pos[k]


def attn_kernel(pos, first, second, third, hidden, router, attn, base):
    base[...] = to_rows([jnp.sum(hidden[...].astype(F32) * router[...], axis=1, keepdims=True)])
    attn[:ROWS, :] = first[...]
    attn[ROWS : ROWS + 2 * BLOCK, :] = second[...]
    attn[ROWS + 2 * BLOCK :, :] = third[...]


def plane_kernel(pos, *refs):
    a, b, (left, right) = refs[:4], refs[4:8], refs[8:]
    x, y = pos[0], pos[2]
    for k in range(4):
        left[pl.ds(pl.multiple_of(((x + k) & 3) * 128, 128), 128), :] = a[k][...]
        for j in range(4):
            row = pl.multiple_of(j * 128 + ((y + k) & 3) * SPAN, SPAN)
            right[pl.ds(row, SPAN), :] = b[k][j * SPAN : (j + 1) * SPAN, :]


def final_kernel(own, ahead, far, behind, router, heads, out):
    total = own[...] + (ahead[...].astype(F32) + far[...].astype(F32) + behind[...].astype(F32))
    scale = float(ROWS * NF) ** (-0.5)
    out[...] = ((total + router[...] * heads[...]) * scale).astype(BF16)


def grads_kernel(kept2, kept3, rows, keep, sent, heads, heads_o, grad, router, gin, g1, g2, g3, proj):
    columns = to_columns(rows[...])
    gin[...] = (grad[...].astype(F32) + columns[:, 5:6] * router[...]).astype(BF16)
    proj[...] = keep[...] + sent[...]
    r = heads[...] + heads_o[...]
    g1[...] = (columns[:, 0:1] * (proj[...] + columns[:, 3:4] * r)).astype(BF16)

    def at_slot(kept, j):
        safe = jnp.maximum(kept[0, j], 0)
        live = (kept[0, j] >= 0).astype(F32)
        col = jnp.zeros((BLOCK, 128), F32)
        for b in range(NB):
            col = jnp.where(safe == b, columns[b * BLOCK : (b + 1) * BLOCK], col)
        return proj[pl.ds(pl.multiple_of(safe * BLOCK, BLOCK), BLOCK), :], col, live

    for j in range(2):
        p, col, live = at_slot(kept2, j)
        v = live * col[:, 1:2] * (p + col[:, 4:5] * r)
        g2[j * BLOCK : (j + 1) * BLOCK, :] = v.astype(BF16)
    p, col, live = at_slot(kept3, 0)
    g3[...] = (live * col[:, 2:3] * p).astype(BF16)


def local(
    hidden_in,
    attn_first,
    attn_second,
    attn_third,
    out_weight,
    router,
    kept_second,
    kept_third,
    grad_out,
):
    x, z, y, c, t = (lax.axis_index(a) for a in "xzyct")
    f = ((x * NZ + z) * NY + y) * NC + c
    pos = jnp.stack([x, z, y, c, t, t, t, t]).astype(jnp.int32)
    router_part = lax.dynamic_slice_in_dim(router, t * WIDTH, WIDTH, 0).reshape(1, WIDTH)

    router_half = lax.dynamic_index_in_dim(
        router.reshape(NX * NZ * NY, NC, SPAN), c, 1, keepdims=False
    ).reshape(1, WIDTH)
    own_router = lax.dynamic_slice_in_dim(router, f * SPAN, SPAN, 0).reshape(SPAN, 1)

    zs = [shifted(out_weight, "z", k) for k in (1, 2, 3)]
    mine, other, info = call(
        split_kernel, [((DEPTH, ROWS), BF16)] * 2 + [((8, 2 * ROWS), F32)], [],
        pos, kept_second, kept_third, grad_out,
    )
    received = shifted(other, "c", 1)
    info = lax.psum(info, "c")
    zs, received, info = tie(zs, received, info)
    left, right, *here, later = call(
        block_kernel, [((128, HALF), BF16)] * 2 + [((CHUNK, 2 * ROWS), BF16)] * 2 + [((8,), jnp.int32)], [],
        pos, out_weight, *zs, mine, received,
    )

    lefts = [shifted(left, "x", k) for k in (1, 2, 3)]
    rights = [shifted(right, "y", k) for k in (1, 2, 3)]
    there0 = swap_tp(here[0])
    attn, base = call(
        attn_kernel, [((2 * ROWS, HEADS), BF16), ((8, ROWS), F32)], [],
        later, attn_first, attn_second, attn_third, hidden_in, router_part,
    )
    lefts, rights, attn, there0, here = tie(lefts, rights, attn, there0, here)
    left, right = call(plane_kernel, [((CHUNK, HALF), BF16)] * 2, [], pos, left, *lefts, right, *rights)
    info_o = jnp.where(c == 0, info[:, ROWS:], info[:, :ROWS])
    info = jnp.where(c == 0, info[:, :ROWS], info[:, ROWS:])

    near = [shifted(v, a, s) for s in (1, -1) for v, a in ((left, "y"), (right, "x"))]
    there1 = swap_tp(here[1])
    near, left, right, attn, there1 = tie(near, left, right, attn, there1)
    far = [shifted(left, "y", 2), shifted(right, "x", 2)]
    attn_o = shifted(attn, "c", 1)
    weight = call(near_kernel, ((WIDTH, HEADS), BF16), [], pos, left, right, *near)
    far, weight, attn_o = tie(far, weight, attn_o)
    side = (info, info_o, attn, attn_o)
    grads = (*here, there0, there1)

    weight, heads, sums = call(
        along_kernel, [((WIDTH, HEADS), BF16), ((1, HEADS), F32), ((8, 2 * ROWS), F32)], [],
        pos, *side, base, router_half, *far, weight, alias={9: 0},
    )
    others, heads_o = quad(sums), shifted(heads, "c", 1)
    keep, send = call(proj_kernel, [((ROWS, HEADS), F32)] * 2, [], pos, *grads, weight)
    others, heads_o, keep, send = tie(others, heads_o, keep, send)
    gates, scaled = call(
        scaled_kernel, [((8, 2 * ROWS), F32), ((2 * ROWS, HEADS), BF16)], [], *side, sums, *others
    )
    sums = call(match_kernel, ((8, 2 * ROWS), F32), [], *side, keep, send)
    sums, scaled = tie(sums, scaled)
    others = quad(sums)

    kinds = [F32, BF16, BF16, BF16]
    *terms, later = call(
        term_kernel,
        [((CHUNK, HALF), k) for k in kinds * 2] + [((8,), jnp.int32)],
        [((CHUNK, 2 * ROWS), BF16)], pos, *grads, scaled,
    )
    sent = shifted(send, "c", 1)
    terms, others, sent, later = tie(terms, others, sent, later)
    got = [shifted(terms[4 * n + k], a, -k) for k in (1, 3) for n, a in enumerate("yx")]
    rows, vector = call(
        slope_kernel, [((8, ROWS), F32), ((1, HEADS + 2 * WIDTH), F32)], [],
        later, *side, gates, sums, *others, hidden_in, weight,
    )
    vector = fly_sum(vector.reshape(-1), "x")
    got, vector, terms = tie(got, vector, terms)
    far = [shifted(terms[4 * n + 2], a, 2) for n, a in enumerate("yx")]
    vector = ring_sum(ring_sum(vector, "y"), "z")
    far, vector = tie(far, vector)
    cuts = call(
        cut_kernel, [((CHUNK // 4, HALF), k) for k in kinds * 2], [((CHUNK, HALF), F32)],
        pos, terms[0], got[0], got[2], far[0], terms[4], got[1], got[3], far[1],
    )

    def sent_round(parts, axis):
        return [parts[0]] + [shifted(parts[k], axis, -k) for k in (1, 2, 3)]

    cuts = sent_round(cuts[:4], "x") + sent_round(cuts[4:], "y")
    cuts, rows, vector = tie(cuts, rows, vector)
    last = [((SPAN, HEADS), k) for k in kinds]
    cuts = call(cut_last_kernel, last, [((4 * SPAN, HEADS), F32)], pos, *cuts)
    cuts, vector, rows = tie(cuts, vector, rows)
    cuts = sent_round(cuts, "z")
    grads = call(
        grads_kernel,
        [((ROWS, WIDTH), BF16), ((ROWS, HEADS), BF16), ((2 * BLOCK, HEADS), BF16), ((BLOCK, HEADS), BF16)],
        [((ROWS, HEADS), F32)],
        kept_second, kept_third, rows, keep, sent, heads, heads_o, grad_out, router_part,
    )
    heads_total, vector = vector[:HEADS].reshape(1, HEADS), vector[HEADS:]
    vector = vector + swap_tp(vector)
    router_grad = (vector + shifted(vector, "c", 1)) * float(ROWS * NF) ** (-0.5)
    cuts, grads, router_grad = tie(cuts, grads, router_grad)
    weight_grad = call(final_kernel, ((SPAN, HEADS), BF16), [], *cuts, own_router, heads_total)
    return (*grads, weight_grad, router_grad)


def solution(mesh):
    fine = jax.sharding.Mesh(mesh.devices.reshape(NX, NZ, NY, NC, 2), ("x", "z", "y", "c", "t"))
    rows = ("x", "z", "y", "c")
    both, lists = P(rows, "t"), P(rows, None)
    return jax.shard_map(
        local,
        mesh=fine,
        in_specs=(both, both, both, both, both, P(), lists, lists, both),
        out_specs=(both, both, both, both, both, P()),
        check_vma=False,
    )
```

```python
import jax
import jax.numpy as jnp
from jax import lax
from jax.experimental import pallas as pl
from jax.experimental.pallas import tpu as pltpu
from jax.sharding import PartitionSpec as P

NB = 3
NX, NZ, NY, NC = 4, 4, 4, 2
NF = NX * NZ * NY * NC
F32, BF16 = jnp.float32, jnp.bfloat16
ROWS, WIDTH, HEADS = 384, 2048, 1024
BLOCK = ROWS // NB
DEPTH = WIDTH // 2
HALF = HEADS // 2
SPAN = 32
CHIP = 2 * SPAN
PART = 4 * CHIP
CHUNK = 4 * PART
SIZES = {"x": NX, "z": NZ, "y": NY, "c": NC, "t": 2}
VMEM = pl.BlockSpec(memory_space=pltpu.VMEM)
SMEM = pl.BlockSpec(memory_space=pltpu.SMEM)


def shifted(v, axis, step):
    n = SIZES[axis]
    return lax.ppermute(v, axis, [((i + step) % n, i) for i in range(n)])


def paired(v, axis, bit):
    return lax.ppermute(v, axis, [(i ^ bit, i) for i in range(SIZES[axis])])


def crossed(v, axes, step):
    pairs = []
    for i in range(NX * NY * NC):
        at = {"x": i // (NY * NC), "y": i // NC % NY, "c": i % NC}
        axis = axes[at["c"]]
        at[axis] = (at[axis] + step) % 4
        pairs.append(((at["x"] * NY + at["y"]) * NC + at["c"], i))
    return lax.ppermute(v, ("x", "y", "c"), pairs)


def swap_tp(v):
    return shifted(v, "t", 1)


def tie(*groups):
    return lax.optimization_barrier(groups)


def ring_sum(v, axis):
    a, b, c = (shifted(v, axis, k) for k in (1, 2, 3))
    return (v + a) + (b + c)


def fly_sum(v, axis):
    v = v + paired(v, axis, 1)
    return v + paired(v, axis, 2)


def quad(v):
    return swap_tp(v), shifted(v, "c", 1), lax.ppermute(v, ("c", "t"), [(3 - i, i) for i in range(4)])


def call(kernel, outs, scratch, *args, alias=None):
    def spec(dtype):
        return SMEM if dtype == jnp.int32 else VMEM

    single = not isinstance(outs, list)
    shapes = [jax.ShapeDtypeStruct(s, d) for s, d in ([outs] if single else outs)]
    got = pl.pallas_call(
        kernel,
        out_shape=shapes,
        in_specs=[spec(a.dtype) for a in args],
        out_specs=[spec(s.dtype) for s in shapes],
        scratch_shapes=[pltpu.VMEM(s, d) for s, d in scratch],
        input_output_aliases=alias or {},
        compiler_params=pltpu.CompilerParams(vmem_limit_bytes=16 * 2**20),
        cost_estimate=pl.CostEstimate(flops=1, bytes_accessed=1, transcendentals=0),
    )(*args)
    return got[0] if single else got


def halves_kernel(pos, weight, mine, other):
    c = pos[3]
    mine[...] = weight[:, pl.ds(pl.multiple_of(c * HALF, HALF), HALF)]
    other[...] = weight[:, pl.ds(pl.multiple_of((1 - c) * HALF, HALF), HALF)]


def chip_kernel(pos, mine, other, out):
    c = pos[3]
    out[pl.ds(pl.multiple_of(c * SPAN, SPAN), SPAN), :] = mine[...]
    out[pl.ds(pl.multiple_of((1 - c) * SPAN, SPAN), SPAN), :] = other[...]


def split_kernel(pos, kept2, kept3, grad, low, high, info):
    c = pos[3]
    row = lax.broadcasted_iota(jnp.int32, (256, 256), 0)
    col = lax.broadcasted_iota(jnp.int32, (256, 256), 1)
    same = (row == col).astype(F32).astype(BF16)
    for k in range(WIDTH // 256):
        piece = grad[:, k * 256 : (k + 1) * 256]
        got = lax.dot_general(same, piece, (((1,), (1,)), ((), ())), preferred_element_type=F32)
        out = low if k < 4 else high
        out[(k % 4) * 256 : (k % 4 + 1) * 256, :] = got.astype(BF16)
    rows = jnp.zeros((8, ROWS), F32)
    at = lax.broadcasted_iota(jnp.int32, (8, ROWS), 0)
    for k, value in enumerate((kept2[0, 0], kept2[0, 1], kept3[0, 0])):
        rows = jnp.where(at == k + 1, value.astype(F32), rows)
    info[:, :ROWS] = jnp.where(c == 0, rows, 0.0)
    info[:, ROWS:] = jnp.where(c == 0, 0.0, rows)


def to_rows(columns):
    lane = lax.broadcasted_iota(jnp.int32, (ROWS, 128), 1)
    wide = jnp.zeros((ROWS, 128), F32)
    for k, column in enumerate(columns):
        wide = jnp.where(lane == k, column, wide)
    return wide.T[:8]


def to_columns(rows):
    wide = jnp.concatenate([rows, jnp.zeros((128 - rows.shape[0], ROWS), F32)], axis=0)
    return wide.T


def chosen(info, j, b):
    return (info[j + 1 : j + 2, 0:1] == float(b)).astype(F32)


def mask_row(info, slots):
    b = (lax.broadcasted_iota(jnp.int32, (1, ROWS), 1) >> 7).astype(F32)
    mask = jnp.zeros((1, ROWS), F32)
    for j in slots:
        mask = jnp.where(info[j + 1 : j + 2, :] == b, 1.0, mask)
    return mask


def slot(attn, j):
    return attn[ROWS + j * BLOCK : ROWS + (j + 1) * BLOCK, :].astype(F32)


def put_pieces(pos, pieces, which, weight):
    x, y, c = pos[0], pos[2], pos[3]
    for piece, k in zip(pieces, which):

        @pl.when(c == 0)
        def _():
            for g in range(16):
                row = pl.multiple_of(g * PART + ((y + k) & 3) * CHIP, CHIP)
                weight[pl.ds(row, CHIP), :] = piece[g * CHIP : (g + 1) * CHIP, :]

        @pl.when(c == 1)
        def _():
            weight[pl.ds(pl.multiple_of(((x + k) & 3) * CHUNK, CHUNK), CHUNK), :] = piece[...]


def near_kernel(pos, own, ahead, behind, weight):
    put_pieces(pos, (own, ahead, behind), (0, 1, 3), weight)


def along_kernel(pos, info, info_o, attn, attn_o, base, router, far, weight_in, weight, heads, out):
    put_pieces(pos, (far,), (2,), weight)
    r = jnp.sum(jnp.dot(split3(router[...]), weight[...], preferred_element_type=F32), axis=0, keepdims=True)
    heads[...] = r
    for n, (i, a) in enumerate(((info, attn), (info_o, attn_o))):
        along0 = jnp.sum(a[:ROWS, :].astype(F32) * r, axis=1, keepdims=True)
        parts = [jnp.sum(slot(a, j) * r, axis=1, keepdims=True) for j in range(2)]
        along1 = jnp.concatenate(
            [chosen(i, 0, b) * parts[0] + chosen(i, 1, b) * parts[1] for b in range(NB)], axis=0
        )
        rows = to_rows([along0, along1])
        if n == 0:
            first = jnp.concatenate([jnp.zeros((2, ROWS), F32), base[0:1, :], jnp.zeros((5, ROWS), F32)], axis=0)
            rows = rows + first
        out[:, n * ROWS : (n + 1) * ROWS] = rows


def quad_sum(n, sums, by_t, by_c, by_ct):
    cols = slice(n * ROWS, (n + 1) * ROWS)
    swapped = slice((1 - n) * ROWS, (2 - n) * ROWS)
    return (sums[:, cols] + by_t[:, cols]) + (by_c[:, swapped] + by_ct[:, swapped])


def scaled_kernel(info, info_o, attn, attn_o, sums, by_t, by_c, by_ct, gates, scaled):
    for n, (i, a) in enumerate(((info, attn), (info_o, attn_o))):
        cols = slice(n * ROWS, (n + 1) * ROWS)
        both = quad_sum(n, sums, by_t, by_c, by_ct)
        along0, along1, base = both[0:1], both[1:2], both[2:3]
        gate0 = jax.nn.sigmoid(base)
        logit1 = base + gate0 * along0
        gate1 = jax.nn.sigmoid(logit1)
        gate2 = jax.nn.sigmoid(logit1 + mask_row(i, (0, 1)) * gate1 * along1)
        rows = jnp.concatenate([gate0, gate1, gate2, along0, along1, jnp.zeros((3, ROWS), F32)], axis=0)
        gates[:, cols] = rows
        columns = to_columns(rows)
        for b in range(NB):
            at = slice(b * BLOCK, (b + 1) * BLOCK)
            g = columns[at]
            total = (g[:, 0:1] * a[at, :].astype(F32)).astype(BF16).astype(F32)
            for j in range(3):
                w = g[:, 1:2] if j < 2 else g[:, 2:3]
                total = total + chosen(i, j, b) * (w * slot(a, j)).astype(BF16).astype(F32)
            scaled[n * ROWS + b * BLOCK : n * ROWS + (b + 1) * BLOCK, :] = total.astype(BF16)


def term_kernel(pos, *refs):
    mine, other, scaled, outs, later, lhs = refs[:4], refs[4:8], refs[8], refs[9:13], refs[13], refs[14]
    x, y, c, t = pos[0], pos[2], pos[3], pos[4]
    for k in range(8):
        later[k] = pos[k]
    for k in (1, 3, 2, 0):
        xx = (x + k) & 3
        for n in range(4):
            half = t if n < 2 else 1 - t

            @pl.when(c == 0)
            def _():
                for g in range(4):
                    row = pl.multiple_of(g * PART + ((y + k) & 3) * CHIP, CHIP)
                    at = slice(n * PART + g * CHIP, n * PART + (g + 1) * CHIP)
                    lhs[at, :ROWS] = mine[n][pl.ds(row, CHIP), :]
                    lhs[at, ROWS:] = other[n][pl.ds(row, CHIP), :]

            @pl.when((c == 1) & (xx == 2 * half + n % 2))
            def _():
                lhs[:, :ROWS] = mine[n][...]
                lhs[:, ROWS:] = other[n][...]

        for h in range(2):
            at = slice(h * 512, (h + 1) * 512)
            got = jnp.dot(lhs[at, :], scaled[...], preferred_element_type=F32)
            outs[k][at, :] = got.astype(outs[k].dtype)


def cut_kernel(pos, *refs):
    outs, tmp = refs[4:8], refs[8]
    x, y, c, t = pos[0], pos[2], pos[3], pos[4]
    total = refs[0][...]
    for part in refs[1:4]:
        total = total + part[...].astype(F32)
    tmp[...] = total
    for k in range(4):
        out = outs[k]

        @pl.when(c == 0)
        def _():
            xx = (x + k) & 3
            row = pl.multiple_of(((xx >> 1) ^ t) * 512 + (xx & 1) * PART, PART)
            out[...] = tmp[pl.ds(row, PART), :].astype(out.dtype)

        @pl.when(c == 1)
        def _():
            for j in range(4):
                row = pl.multiple_of(j * PART + ((y + k) & 3) * CHIP, CHIP)
                out[j * CHIP : (j + 1) * CHIP, :] = tmp[pl.ds(row, CHIP), :].astype(out.dtype)


def cut_last_kernel(pos, *refs):
    parts, outs, tmp = refs[:4], refs[4:8], refs[8]
    z = pos[1]
    total = parts[0][...]
    for part in parts[1:]:
        total = total + part[...].astype(F32)
    tmp[...] = total
    for k in range(4):
        row = pl.multiple_of(((z + k) & 3) * CHIP, CHIP)
        outs[k][...] = tmp[pl.ds(row, CHIP), :].astype(outs[k].dtype)


def proj_kernel(pos, *refs):
    mine, other, weight, keep, send = refs[:4], refs[4:8], refs[8], refs[9], refs[10]
    t = pos[4]
    for out, grads in ((send, other), (keep, mine)):
        total = 0.0
        for n in range(4):
            half = t if n < 2 else 1 - t
            rows = pl.ds(pl.multiple_of((2 * half + n % 2) * CHUNK, CHUNK), CHUNK)
            total = total + lax.dot_general(
                grads[n][...], weight[rows, :], (((0,), (0,)), ((), ())), preferred_element_type=F32
            )
        out[...] = total


def match_kernel(info, info_o, attn, attn_o, keep, send, out):
    for n, (i, a, p) in enumerate(((info, attn, keep), (info_o, attn_o, send))):
        columns = [jnp.sum(a[:ROWS, :].astype(F32) * p[...], axis=1, keepdims=True)]
        for slots in ((0, 1), (2,)):
            parts = []
            for b in range(NB):
                value = sum(chosen(i, j, b) * slot(a, j) for j in slots)
                parts.append(jnp.sum(value * p[b * BLOCK : (b + 1) * BLOCK, :], axis=1, keepdims=True))
            columns.append(jnp.concatenate(parts, axis=0))
        out[:, n * ROWS : (n + 1) * ROWS] = to_rows(columns)


def slope_kernel(pos, info, info_o, attn, attn_o, gates, sums, by_t, by_c, by_ct, hidden, weight, out, vector):
    heads = 0.0
    for n, (i, a) in enumerate(((info, attn), (info_o, attn_o))):
        cols = slice(n * ROWS, (n + 1) * ROWS)
        both = quad_sum(n, sums, by_t, by_c, by_ct)
        match0, match1, match2 = both[0:1], both[1:2], both[2:3]
        g = gates[:, cols]
        gate0, gate1, gate2, along0, along1 = g[0:1], g[1:2], g[2:3], g[3:4], g[4:5]
        slope2 = mask_row(i, (2,)) * match2 * gate2 * (1.0 - gate2)
        slope1 = mask_row(i, (0, 1)) * (match1 + slope2 * along1) * gate1 * (1.0 - gate1)
        later0 = slope1 + slope2
        slope0 = (match0 + later0 * along0) * gate0 * (1.0 - gate0)
        total = later0 + slope0
        rows = jnp.concatenate(
            [gate0, gate1, gate2, later0, slope2, total, later0 * gate0, gate1 * slope2], axis=0
        )
        columns = to_columns(rows)
        heads = heads + jnp.sum(columns[:, 6:7] * a[:ROWS, :].astype(F32), axis=0, keepdims=True)
        for j in range(2):
            w = sum(chosen(i, j, b) * columns[b * BLOCK : (b + 1) * BLOCK, 7:8] for b in range(NB))
            heads = heads + jnp.sum(w * slot(a, j), axis=0, keepdims=True)
        if n == 0:
            out[...] = rows
            hid = jnp.sum(columns[:, 5:6] * hidden[...].astype(F32), axis=0, keepdims=True)
    vector[:, :HALF] = heads
    got = lax.dot_general(split3(heads), weight[...], (((1,), (1,)), ((), ())), preferred_element_type=F32)
    term = jnp.sum(got, axis=0, keepdims=True)
    for n in range(2):
        part = term[:, n * WIDTH : (n + 1) * WIDTH] + jnp.where(pos[4] == n, hid, 0.0)
        vector[:, HALF + n * WIDTH : HALF + (n + 1) * WIDTH] = part


def split3(v):
    a = v.astype(BF16)
    rest = v - a.astype(F32)
    b = rest.astype(BF16)
    d = (rest - b.astype(F32)).astype(BF16)
    return jnp.concatenate([a, b, d, jnp.zeros((13, v.shape[1]), BF16)], axis=0)


def block_kernel(pos, own, ahead, far, behind, block, later):
    z = pos[1]
    for k, part in enumerate((own, ahead, far, behind)):
        block[pl.ds(pl.multiple_of(((z + k) & 3) * CHIP, CHIP), CHIP), :] = part[...]
    for k in range(8):
        later[k] = pos[k]


def attn_kernel(pos, first, second, third, hidden, router, attn, give, base):
    base[...] = to_rows([jnp.sum(hidden[...].astype(F32) * router[...], axis=1, keepdims=True)])
    c = pos[3]
    for out, half in ((attn, c), (give, 1 - c)):
        cols = pl.ds(pl.multiple_of(half * HALF, HALF), HALF)
        out[:ROWS, :] = first[:, cols]
        out[ROWS : ROWS + 2 * BLOCK, :] = second[:, cols]
        out[ROWS + 2 * BLOCK :, :] = third[:, cols]


def plane_kernel(pos, own, ahead, far, behind, out):
    x, y, c = pos[0], pos[2], pos[3]
    for k, part in enumerate((own, ahead, far, behind)):

        @pl.when(c == 0)
        def _():
            out[pl.ds(pl.multiple_of(((x + k) & 3) * PART, PART), PART), :] = part[...]

        @pl.when(c == 1)
        def _():
            for j in range(4):
                row = pl.multiple_of(j * PART + ((y + k) & 3) * CHIP, CHIP)
                out[pl.ds(row, CHIP), :] = part[j * CHIP : (j + 1) * CHIP, :]


def final_kernel(pos, own, ahead, far, behind, router, heads, mine, other):
    total = own[...] + (ahead[...].astype(F32) + far[...].astype(F32) + behind[...].astype(F32))
    scale = float(ROWS * NF) ** (-0.5)
    total = (total + router[...] * heads[...]) * scale
    low, high = total[:SPAN].astype(BF16), total[SPAN:].astype(BF16)
    mine[...] = jnp.where(pos[3] == 0, low, high)
    other[...] = jnp.where(pos[3] == 0, high, low)


def grads_kernel(pos, kept2, kept3, rows, keep, sent, heads, heads_o, grad, router, gin, g1, g2, g3, proj, line):
    columns = to_columns(rows[...])
    gin[...] = (grad[...].astype(F32) + columns[:, 5:6] * router[...]).astype(BF16)
    c = pos[3]
    for half, part, head in ((c, keep, heads), (1 - c, sent, heads_o)):
        at = pl.ds(pl.multiple_of(half * HALF, HALF), HALF)
        proj[:, at] = part[...]
        line[:, at] = head[...]
    r = line[...]
    g1[...] = (columns[:, 0:1] * (proj[...] + columns[:, 3:4] * r)).astype(BF16)

    def at_slot(kept, j):
        safe = jnp.maximum(kept[0, j], 0)
        live = (kept[0, j] >= 0).astype(F32)
        col = jnp.zeros((BLOCK, 128), F32)
        for b in range(NB):
            col = jnp.where(safe == b, columns[b * BLOCK : (b + 1) * BLOCK], col)
        return proj[pl.ds(pl.multiple_of(safe * BLOCK, BLOCK), BLOCK), :], col, live

    for j in range(2):
        p, col, live = at_slot(kept2, j)
        v = live * col[:, 1:2] * (p + col[:, 4:5] * r)
        g2[j * BLOCK : (j + 1) * BLOCK, :] = v.astype(BF16)
    p, col, live = at_slot(kept3, 0)
    g3[...] = (live * col[:, 2:3] * p).astype(BF16)


def local(
    hidden_in,
    attn_first,
    attn_second,
    attn_third,
    out_weight,
    router,
    kept_second,
    kept_third,
    grad_out,
):
    x, z, y, c, t = (lax.axis_index(a) for a in "xzyct")
    f = ((x * NZ + z) * NY + y) * NC + c
    pos = jnp.stack([x, z, y, c, t, t, t, t]).astype(jnp.int32)
    router_part = lax.dynamic_slice_in_dim(router, t * WIDTH, WIDTH, 0).reshape(1, WIDTH)

    router_chip = lax.dynamic_slice_in_dim(router, f // NC * CHIP, CHIP, 0).reshape(CHIP, 1)

    own_half, other_half = call(halves_kernel, [((SPAN, HALF), BF16)] * 2, [], pos, out_weight)
    own = call(chip_kernel, ((CHIP, HALF), BF16), [], pos, own_half, shifted(other_half, "c", 1))
    zs = [shifted(own, "z", k) for k in (1, 2, 3)]
    low, high, info = call(
        split_kernel, [((CHUNK, ROWS), BF16)] * 2 + [((8, 2 * ROWS), F32)], [],
        pos, kept_second, kept_third, grad_out,
    )
    low_t = swap_tp(low)
    info = lax.psum(info, "c")
    zs, info = tie(zs, info)
    block, later = call(block_kernel, [((PART, HALF), BF16), ((8,), jnp.int32)], [], pos, own, *zs)

    blocks = [crossed(block, "xy", k) for k in (1, 3, 2)]
    attn, give, base = call(
        attn_kernel, [((2 * ROWS, HALF), BF16)] * 2 + [((8, ROWS), F32)], [],
        later, attn_first, attn_second, attn_third, hidden_in, router_part,
    )
    low_o = shifted(low, "c", 1)
    blocks, attn, give, low_t, low_o, high = tie(blocks, attn, give, low_t, low_o, high)
    plane = call(plane_kernel, ((CHUNK, HALF), BF16), [], pos, block, blocks[0], blocks[2], blocks[1])
    info_o = jnp.where(c == 0, info[:, ROWS:], info[:, :ROWS])
    info = jnp.where(c == 0, info[:, :ROWS], info[:, ROWS:])

    planes = [crossed(plane, "yx", k) for k in (1, 3, 2)]
    high_t = swap_tp(high)
    low_to, high_o, attn_o = shifted(low_t, "c", 1), shifted(high, "c", 1), shifted(give, "c", 1)
    high_to = shifted(high_t, "c", 1)
    weight = call(near_kernel, ((2 * WIDTH, HALF), BF16), [], pos, plane, planes[0], planes[1])
    planes, weight, attn_o, high_t, low_to, high_o, high_to = tie(
        planes, weight, attn_o, high_t, low_to, high_o, high_to
    )
    side = (info, info_o, attn, attn_o)
    grads = (low, high, low_t, high_t, low_o, high_o, low_to, high_to)

    weight, heads, sums = call(
        along_kernel, [((2 * WIDTH, HALF), BF16), ((1, HALF), F32), ((8, 2 * ROWS), F32)], [],
        pos, *side, base, router.reshape(1, 2 * WIDTH), planes[2], weight, alias={8: 0},
    )
    others, heads_o = quad(sums), shifted(heads, "c", 1)
    keep, send = call(proj_kernel, [((ROWS, HALF), F32)] * 2, [], pos, *grads, weight)
    others, heads_o, keep, send = tie(others, heads_o, keep, send)
    gates, scaled = call(
        scaled_kernel, [((8, 2 * ROWS), F32), ((2 * ROWS, HALF), BF16)], [], *side, sums, *others
    )
    sums = call(match_kernel, ((8, 2 * ROWS), F32), [], *side, keep, send)
    sums, scaled = tie(sums, scaled)
    others = quad(sums)

    kinds = [F32, BF16, BF16, BF16]
    *terms, later = call(
        term_kernel, [((CHUNK, HALF), k) for k in kinds] + [((8,), jnp.int32)],
        [((CHUNK, 2 * ROWS), BF16)], pos, *grads, scaled,
    )
    sent = shifted(send, "c", 1)
    terms, others, sent, later = tie(terms, others, sent, later)
    got = [crossed(terms[k], "yx", -k) for k in (1, 3, 2)]
    rows, vector = call(
        slope_kernel, [((8, ROWS), F32), ((1, HALF + 2 * WIDTH), F32)], [],
        later, *side, gates, sums, *others, hidden_in, weight,
    )
    vector = fly_sum(fly_sum(vector.reshape(-1), "x"), "y")
    got, vector = tie(got, vector)
    cuts = call(
        cut_kernel, [((PART, HALF), k) for k in kinds], [((CHUNK, HALF), F32)], pos, terms[0], *got
    )
    got = [crossed(cuts[k], "xy", -k) for k in (1, 3, 2)]
    vector = fly_sum(vector, "z")
    got, vector, rows = tie(got, vector, rows)
    cuts = call(
        cut_last_kernel, [((CHIP, HALF), k) for k in kinds], [((PART, HALF), F32)], pos, cuts[0], *got
    )
    cuts, vector, rows = tie(cuts, vector, rows)
    got = [shifted(cuts[k], "z", -k) for k in (1, 2, 3)]
    grads = call(
        grads_kernel,
        [((ROWS, WIDTH), BF16), ((ROWS, HEADS), BF16), ((2 * BLOCK, HEADS), BF16), ((BLOCK, HEADS), BF16)],
        [((ROWS, HEADS), F32), ((1, HEADS), F32)],
        pos, kept_second, kept_third, rows, keep, sent, heads, heads_o, grad_out, router_part,
    )
    heads_total, vector = vector[:HALF].reshape(1, HALF), vector[HALF:]
    vector = vector + swap_tp(vector)
    got, grads, vector = tie(got, grads, vector)
    mine, other = call(
        final_kernel, [((SPAN, HALF), BF16)] * 2, [], pos, cuts[0], *got, router_chip, heads_total
    )
    other = shifted(other, "c", 1)
    weight_grad = jnp.where(
        c == 0, jnp.concatenate([mine, other], axis=1), jnp.concatenate([other, mine], axis=1)
    )
    router_grad = (vector + shifted(vector, "c", 1)) * float(ROWS * NF) ** (-0.5)
    return (*grads, weight_grad, router_grad)


def solution(mesh):
    fine = jax.sharding.Mesh(mesh.devices.reshape(NX, NZ, NY, NC, 2), ("x", "z", "y", "c", "t"))
    rows = ("x", "z", "y", "c")
    both, lists = P(rows, "t"), P(rows, None)
    return jax.shard_map(
        local,
        mesh=fine,
        in_specs=(both, both, both, both, both, P(), lists, lists, both),
        out_specs=(both, both, both, both, both, P()),
        check_vma=False,
    )
```

```python
import jax
import jax.numpy as jnp
from jax import lax
from jax.experimental import pallas as pl
from jax.experimental.pallas import tpu as pltpu
from jax.sharding import PartitionSpec as P

NB = 3
NX, NZ, NY, NC = 4, 4, 4, 2
NF = NX * NZ * NY * NC
F32, BF16 = jnp.float32, jnp.bfloat16
ROWS, WIDTH, HEADS = 384, 2048, 1024
BLOCK = ROWS // NB
DEPTH = WIDTH // 2
HALF = HEADS // 2
SPAN = 32
CHIP = 2 * SPAN
PART = 4 * CHIP
CHUNK = 4 * PART
SIZES = {"x": NX, "z": NZ, "y": NY, "c": NC, "t": 2}
VMEM = pl.BlockSpec(memory_space=pltpu.VMEM)
SMEM = pl.BlockSpec(memory_space=pltpu.SMEM)


def shifted(v, axis, step):
    n = SIZES[axis]
    return lax.ppermute(v, axis, [((i + step) % n, i) for i in range(n)])


def paired(v, axis, bit):
    return lax.ppermute(v, axis, [(i ^ bit, i) for i in range(SIZES[axis])])


def crossed(v, axes, step):
    pairs = []
    for i in range(NX * NY * NC):
        at = {"x": i // (NY * NC), "y": i // NC % NY, "c": i % NC}
        axis = axes[at["c"]]
        at[axis] = (at[axis] + step) % 4
        pairs.append(((at["x"] * NY + at["y"]) * NC + at["c"], i))
    return lax.ppermute(v, ("x", "y", "c"), pairs)


def swap_tp(v):
    return shifted(v, "t", 1)


def tie(*groups):
    return lax.optimization_barrier(groups)


def ring_sum(v, axis):
    a, b, c = (shifted(v, axis, k) for k in (1, 2, 3))
    return (v + a) + (b + c)


def fly_sum(v, axis):
    v = v + paired(v, axis, 1)
    return v + paired(v, axis, 2)


def quad(v):
    return swap_tp(v), shifted(v, "c", 1), lax.ppermute(v, ("c", "t"), [(3 - i, i) for i in range(4)])


def call(kernel, outs, scratch, *args, alias=None):
    def spec(dtype):
        return SMEM if dtype == jnp.int32 else VMEM

    single = not isinstance(outs, list)
    shapes = [jax.ShapeDtypeStruct(s, d) for s, d in ([outs] if single else outs)]
    got = pl.pallas_call(
        kernel,
        out_shape=shapes,
        in_specs=[spec(a.dtype) for a in args],
        out_specs=[spec(s.dtype) for s in shapes],
        scratch_shapes=[pltpu.VMEM(s, d) for s, d in scratch],
        input_output_aliases=alias or {},
        compiler_params=pltpu.CompilerParams(vmem_limit_bytes=12 * 2**20),
        cost_estimate=pl.CostEstimate(flops=1, bytes_accessed=1, transcendentals=0),
    )(*args)
    return got[0] if single else got


def halves_kernel(pos, kept2, kept3, weight, mine, other, info):
    c = pos[3]
    mine[...] = weight[:, pl.ds(pl.multiple_of(c * HALF, HALF), HALF)]
    other[...] = weight[:, pl.ds(pl.multiple_of((1 - c) * HALF, HALF), HALF)]
    rows = jnp.zeros((8, ROWS), F32)
    at = lax.broadcasted_iota(jnp.int32, (8, ROWS), 0)
    for k, value in enumerate((kept2[0, 0], kept2[0, 1], kept3[0, 0])):
        rows = jnp.where(at == k + 1, value.astype(F32), rows)
    info[:, :ROWS] = jnp.where(c == 0, rows, 0.0)
    info[:, ROWS:] = jnp.where(c == 0, 0.0, rows)


def chip_kernel(pos, mine, other, out):
    c = pos[3]
    out[pl.ds(pl.multiple_of(c * SPAN, SPAN), SPAN), :] = mine[...]
    out[pl.ds(pl.multiple_of((1 - c) * SPAN, SPAN), SPAN), :] = other[...]


def split_kernel(grad, low, high):
    row = lax.broadcasted_iota(jnp.int32, (256, 256), 0)
    col = lax.broadcasted_iota(jnp.int32, (256, 256), 1)
    same = (row == col).astype(F32).astype(BF16)
    for k in range(WIDTH // 256):
        piece = grad[:, k * 256 : (k + 1) * 256]
        got = lax.dot_general(same, piece, (((1,), (1,)), ((), ())), preferred_element_type=F32)
        out = low if k < 4 else high
        out[(k % 4) * 256 : (k % 4 + 1) * 256, :] = got.astype(BF16)


def to_rows(columns):
    lane = lax.broadcasted_iota(jnp.int32, (ROWS, 128), 1)
    wide = jnp.zeros((ROWS, 128), F32)
    for k, column in enumerate(columns):
        wide = jnp.where(lane == k, column, wide)
    return wide.T[:8]


def to_columns(rows):
    wide = jnp.concatenate([rows, jnp.zeros((128 - rows.shape[0], ROWS), F32)], axis=0)
    return wide.T


def chosen(info, j, b):
    return (info[j + 1 : j + 2, 0:1] == float(b)).astype(F32)


def mask_row(info, slots):
    b = (lax.broadcasted_iota(jnp.int32, (1, ROWS), 1) >> 7).astype(F32)
    mask = jnp.zeros((1, ROWS), F32)
    for j in slots:
        mask = jnp.where(info[j + 1 : j + 2, :] == b, 1.0, mask)
    return mask


def slot(attn, j):
    return attn[ROWS + j * BLOCK : ROWS + (j + 1) * BLOCK, :].astype(F32)


def put_pieces(pos, pieces, which, weight):
    x, y, c = pos[0], pos[2], pos[3]
    for piece, k in zip(pieces, which):

        @pl.when(c == 0)
        def _():
            for g in range(16):
                row = pl.multiple_of(g * PART + ((y + k) & 3) * CHIP, CHIP)
                weight[pl.ds(row, CHIP), :] = piece[g * CHIP : (g + 1) * CHIP, :]

        @pl.when(c == 1)
        def _():
            weight[pl.ds(pl.multiple_of(((x + k) & 3) * CHUNK, CHUNK), CHUNK), :] = piece[...]


def near_kernel(pos, own, ahead, behind, weight):
    put_pieces(pos, (own, ahead, behind), (0, 1, 3), weight)


def along_kernel(pos, info, info_o, attn, attn_o, base, router, far, weight_in, weight, heads, out):
    put_pieces(pos, (far,), (2,), weight)
    r = jnp.sum(jnp.dot(split3(router[...]), weight[...], preferred_element_type=F32), axis=0, keepdims=True)
    heads[...] = r
    for n, (i, a) in enumerate(((info, attn), (info_o, attn_o))):
        along0 = jnp.sum(a[:ROWS, :].astype(F32) * r, axis=1, keepdims=True)
        parts = [jnp.sum(slot(a, j) * r, axis=1, keepdims=True) for j in range(2)]
        along1 = jnp.concatenate(
            [chosen(i, 0, b) * parts[0] + chosen(i, 1, b) * parts[1] for b in range(NB)], axis=0
        )
        rows = to_rows([along0, along1])
        if n == 0:
            first = jnp.concatenate([jnp.zeros((2, ROWS), F32), base[0:1, :], jnp.zeros((5, ROWS), F32)], axis=0)
            rows = rows + first
        out[:, n * ROWS : (n + 1) * ROWS] = rows


def quad_sum(n, sums, by_t, by_c, by_ct):
    cols = slice(n * ROWS, (n + 1) * ROWS)
    swapped = slice((1 - n) * ROWS, (2 - n) * ROWS)
    return (sums[:, cols] + by_t[:, cols]) + (by_c[:, swapped] + by_ct[:, swapped])


def scaled_kernel(info, info_o, attn, attn_o, sums, by_t, by_c, by_ct, gates, scaled):
    for n, (i, a) in enumerate(((info, attn), (info_o, attn_o))):
        cols = slice(n * ROWS, (n + 1) * ROWS)
        both = quad_sum(n, sums, by_t, by_c, by_ct)
        along0, along1, base = both[0:1], both[1:2], both[2:3]
        gate0 = jax.nn.sigmoid(base)
        logit1 = base + gate0 * along0
        gate1 = jax.nn.sigmoid(logit1)
        gate2 = jax.nn.sigmoid(logit1 + mask_row(i, (0, 1)) * gate1 * along1)
        rows = jnp.concatenate([gate0, gate1, gate2, along0, along1, jnp.zeros((3, ROWS), F32)], axis=0)
        gates[:, cols] = rows
        columns = to_columns(rows)
        for b in range(NB):
            at = slice(b * BLOCK, (b + 1) * BLOCK)
            g = columns[at]
            total = (g[:, 0:1] * a[at, :].astype(F32)).astype(BF16).astype(F32)
            for j in range(3):
                w = g[:, 1:2] if j < 2 else g[:, 2:3]
                total = total + chosen(i, j, b) * (w * slot(a, j)).astype(BF16).astype(F32)
            scaled[n * ROWS + b * BLOCK : n * ROWS + (b + 1) * BLOCK, :] = total.astype(BF16)


def term_kernel(pos, *refs):
    mine, other, scaled, outs, later, lhs = refs[:4], refs[4:8], refs[8], refs[9:13], refs[13], refs[14]
    x, y, c, t = pos[0], pos[2], pos[3], pos[4]
    for k in range(8):
        later[k] = pos[k]
    for k in (1, 3, 2, 0):
        xx = (x + k) & 3
        for n in range(4):
            half = t if n < 2 else 1 - t

            @pl.when(c == 0)
            def _():
                for g in range(4):
                    row = pl.multiple_of(g * PART + ((y + k) & 3) * CHIP, CHIP)
                    at = slice(n * PART + g * CHIP, n * PART + (g + 1) * CHIP)
                    lhs[at, :ROWS] = mine[n][pl.ds(row, CHIP), :]
                    lhs[at, ROWS:] = other[n][pl.ds(row, CHIP), :]

            @pl.when((c == 1) & (xx == 2 * half + n % 2))
            def _():
                lhs[:, :ROWS] = mine[n][...]
                lhs[:, ROWS:] = other[n][...]

        for h in range(4):
            at = slice(h * 256, (h + 1) * 256)
            got = jnp.dot(lhs[at, :], scaled[...], preferred_element_type=F32)
            outs[k][at, :] = got.astype(outs[k].dtype)


def cut_kernel(pos, *refs):
    outs, tmp = refs[4:8], refs[8]
    x, y, c, t = pos[0], pos[2], pos[3], pos[4]
    total = refs[0][...]
    for part in refs[1:4]:
        total = total + part[...].astype(F32)
    tmp[...] = total
    for k in range(4):
        out = outs[k]

        @pl.when(c == 0)
        def _():
            xx = (x + k) & 3
            row = pl.multiple_of(((xx >> 1) ^ t) * 512 + (xx & 1) * PART, PART)
            out[...] = tmp[pl.ds(row, PART), :].astype(out.dtype)

        @pl.when(c == 1)
        def _():
            for j in range(4):
                row = pl.multiple_of(j * PART + ((y + k) & 3) * CHIP, CHIP)
                out[j * CHIP : (j + 1) * CHIP, :] = tmp[pl.ds(row, CHIP), :].astype(out.dtype)


def cut_last_kernel(pos, *refs):
    parts, outs, tmp = refs[:4], refs[4:8], refs[8]
    z = pos[1]
    total = parts[0][...]
    for part in parts[1:]:
        total = total + part[...].astype(F32)
    tmp[...] = total
    for k in range(4):
        row = pl.multiple_of(((z + k) & 3) * CHIP, CHIP)
        outs[k][...] = tmp[pl.ds(row, CHIP), :].astype(outs[k].dtype)


def proj_kernel(pos, *refs):
    mine, other, weight, keep, send = refs[:4], refs[4:8], refs[8], refs[9], refs[10]
    t = pos[4]
    for out, grads in ((send, other), (keep, mine)):
        for cols in (slice(0, 256), slice(256, 512)):
            total = 0.0
            for n in range(4):
                half = t if n < 2 else 1 - t
                rows = pl.ds(pl.multiple_of((2 * half + n % 2) * CHUNK, CHUNK), CHUNK)
                total = total + lax.dot_general(
                    grads[n][...], weight[rows, cols], (((0,), (0,)), ((), ())), preferred_element_type=F32
                )
            out[:, cols] = total


def match_kernel(info, info_o, attn, attn_o, keep, send, out):
    for n, (i, a, p) in enumerate(((info, attn, keep), (info_o, attn_o, send))):
        columns = [jnp.sum(a[:ROWS, :].astype(F32) * p[...], axis=1, keepdims=True)]
        for slots in ((0, 1), (2,)):
            parts = []
            for b in range(NB):
                value = sum(chosen(i, j, b) * slot(a, j) for j in slots)
                parts.append(jnp.sum(value * p[b * BLOCK : (b + 1) * BLOCK, :], axis=1, keepdims=True))
            columns.append(jnp.concatenate(parts, axis=0))
        out[:, n * ROWS : (n + 1) * ROWS] = to_rows(columns)


def slope_kernel(pos, info, info_o, attn, attn_o, gates, sums, by_t, by_c, by_ct, hidden, weight, out, vector):
    heads = 0.0
    for n, (i, a) in enumerate(((info, attn), (info_o, attn_o))):
        cols = slice(n * ROWS, (n + 1) * ROWS)
        both = quad_sum(n, sums, by_t, by_c, by_ct)
        match0, match1, match2 = both[0:1], both[1:2], both[2:3]
        g = gates[:, cols]
        gate0, gate1, gate2, along0, along1 = g[0:1], g[1:2], g[2:3], g[3:4], g[4:5]
        slope2 = mask_row(i, (2,)) * match2 * gate2 * (1.0 - gate2)
        slope1 = mask_row(i, (0, 1)) * (match1 + slope2 * along1) * gate1 * (1.0 - gate1)
        later0 = slope1 + slope2
        slope0 = (match0 + later0 * along0) * gate0 * (1.0 - gate0)
        total = later0 + slope0
        rows = jnp.concatenate(
            [gate0, gate1, gate2, later0, slope2, total, later0 * gate0, gate1 * slope2], axis=0
        )
        columns = to_columns(rows)
        heads = heads + jnp.sum(columns[:, 6:7] * a[:ROWS, :].astype(F32), axis=0, keepdims=True)
        for j in range(2):
            w = sum(chosen(i, j, b) * columns[b * BLOCK : (b + 1) * BLOCK, 7:8] for b in range(NB))
            heads = heads + jnp.sum(w * slot(a, j), axis=0, keepdims=True)
        if n == 0:
            out[...] = rows
            hid = jnp.sum(columns[:, 5:6] * hidden[...].astype(F32), axis=0, keepdims=True)
    vector[:, :HALF] = heads
    got = lax.dot_general(split3(heads), weight[...], (((1,), (1,)), ((), ())), preferred_element_type=F32)
    term = jnp.sum(got, axis=0, keepdims=True)
    for n in range(2):
        part = term[:, n * WIDTH : (n + 1) * WIDTH] + jnp.where(pos[4] == n, hid, 0.0)
        vector[:, HALF + n * WIDTH : HALF + (n + 1) * WIDTH] = part


def split3(v):
    a = v.astype(BF16)
    rest = v - a.astype(F32)
    b = rest.astype(BF16)
    d = (rest - b.astype(F32)).astype(BF16)
    return jnp.concatenate([a, b, d, jnp.zeros((13, v.shape[1]), BF16)], axis=0)


def block_kernel(pos, own, ahead, far, behind, block, later):
    z = pos[1]
    for k, part in enumerate((own, ahead, far, behind)):
        block[pl.ds(pl.multiple_of(((z + k) & 3) * CHIP, CHIP), CHIP), :] = part[...]
    for k in range(8):
        later[k] = pos[k]


def attn_kernel(pos, first, second, third, hidden, router, attn, give, base):
    base[...] = to_rows([jnp.sum(hidden[...].astype(F32) * router[...], axis=1, keepdims=True)])
    c = pos[3]
    for out, half in ((attn, c), (give, 1 - c)):
        cols = pl.ds(pl.multiple_of(half * HALF, HALF), HALF)
        out[:ROWS, :] = first[:, cols]
        out[ROWS : ROWS + 2 * BLOCK, :] = second[:, cols]
        out[ROWS + 2 * BLOCK :, :] = third[:, cols]


def plane_kernel(pos, own, ahead, far, behind, out):
    x, y, c = pos[0], pos[2], pos[3]
    for k, part in enumerate((own, ahead, far, behind)):

        @pl.when(c == 0)
        def _():
            out[pl.ds(pl.multiple_of(((x + k) & 3) * PART, PART), PART), :] = part[...]

        @pl.when(c == 1)
        def _():
            for j in range(4):
                row = pl.multiple_of(j * PART + ((y + k) & 3) * CHIP, CHIP)
                out[pl.ds(row, CHIP), :] = part[j * CHIP : (j + 1) * CHIP, :]


def final_kernel(pos, own, ahead, far, behind, router, heads, mine, other):
    total = own[...] + (ahead[...].astype(F32) + far[...].astype(F32) + behind[...].astype(F32))
    scale = float(ROWS * NF) ** (-0.5)
    total = (total + router[...] * heads[...]) * scale
    low, high = total[:SPAN].astype(BF16), total[SPAN:].astype(BF16)
    mine[...] = jnp.where(pos[3] == 0, low, high)
    other[...] = jnp.where(pos[3] == 0, high, low)


def grads_kernel(pos, kept2, kept3, rows, keep, sent, heads, heads_o, grad, router, gin, g1, g2, g3, proj, line):
    columns = to_columns(rows[...])
    gin[...] = (grad[...].astype(F32) + columns[:, 5:6] * router[...]).astype(BF16)
    c = pos[3]
    for half, part, head in ((c, keep, heads), (1 - c, sent, heads_o)):
        at = pl.ds(pl.multiple_of(half * HALF, HALF), HALF)
        proj[:, at] = part[...]
        line[:, at] = head[...]
    r = line[...]
    g1[...] = (columns[:, 0:1] * (proj[...] + columns[:, 3:4] * r)).astype(BF16)

    def at_slot(kept, j):
        safe = jnp.maximum(kept[0, j], 0)
        live = (kept[0, j] >= 0).astype(F32)
        col = jnp.zeros((BLOCK, 128), F32)
        for b in range(NB):
            col = jnp.where(safe == b, columns[b * BLOCK : (b + 1) * BLOCK], col)
        return proj[pl.ds(pl.multiple_of(safe * BLOCK, BLOCK), BLOCK), :], col, live

    for j in range(2):
        p, col, live = at_slot(kept2, j)
        v = live * col[:, 1:2] * (p + col[:, 4:5] * r)
        g2[j * BLOCK : (j + 1) * BLOCK, :] = v.astype(BF16)
    p, col, live = at_slot(kept3, 0)
    g3[...] = (live * col[:, 2:3] * p).astype(BF16)


def local(
    hidden_in,
    attn_first,
    attn_second,
    attn_third,
    out_weight,
    router,
    kept_second,
    kept_third,
    grad_out,
):
    x, z, y, c, t = (lax.axis_index(a) for a in "xzyct")
    f = ((x * NZ + z) * NY + y) * NC + c
    pos = jnp.stack([x, z, y, c, t, t, t, t]).astype(jnp.int32)
    router_part = lax.dynamic_slice_in_dim(router, t * WIDTH, WIDTH, 0).reshape(1, WIDTH)

    router_chip = lax.dynamic_slice_in_dim(router, f // NC * CHIP, CHIP, 0).reshape(CHIP, 1)

    own_half, other_half, info = call(
        halves_kernel, [((SPAN, HALF), BF16)] * 2 + [((8, 2 * ROWS), F32)], [],
        pos, kept_second, kept_third, out_weight,
    )
    own = call(chip_kernel, ((CHIP, HALF), BF16), [], pos, own_half, shifted(other_half, "c", 1))
    zs = [shifted(own, "z", k) for k in (1, 2, 3)]
    low, high = call(split_kernel, [((CHUNK, ROWS), BF16)] * 2, [], grad_out)
    info = lax.psum(info, "c")
    zs, info, low, high = tie(zs, info, low, high)
    low_t = swap_tp(low)
    block, later = call(block_kernel, [((PART, HALF), BF16), ((8,), jnp.int32)], [], pos, own, *zs)

    blocks = [crossed(block, "xy", k) for k in (1, 3, 2)]
    attn, give, base = call(
        attn_kernel, [((2 * ROWS, HALF), BF16)] * 2 + [((8, ROWS), F32)], [],
        later, attn_first, attn_second, attn_third, hidden_in, router_part,
    )
    low_o = shifted(low, "c", 1)
    blocks, attn, give, low_o, high = tie(blocks, attn, give, low_o, high)
    plane = call(plane_kernel, ((CHUNK, HALF), BF16), [], pos, block, blocks[0], blocks[2], blocks[1])
    info_o = jnp.where(c == 0, info[:, ROWS:], info[:, :ROWS])
    info = jnp.where(c == 0, info[:, :ROWS], info[:, ROWS:])

    planes = [crossed(plane, "yx", k) for k in (1, 3, 2)]
    low_t, high = tie(low_t, high)
    high_t = swap_tp(high)
    low_to, high_o, attn_o = shifted(low_t, "c", 1), shifted(high, "c", 1), shifted(give, "c", 1)
    high_to = shifted(high_t, "c", 1)
    weight = call(near_kernel, ((2 * WIDTH, HALF), BF16), [], pos, plane, planes[0], planes[1])
    planes, weight, attn_o, high_t, low_to, high_o, high_to = tie(
        planes, weight, attn_o, high_t, low_to, high_o, high_to
    )
    side = (info, info_o, attn, attn_o)
    grads = (low, high, low_t, high_t, low_o, high_o, low_to, high_to)

    weight, heads, sums = call(
        along_kernel, [((2 * WIDTH, HALF), BF16), ((1, HALF), F32), ((8, 2 * ROWS), F32)], [],
        pos, *side, base, router.reshape(1, 2 * WIDTH), planes[2], weight, alias={8: 0},
    )
    others, heads_o = quad(sums), shifted(heads, "c", 1)
    keep, send = call(proj_kernel, [((ROWS, HALF), F32)] * 2, [], pos, *grads, weight)
    others, heads_o, keep, send = tie(others, heads_o, keep, send)
    gates, scaled = call(
        scaled_kernel, [((8, 2 * ROWS), F32), ((2 * ROWS, HALF), BF16)], [], *side, sums, *others
    )
    sums = call(match_kernel, ((8, 2 * ROWS), F32), [], *side, keep, send)
    sums, scaled = tie(sums, scaled)
    others = quad(sums)

    kinds = [F32, BF16, BF16, BF16]
    *terms, later = call(
        term_kernel, [((CHUNK, HALF), k) for k in kinds] + [((8,), jnp.int32)],
        [((CHUNK, 2 * ROWS), BF16)], pos, *grads, scaled,
    )
    sent = shifted(send, "c", 1)
    terms, others, sent, later = tie(terms, others, sent, later)
    got = [crossed(terms[k], "yx", -k) for k in (1, 3, 2)]
    rows, vector = call(
        slope_kernel, [((8, ROWS), F32), ((1, HALF + 2 * WIDTH), F32)], [],
        later, *side, gates, sums, *others, hidden_in, weight,
    )
    vector = fly_sum(vector.reshape(-1), "x")
    got, vector = tie(got, vector)
    cuts = call(
        cut_kernel, [((PART, HALF), k) for k in kinds], [((CHUNK, HALF), F32)], pos, terms[0], *got
    )
    got = [crossed(cuts[k], "xy", -k) for k in (1, 3, 2)]
    vector = fly_sum(vector, "y")
    got, vector, rows = tie(got, vector, rows)
    cuts = call(
        cut_last_kernel, [((CHIP, HALF), k) for k in kinds], [((PART, HALF), F32)], pos, cuts[0], *got
    )
    cuts, vector, rows = tie(cuts, vector, rows)
    got = [shifted(cuts[k], "z", -k) for k in (1, 2, 3)]
    grads = call(
        grads_kernel,
        [((ROWS, WIDTH), BF16), ((ROWS, HEADS), BF16), ((2 * BLOCK, HEADS), BF16), ((BLOCK, HEADS), BF16)],
        [((ROWS, HEADS), F32), ((1, HEADS), F32)],
        pos, kept_second, kept_third, rows, keep, sent, heads, heads_o, grad_out, router_part,
    )
    vector = fly_sum(vector, "z")
    got, grads, vector = tie(got, grads, vector)
    heads_total, vector = vector[:HALF].reshape(1, HALF), vector[HALF:]
    mine, other = call(
        final_kernel, [((SPAN, HALF), BF16)] * 2, [], pos, cuts[0], *got, router_chip, heads_total
    )
    other = shifted(other, "c", 1)
    weight_grad = jnp.where(
        c == 0, jnp.concatenate([mine, other], axis=1), jnp.concatenate([other, mine], axis=1)
    )
    by_t, by_c, by_ct = quad(vector)
    router_grad = ((vector + by_t) + (by_c + by_ct)) * float(ROWS * NF) ** (-0.5)
    return (*grads, weight_grad, router_grad)


def solution(mesh):
    fine = jax.sharding.Mesh(mesh.devices.reshape(NX, NZ, NY, NC, 2), ("x", "z", "y", "c", "t"))
    rows = ("x", "z", "y", "c")
    both, lists = P(rows, "t"), P(rows, None)
    return jax.shard_map(
        local,
        mesh=fine,
        in_specs=(both, both, both, both, both, P(), lists, lists, both),
        out_specs=(both, both, both, both, both, P()),
        check_vma=False,
    )
```

```python
import jax
import jax.numpy as jnp
from jax import lax
from jax.experimental import pallas as pl
from jax.experimental.pallas import tpu as pltpu
from jax.sharding import PartitionSpec as P

NB = 3
NX, NZ, NY, NC = 4, 4, 4, 2
NF = NX * NZ * NY * NC
F32, BF16 = jnp.float32, jnp.bfloat16
ROWS, WIDTH, HEADS = 384, 2048, 1024
BLOCK = ROWS // NB
DEPTH = WIDTH // 2
HALF = HEADS // 2
SPAN = 32
CHIP = 2 * SPAN
PART = 4 * CHIP
CHUNK = 4 * PART
SIZES = {"x": NX, "z": NZ, "y": NY, "c": NC, "t": 2}
VMEM = pl.BlockSpec(memory_space=pltpu.VMEM)
SMEM = pl.BlockSpec(memory_space=pltpu.SMEM)


def shifted(v, axis, step):
    n = SIZES[axis]
    return lax.ppermute(v, axis, [((i + step) % n, i) for i in range(n)])


def paired(v, axis, bit):
    return lax.ppermute(v, axis, [(i ^ bit, i) for i in range(SIZES[axis])])


def crossed(v, axes, step):
    pairs = []
    for i in range(NX * NY * NC):
        at = {"x": i // (NY * NC), "y": i // NC % NY, "c": i % NC}
        axis = axes[at["c"]]
        at[axis] = (at[axis] + step) % 4
        pairs.append(((at["x"] * NY + at["y"]) * NC + at["c"], i))
    return lax.ppermute(v, ("x", "y", "c"), pairs)


def swap_tp(v):
    return shifted(v, "t", 1)


def tie(*groups):
    return lax.optimization_barrier(groups)


def fly_step(v, axis, bit):
    return v + paired(v, axis, bit)


def quad(v):
    return swap_tp(v), shifted(v, "c", 1), lax.ppermute(v, ("c", "t"), [(3 - i, i) for i in range(4)])


def call(kernel, outs, scratch, *args, alias=None):
    def spec(dtype):
        return SMEM if dtype == jnp.int32 else VMEM

    single = not isinstance(outs, list)
    shapes = [jax.ShapeDtypeStruct(s, d) for s, d in ([outs] if single else outs)]
    got = pl.pallas_call(
        kernel,
        out_shape=shapes,
        in_specs=[spec(a.dtype) for a in args],
        out_specs=[spec(s.dtype) for s in shapes],
        scratch_shapes=[pltpu.VMEM(s, d) for s, d in scratch],
        input_output_aliases=alias or {},
        compiler_params=pltpu.CompilerParams(vmem_limit_bytes=12 * 2**20),
        cost_estimate=pl.CostEstimate(flops=1, bytes_accessed=1, transcendentals=0),
    )(*args)
    return got[0] if single else got


def halves_kernel(pos, kept2, kept3, weight, mine, other, info):
    c = pos[3]
    mine[...] = weight[:, pl.ds(pl.multiple_of(c * HALF, HALF), HALF)]
    other[...] = weight[:, pl.ds(pl.multiple_of((1 - c) * HALF, HALF), HALF)]
    rows = jnp.zeros((8, ROWS), F32)
    at = lax.broadcasted_iota(jnp.int32, (8, ROWS), 0)
    for k, value in enumerate((kept2[0, 0], kept2[0, 1], kept3[0, 0])):
        rows = jnp.where(at == k + 1, value.astype(F32), rows)
    info[:, :ROWS] = jnp.where(c == 0, rows, 0.0)
    info[:, ROWS:] = jnp.where(c == 0, 0.0, rows)


def chip_kernel(pos, mine, other, out):
    c = pos[3]
    out[pl.ds(pl.multiple_of(c * SPAN, SPAN), SPAN), :] = mine[...]
    out[pl.ds(pl.multiple_of((1 - c) * SPAN, SPAN), SPAN), :] = other[...]


def split_kernel(grad, low, high):
    row = lax.broadcasted_iota(jnp.int32, (256, 256), 0)
    col = lax.broadcasted_iota(jnp.int32, (256, 256), 1)
    same = (row == col).astype(F32).astype(BF16)
    for k in range(WIDTH // 256):
        piece = grad[:, k * 256 : (k + 1) * 256]
        got = lax.dot_general(same, piece, (((1,), (1,)), ((), ())), preferred_element_type=F32)
        out = low if k < 4 else high
        out[(k % 4) * 256 : (k % 4 + 1) * 256, :] = got.astype(BF16)


def to_rows(columns):
    lane = lax.broadcasted_iota(jnp.int32, (ROWS, 128), 1)
    wide = jnp.zeros((ROWS, 128), F32)
    for k, column in enumerate(columns):
        wide = jnp.where(lane == k, column, wide)
    return wide.T[:8]


def to_columns(rows):
    wide = jnp.concatenate([rows, jnp.zeros((128 - rows.shape[0], ROWS), F32)], axis=0)
    return wide.T


def chosen(info, j, b):
    return (info[j + 1 : j + 2, 0:1] == float(b)).astype(F32)


def mask_row(info, slots):
    b = (lax.broadcasted_iota(jnp.int32, (1, ROWS), 1) >> 7).astype(F32)
    mask = jnp.zeros((1, ROWS), F32)
    for j in slots:
        mask = jnp.where(info[j + 1 : j + 2, :] == b, 1.0, mask)
    return mask


def slot(attn, j):
    return attn[ROWS + j * BLOCK : ROWS + (j + 1) * BLOCK, :].astype(F32)


def put_pieces(pos, pieces, which, weight):
    x, y, c = pos[0], pos[2], pos[3]
    for piece, k in zip(pieces, which):

        @pl.when(c == 0)
        def _():
            for g in range(16):
                row = pl.multiple_of(g * PART + ((y + k) & 3) * CHIP, CHIP)
                weight[pl.ds(row, CHIP), :] = piece[g * CHIP : (g + 1) * CHIP, :]

        @pl.when(c == 1)
        def _():
            weight[pl.ds(pl.multiple_of(((x + k) & 3) * CHUNK, CHUNK), CHUNK), :] = piece[...]


def near_kernel(pos, own, ahead, behind, weight):
    put_pieces(pos, (own, ahead, behind), (0, 1, 3), weight)


def along_kernel(pos, info, info_o, attn, attn_o, base, router, far, weight_in, weight, heads, out):
    put_pieces(pos, (far,), (2,), weight)
    r = jnp.sum(jnp.dot(split3(router[...]), weight[...], preferred_element_type=F32), axis=0, keepdims=True)
    heads[...] = r
    for n, (i, a) in enumerate(((info, attn), (info_o, attn_o))):
        along0 = jnp.sum(a[:ROWS, :].astype(F32) * r, axis=1, keepdims=True)
        parts = [jnp.sum(slot(a, j) * r, axis=1, keepdims=True) for j in range(2)]
        along1 = jnp.concatenate(
            [chosen(i, 0, b) * parts[0] + chosen(i, 1, b) * parts[1] for b in range(NB)], axis=0
        )
        rows = to_rows([along0, along1])
        if n == 0:
            first = jnp.concatenate([jnp.zeros((2, ROWS), F32), base[0:1, :], jnp.zeros((5, ROWS), F32)], axis=0)
            rows = rows + first
        out[:, n * ROWS : (n + 1) * ROWS] = rows


def quad_sum(n, sums, by_t, by_c, by_ct):
    cols = slice(n * ROWS, (n + 1) * ROWS)
    swapped = slice((1 - n) * ROWS, (2 - n) * ROWS)
    return (sums[:, cols] + by_t[:, cols]) + (by_c[:, swapped] + by_ct[:, swapped])


def scaled_kernel(info, info_o, attn, attn_o, sums, by_t, by_c, by_ct, gates, scaled):
    for n, (i, a) in enumerate(((info, attn), (info_o, attn_o))):
        cols = slice(n * ROWS, (n + 1) * ROWS)
        both = quad_sum(n, sums, by_t, by_c, by_ct)
        along0, along1, base = both[0:1], both[1:2], both[2:3]
        gate0 = jax.nn.sigmoid(base)
        logit1 = base + gate0 * along0
        gate1 = jax.nn.sigmoid(logit1)
        gate2 = jax.nn.sigmoid(logit1 + mask_row(i, (0, 1)) * gate1 * along1)
        rows = jnp.concatenate([gate0, gate1, gate2, along0, along1, jnp.zeros((3, ROWS), F32)], axis=0)
        gates[:, cols] = rows
        columns = to_columns(rows)
        for b in range(NB):
            at = slice(b * BLOCK, (b + 1) * BLOCK)
            g = columns[at]
            total = (g[:, 0:1] * a[at, :].astype(F32)).astype(BF16).astype(F32)
            for j in range(3):
                w = g[:, 1:2] if j < 2 else g[:, 2:3]
                total = total + chosen(i, j, b) * (w * slot(a, j)).astype(BF16).astype(F32)
            scaled[n * ROWS + b * BLOCK : n * ROWS + (b + 1) * BLOCK, :] = total.astype(BF16)


def term_kernel(pos, *refs):
    mine, other, scaled, outs, later, lhs = refs[:4], refs[4:8], refs[8], refs[9:-2], refs[-2], refs[-1]
    x, y, c, t = pos[0], pos[2], pos[3], pos[4]
    for k in range(8):
        later[k] = pos[k]
    for out, k in zip(outs, (1, 3, 2) if len(outs) == 3 else (0,)):
        xx = (x + k) & 3
        for n in range(4):
            half = t if n < 2 else 1 - t

            @pl.when(c == 0)
            def _():
                for g in range(4):
                    row = pl.multiple_of(g * PART + ((y + k) & 3) * CHIP, CHIP)
                    at = slice(n * PART + g * CHIP, n * PART + (g + 1) * CHIP)
                    lhs[at, :ROWS] = mine[n][pl.ds(row, CHIP), :]
                    lhs[at, ROWS:] = other[n][pl.ds(row, CHIP), :]

            @pl.when((c == 1) & (xx == 2 * half + n % 2))
            def _():
                lhs[:, :ROWS] = mine[n][...]
                lhs[:, ROWS:] = other[n][...]

        for h in range(4):
            at = slice(h * 256, (h + 1) * 256)
            got = jnp.dot(lhs[at, :], scaled[...], preferred_element_type=F32)
            out[at, :] = got.astype(out.dtype)


def cut_kernel(pos, *refs):
    outs, tmp = refs[4:8], refs[8]
    x, y, c, t = pos[0], pos[2], pos[3], pos[4]
    total = refs[0][...]
    for part in refs[1:4]:
        total = total + part[...].astype(F32)
    tmp[...] = total
    for k in range(4):
        out = outs[k]

        @pl.when(c == 0)
        def _():
            xx = (x + k) & 3
            row = pl.multiple_of(((xx >> 1) ^ t) * 512 + (xx & 1) * PART, PART)
            out[...] = tmp[pl.ds(row, PART), :].astype(out.dtype)

        @pl.when(c == 1)
        def _():
            for j in range(4):
                row = pl.multiple_of(j * PART + ((y + k) & 3) * CHIP, CHIP)
                out[j * CHIP : (j + 1) * CHIP, :] = tmp[pl.ds(row, CHIP), :].astype(out.dtype)


def cut_last_kernel(pos, *refs):
    parts, outs, tmp = refs[:4], refs[4:8], refs[8]
    z = pos[1]
    total = parts[0][...]
    for part in parts[1:]:
        total = total + part[...].astype(F32)
    tmp[...] = total
    for k in range(4):
        row = pl.multiple_of(((z + k) & 3) * CHIP, CHIP)
        outs[k][...] = tmp[pl.ds(row, CHIP), :].astype(outs[k].dtype)


def proj_kernel(pos, *refs):
    mine, other, weight, keep, send = refs[:4], refs[4:8], refs[8], refs[9], refs[10]
    t = pos[4]
    for out, grads in ((send, other), (keep, mine)):
        for cols in (slice(0, 256), slice(256, 512)):
            total = 0.0
            for n in range(4):
                half = t if n < 2 else 1 - t
                rows = pl.ds(pl.multiple_of((2 * half + n % 2) * CHUNK, CHUNK), CHUNK)
                total = total + lax.dot_general(
                    grads[n][...], weight[rows, cols], (((0,), (0,)), ((), ())), preferred_element_type=F32
                )
            out[:, cols] = total


def match_kernel(info, info_o, attn, attn_o, keep, send, out):
    for n, (i, a, p) in enumerate(((info, attn, keep), (info_o, attn_o, send))):
        columns = [jnp.sum(a[:ROWS, :].astype(F32) * p[...], axis=1, keepdims=True)]
        for slots in ((0, 1), (2,)):
            parts = []
            for b in range(NB):
                value = sum(chosen(i, j, b) * slot(a, j) for j in slots)
                parts.append(jnp.sum(value * p[b * BLOCK : (b + 1) * BLOCK, :], axis=1, keepdims=True))
            columns.append(jnp.concatenate(parts, axis=0))
        out[:, n * ROWS : (n + 1) * ROWS] = to_rows(columns)


def slope_kernel(pos, info, info_o, attn, attn_o, gates, sums, by_t, by_c, by_ct, hidden, weight, out, vector):
    heads = 0.0
    for n, (i, a) in enumerate(((info, attn), (info_o, attn_o))):
        cols = slice(n * ROWS, (n + 1) * ROWS)
        both = quad_sum(n, sums, by_t, by_c, by_ct)
        match0, match1, match2 = both[0:1], both[1:2], both[2:3]
        g = gates[:, cols]
        gate0, gate1, gate2, along0, along1 = g[0:1], g[1:2], g[2:3], g[3:4], g[4:5]
        slope2 = mask_row(i, (2,)) * match2 * gate2 * (1.0 - gate2)
        slope1 = mask_row(i, (0, 1)) * (match1 + slope2 * along1) * gate1 * (1.0 - gate1)
        later0 = slope1 + slope2
        slope0 = (match0 + later0 * along0) * gate0 * (1.0 - gate0)
        total = later0 + slope0
        rows = jnp.concatenate(
            [gate0, gate1, gate2, later0, slope2, total, later0 * gate0, gate1 * slope2], axis=0
        )
        columns = to_columns(rows)
        heads = heads + jnp.sum(columns[:, 6:7] * a[:ROWS, :].astype(F32), axis=0, keepdims=True)
        for j in range(2):
            w = sum(chosen(i, j, b) * columns[b * BLOCK : (b + 1) * BLOCK, 7:8] for b in range(NB))
            heads = heads + jnp.sum(w * slot(a, j), axis=0, keepdims=True)
        if n == 0:
            out[...] = rows
            hid = jnp.sum(columns[:, 5:6] * hidden[...].astype(F32), axis=0, keepdims=True)
    vector[:, :HALF] = heads
    got = lax.dot_general(split3(heads), weight[...], (((1,), (1,)), ((), ())), preferred_element_type=F32)
    term = jnp.sum(got, axis=0, keepdims=True)
    for n in range(2):
        part = term[:, n * WIDTH : (n + 1) * WIDTH] + jnp.where(pos[4] == n, hid, 0.0)
        vector[:, HALF + n * WIDTH : HALF + (n + 1) * WIDTH] = part


def split3(v):
    a = v.astype(BF16)
    rest = v - a.astype(F32)
    b = rest.astype(BF16)
    d = (rest - b.astype(F32)).astype(BF16)
    return jnp.concatenate([a, b, d, jnp.zeros((13, v.shape[1]), BF16)], axis=0)


def block_kernel(pos, own, ahead, far, behind, block, later):
    z = pos[1]
    for k, part in enumerate((own, ahead, far, behind)):
        block[pl.ds(pl.multiple_of(((z + k) & 3) * CHIP, CHIP), CHIP), :] = part[...]
    for k in range(8):
        later[k] = pos[k]


def attn_kernel(pos, first, second, third, hidden, router, attn, give, base):
    base[...] = to_rows([jnp.sum(hidden[...].astype(F32) * router[...], axis=1, keepdims=True)])
    c = pos[3]
    for out, half in ((attn, c), (give, 1 - c)):
        cols = pl.ds(pl.multiple_of(half * HALF, HALF), HALF)
        out[:ROWS, :] = first[:, cols]
        out[ROWS : ROWS + 2 * BLOCK, :] = second[:, cols]
        out[ROWS + 2 * BLOCK :, :] = third[:, cols]


def plane_kernel(pos, own, ahead, far, behind, out):
    x, y, c = pos[0], pos[2], pos[3]
    for k, part in enumerate((own, ahead, far, behind)):

        @pl.when(c == 0)
        def _():
            out[pl.ds(pl.multiple_of(((x + k) & 3) * PART, PART), PART), :] = part[...]

        @pl.when(c == 1)
        def _():
            for j in range(4):
                row = pl.multiple_of(j * PART + ((y + k) & 3) * CHIP, CHIP)
                out[pl.ds(row, CHIP), :] = part[j * CHIP : (j + 1) * CHIP, :]


def final_kernel(pos, own, ahead, far, behind, router, heads, mine, other):
    total = own[...] + (ahead[...].astype(F32) + far[...].astype(F32) + behind[...].astype(F32))
    scale = float(ROWS * NF) ** (-0.5)
    total = (total + router[...] * heads[...]) * scale
    low, high = total[:SPAN].astype(BF16), total[SPAN:].astype(BF16)
    mine[...] = jnp.where(pos[3] == 0, low, high)
    other[...] = jnp.where(pos[3] == 0, high, low)


def grads_kernel(pos, kept2, kept3, rows, keep, sent, heads, heads_o, grad, router, gin, g1, g2, g3, proj, line):
    columns = to_columns(rows[...])
    gin[...] = (grad[...].astype(F32) + columns[:, 5:6] * router[...]).astype(BF16)
    c = pos[3]
    for half, part, head in ((c, keep, heads), (1 - c, sent, heads_o)):
        at = pl.ds(pl.multiple_of(half * HALF, HALF), HALF)
        proj[:, at] = part[...]
        line[:, at] = head[...]
    r = line[...]
    g1[...] = (columns[:, 0:1] * (proj[...] + columns[:, 3:4] * r)).astype(BF16)

    def at_slot(kept, j):
        safe = jnp.maximum(kept[0, j], 0)
        live = (kept[0, j] >= 0).astype(F32)
        col = jnp.zeros((BLOCK, 128), F32)
        for b in range(NB):
            col = jnp.where(safe == b, columns[b * BLOCK : (b + 1) * BLOCK], col)
        return proj[pl.ds(pl.multiple_of(safe * BLOCK, BLOCK), BLOCK), :], col, live

    for j in range(2):
        p, col, live = at_slot(kept2, j)
        v = live * col[:, 1:2] * (p + col[:, 4:5] * r)
        g2[j * BLOCK : (j + 1) * BLOCK, :] = v.astype(BF16)
    p, col, live = at_slot(kept3, 0)
    g3[...] = (live * col[:, 2:3] * p).astype(BF16)


def local(
    hidden_in,
    attn_first,
    attn_second,
    attn_third,
    out_weight,
    router,
    kept_second,
    kept_third,
    grad_out,
):
    x, z, y, c, t = (lax.axis_index(a) for a in "xzyct")
    f = ((x * NZ + z) * NY + y) * NC + c
    pos = jnp.stack([x, z, y, c, t, t, t, t]).astype(jnp.int32)
    router_part = lax.dynamic_slice_in_dim(router, t * WIDTH, WIDTH, 0).reshape(1, WIDTH)

    router_chip = lax.dynamic_slice_in_dim(router, f // NC * CHIP, CHIP, 0).reshape(CHIP, 1)

    own_half, other_half, info = call(
        halves_kernel, [((SPAN, HALF), BF16)] * 2 + [((8, 2 * ROWS), F32)], [],
        pos, kept_second, kept_third, out_weight,
    )
    own = call(chip_kernel, ((CHIP, HALF), BF16), [], pos, own_half, shifted(other_half, "c", 1))
    zs = [shifted(own, "z", k) for k in (1, 2, 3)]
    low, high = call(split_kernel, [((CHUNK, ROWS), BF16)] * 2, [], grad_out)
    zs, low, high = tie(zs, low, high)
    low_t = swap_tp(low)
    block, later = call(block_kernel, [((PART, HALF), BF16), ((8,), jnp.int32)], [], pos, own, *zs)

    blocks = [crossed(block, "xy", k) for k in (1, 3, 2)]
    attn, give, base = call(
        attn_kernel, [((2 * ROWS, HALF), BF16)] * 2 + [((8, ROWS), F32)], [],
        later, attn_first, attn_second, attn_third, hidden_in, router_part,
    )
    low_o = shifted(low, "c", 1)
    blocks, attn, give, low_o, high, info = tie(blocks, attn, give, low_o, high, info)
    plane = call(plane_kernel, ((CHUNK, HALF), BF16), [], pos, block, blocks[0], blocks[2], blocks[1])
    info = lax.psum(info, "c")
    info_o = jnp.where(c == 0, info[:, ROWS:], info[:, :ROWS])
    info = jnp.where(c == 0, info[:, :ROWS], info[:, ROWS:])

    planes = [crossed(plane, "yx", k) for k in (1, 3, 2)]
    low_t, high = tie(low_t, high)
    high_t = swap_tp(high)
    low_to, high_o, attn_o = shifted(low_t, "c", 1), shifted(high, "c", 1), shifted(give, "c", 1)
    weight = call(near_kernel, ((2 * WIDTH, HALF), BF16), [], pos, plane, planes[0], planes[1])
    weight, high_t = tie(weight, high_t)
    high_to = shifted(high_t, "c", 1)
    planes, weight, attn_o, high_t, low_to, high_o, high_to = tie(
        planes, weight, attn_o, high_t, low_to, high_o, high_to
    )
    side = (info, info_o, attn, attn_o)
    grads = (low, high, low_t, high_t, low_o, high_o, low_to, high_to)

    weight, heads, sums = call(
        along_kernel, [((2 * WIDTH, HALF), BF16), ((1, HALF), F32), ((8, 2 * ROWS), F32)], [],
        pos, *side, base, router.reshape(1, 2 * WIDTH), planes[2], weight, alias={8: 0},
    )
    others, heads_o = quad(sums), shifted(heads, "c", 1)
    keep, send = call(proj_kernel, [((ROWS, HALF), F32)] * 2, [], pos, *grads, weight)
    others, heads_o, keep, send = tie(others, heads_o, keep, send)
    gates, scaled = call(
        scaled_kernel, [((8, 2 * ROWS), F32), ((2 * ROWS, HALF), BF16)], [], *side, sums, *others
    )
    sums = call(match_kernel, ((8, 2 * ROWS), F32), [], *side, keep, send)
    sums, scaled = tie(sums, scaled)
    others = quad(sums)

    kinds = [F32, BF16, BF16, BF16]
    *terms, later = call(
        term_kernel, [((CHUNK, HALF), BF16)] * 3 + [((8,), jnp.int32)],
        [((CHUNK, 2 * ROWS), BF16)], pos, *grads, scaled,
    )
    sent = shifted(send, "c", 1)
    terms, others, sent, later = tie(terms, others, sent, later)
    got = [crossed(terms[n], "yx", -k) for n, k in enumerate((1, 3, 2))]
    rows, vector = call(
        slope_kernel, [((8, ROWS), F32), ((1, HALF + 2 * WIDTH), F32)], [],
        later, *side, gates, sums, *others, hidden_in, weight,
    )
    term, _ = call(
        term_kernel, [((CHUNK, HALF), F32), ((8,), jnp.int32)],
        [((CHUNK, 2 * ROWS), BF16)], later, *grads, scaled,
    )
    vector = fly_step(fly_step(fly_step(vector.reshape(-1), "x", 1), "x", 2), "y", 1)
    got, vector, term = tie(got, vector, term)
    cuts = call(
        cut_kernel, [((PART, HALF), k) for k in kinds], [((CHUNK, HALF), F32)], pos, term, *got
    )
    got = [crossed(cuts[k], "xy", -k) for k in (1, 3, 2)]
    vector = fly_step(fly_step(vector, "y", 2), "z", 1)
    got, vector, rows = tie(got, vector, rows)
    cuts = call(
        cut_last_kernel, [((CHIP, HALF), k) for k in kinds], [((PART, HALF), F32)], pos, cuts[0], *got
    )
    cuts, vector, rows = tie(cuts, vector, rows)
    got = [shifted(cuts[k], "z", -k) for k in (1, 2, 3)]
    grads = call(
        grads_kernel,
        [((ROWS, WIDTH), BF16), ((ROWS, HEADS), BF16), ((2 * BLOCK, HEADS), BF16), ((BLOCK, HEADS), BF16)],
        [((ROWS, HEADS), F32), ((1, HEADS), F32)],
        pos, kept_second, kept_third, rows, keep, sent, heads, heads_o, grad_out, router_part,
    )
    vector = fly_step(vector, "z", 2)
    got, grads, vector = tie(got, grads, vector)
    heads_total, vector = vector[:HALF].reshape(1, HALF), vector[HALF:]
    mine, other = call(
        final_kernel, [((SPAN, HALF), BF16)] * 2, [], pos, cuts[0], *got, router_chip, heads_total
    )
    other = shifted(other, "c", 1)
    weight_grad = jnp.where(
        c == 0, jnp.concatenate([mine, other], axis=1), jnp.concatenate([other, mine], axis=1)
    )
    by_t, by_c, by_ct = quad(vector)
    router_grad = ((vector + by_t) + (by_c + by_ct)) * float(ROWS * NF) ** (-0.5)
    return (*grads, weight_grad, router_grad)


def solution(mesh):
    fine = jax.sharding.Mesh(mesh.devices.reshape(NX, NZ, NY, NC, 2), ("x", "z", "y", "c", "t"))
    rows = ("x", "z", "y", "c")
    both, lists = P(rows, "t"), P(rows, None)
    return jax.shard_map(
        local,
        mesh=fine,
        in_specs=(both, both, both, both, both, P(), lists, lists, both),
        out_specs=(both, both, both, both, both, P()),
        check_vma=False,
    )
```

```python
import jax
import jax.numpy as jnp
from jax import lax
from jax.experimental import pallas as pl
from jax.experimental.pallas import tpu as pltpu
from jax.sharding import PartitionSpec as P

NB = 3
NX, NZ, NY, NC = 4, 4, 4, 2
NF = NX * NZ * NY * NC
F32, BF16 = jnp.float32, jnp.bfloat16
ROWS, WIDTH, HEADS = 384, 2048, 1024
BLOCK = ROWS // NB
DEPTH = WIDTH // 2
HALF = HEADS // 2
SPAN = 32
CHIP = 2 * SPAN
PART = 4 * CHIP
CHUNK = 4 * PART
SIZES = {"x": NX, "z": NZ, "y": NY, "c": NC, "t": 2}
VMEM = pl.BlockSpec(memory_space=pltpu.VMEM)
SMEM = pl.BlockSpec(memory_space=pltpu.SMEM)


def shifted(v, axis, step):
    n = SIZES[axis]
    return lax.ppermute(v, axis, [((i + step) % n, i) for i in range(n)])


def paired(v, axis, bit):
    return lax.ppermute(v, axis, [(i ^ bit, i) for i in range(SIZES[axis])])


def crossed(v, axes, step):
    pairs = []
    for i in range(NX * NY * NC):
        at = {"x": i // (NY * NC), "y": i // NC % NY, "c": i % NC}
        axis = axes[at["c"]]
        at[axis] = (at[axis] + step) % 4
        pairs.append(((at["x"] * NY + at["y"]) * NC + at["c"], i))
    return lax.ppermute(v, ("x", "y", "c"), pairs)


def swap_tp(v):
    return shifted(v, "t", 1)


def tie(*groups):
    return lax.optimization_barrier(groups)


def fly_step(v, axis, bit):
    return v + paired(v, axis, bit)


def quad(v):
    return swap_tp(v), shifted(v, "c", 1), lax.ppermute(v, ("c", "t"), [(3 - i, i) for i in range(4)])


def call(kernel, outs, scratch, *args, alias=None):
    def spec(dtype):
        return SMEM if dtype == jnp.int32 else VMEM

    single = not isinstance(outs, list)
    shapes = [jax.ShapeDtypeStruct(s, d) for s, d in ([outs] if single else outs)]
    got = pl.pallas_call(
        kernel,
        out_shape=shapes,
        in_specs=[spec(a.dtype) for a in args],
        out_specs=[spec(s.dtype) for s in shapes],
        scratch_shapes=[pltpu.VMEM(s, d) for s, d in scratch],
        input_output_aliases=alias or {},
        compiler_params=pltpu.CompilerParams(vmem_limit_bytes=12 * 2**20),
        cost_estimate=pl.CostEstimate(flops=1, bytes_accessed=1, transcendentals=0),
    )(*args)
    return got[0] if single else got


def halves_kernel(pos, kept2, kept3, weight, mine, other, info):
    c = pos[3]
    mine[...] = weight[:, pl.ds(pl.multiple_of(c * HALF, HALF), HALF)]
    other[...] = weight[:, pl.ds(pl.multiple_of((1 - c) * HALF, HALF), HALF)]
    rows = jnp.zeros((8, ROWS), F32)
    at = lax.broadcasted_iota(jnp.int32, (8, ROWS), 0)
    for k, value in enumerate((kept2[0, 0], kept2[0, 1], kept3[0, 0])):
        rows = jnp.where(at == k + 1, value.astype(F32), rows)
    info[:, :ROWS] = jnp.where(c == 0, rows, 0.0)
    info[:, ROWS:] = jnp.where(c == 0, 0.0, rows)


def chip_kernel(pos, mine, other, out):
    c = pos[3]
    out[pl.ds(pl.multiple_of(c * SPAN, SPAN), SPAN), :] = mine[...]
    out[pl.ds(pl.multiple_of((1 - c) * SPAN, SPAN), SPAN), :] = other[...]


def split_kernel(grad, low, high):
    row = lax.broadcasted_iota(jnp.int32, (256, 256), 0)
    col = lax.broadcasted_iota(jnp.int32, (256, 256), 1)
    same = (row == col).astype(F32).astype(BF16)
    for k in range(WIDTH // 256):
        piece = grad[:, k * 256 : (k + 1) * 256]
        got = lax.dot_general(same, piece, (((1,), (1,)), ((), ())), preferred_element_type=F32)
        out = low if k < 4 else high
        out[(k % 4) * 256 : (k % 4 + 1) * 256, :] = got.astype(BF16)


def to_rows(columns):
    lane = lax.broadcasted_iota(jnp.int32, (ROWS, 128), 1)
    wide = jnp.zeros((ROWS, 128), F32)
    for k, column in enumerate(columns):
        wide = jnp.where(lane == k, column, wide)
    return wide.T[:8]


def to_columns(rows):
    wide = jnp.concatenate([rows, jnp.zeros((128 - rows.shape[0], ROWS), F32)], axis=0)
    return wide.T


def chosen(info, j, b):
    return (info[j + 1 : j + 2, 0:1] == float(b)).astype(F32)


def mask_row(info, slots):
    b = (lax.broadcasted_iota(jnp.int32, (1, ROWS), 1) >> 7).astype(F32)
    mask = jnp.zeros((1, ROWS), F32)
    for j in slots:
        mask = jnp.where(info[j + 1 : j + 2, :] == b, 1.0, mask)
    return mask


def slot(attn, j):
    return attn[ROWS + j * BLOCK : ROWS + (j + 1) * BLOCK, :].astype(F32)


def put_pieces(pos, pieces, which, weight):
    x, y, c = pos[0], pos[2], pos[3]
    for piece, k in zip(pieces, which):
        for i in range(4):
            xx = (x + jnp.where(c == 0, i, k)) & 3
            yy = (y + jnp.where(c == 0, k, i)) & 3
            for j in range(4):
                row = pl.multiple_of((xx * 4 + j) * PART + yy * CHIP, CHIP)
                at = (i * 4 + j) * CHIP
                weight[pl.ds(row, CHIP), :] = piece[at : at + CHIP, :]


def near_kernel(pos, own, ahead, behind, weight):
    put_pieces(pos, (own, ahead, behind), (0, 1, 3), weight)


def along_kernel(pos, info, info_o, attn, attn_o, base, router, far, weight_in, weight, heads, out):
    put_pieces(pos, (far,), (2,), weight)
    r = jnp.sum(jnp.dot(split3(router[...]), weight[...], preferred_element_type=F32), axis=0, keepdims=True)
    heads[...] = r
    for n, (i, a) in enumerate(((info, attn), (info_o, attn_o))):
        along0 = jnp.sum(a[:ROWS, :].astype(F32) * r, axis=1, keepdims=True)
        parts = [jnp.sum(slot(a, j) * r, axis=1, keepdims=True) for j in range(2)]
        along1 = jnp.concatenate(
            [chosen(i, 0, b) * parts[0] + chosen(i, 1, b) * parts[1] for b in range(NB)], axis=0
        )
        rows = to_rows([along0, along1])
        if n == 0:
            first = jnp.concatenate([jnp.zeros((2, ROWS), F32), base[0:1, :], jnp.zeros((5, ROWS), F32)], axis=0)
            rows = rows + first
        out[:, n * ROWS : (n + 1) * ROWS] = rows


def quad_sum(n, sums, by_t, by_c, by_ct):
    cols = slice(n * ROWS, (n + 1) * ROWS)
    swapped = slice((1 - n) * ROWS, (2 - n) * ROWS)
    return (sums[:, cols] + by_t[:, cols]) + (by_c[:, swapped] + by_ct[:, swapped])


def scaled_kernel(info, info_o, attn, attn_o, sums, by_t, by_c, by_ct, gates, scaled):
    for n, (i, a) in enumerate(((info, attn), (info_o, attn_o))):
        cols = slice(n * ROWS, (n + 1) * ROWS)
        both = quad_sum(n, sums, by_t, by_c, by_ct)
        along0, along1, base = both[0:1], both[1:2], both[2:3]
        gate0 = jax.nn.sigmoid(base)
        logit1 = base + gate0 * along0
        gate1 = jax.nn.sigmoid(logit1)
        gate2 = jax.nn.sigmoid(logit1 + mask_row(i, (0, 1)) * gate1 * along1)
        rows = jnp.concatenate([gate0, gate1, gate2, along0, along1, jnp.zeros((3, ROWS), F32)], axis=0)
        gates[:, cols] = rows
        columns = to_columns(rows)
        for b in range(NB):
            at = slice(b * BLOCK, (b + 1) * BLOCK)
            g = columns[at]
            total = (g[:, 0:1] * a[at, :].astype(F32)).astype(BF16).astype(F32)
            for j in range(3):
                w = g[:, 1:2] if j < 2 else g[:, 2:3]
                total = total + chosen(i, j, b) * (w * slot(a, j)).astype(BF16).astype(F32)
            scaled[n * ROWS + b * BLOCK : n * ROWS + (b + 1) * BLOCK, :] = total.astype(BF16)


def term_kernel(pos, *refs):
    mine, other, scaled, outs, later, lhs = refs[:4], refs[4:8], refs[8], refs[9:-2], refs[-2], refs[-1]
    x, y, c, t = pos[0], pos[2], pos[3], pos[4]
    for k in range(8):
        later[k] = pos[k]
    for out, k in zip(outs, (1, 3, 2) if len(outs) == 3 else (0,)):
        xx = (x + k) & 3
        for n in range(4):
            half = t if n < 2 else 1 - t

            @pl.when(c == 0)
            def _():
                for g in range(4):
                    row = pl.multiple_of(g * PART + ((y + k) & 3) * CHIP, CHIP)
                    at = slice(n * PART + g * CHIP, n * PART + (g + 1) * CHIP)
                    lhs[at, :ROWS] = mine[n][pl.ds(row, CHIP), :]
                    lhs[at, ROWS:] = other[n][pl.ds(row, CHIP), :]

            @pl.when((c == 1) & (xx == 2 * half + n % 2))
            def _():
                lhs[:, :ROWS] = mine[n][...]
                lhs[:, ROWS:] = other[n][...]

        for h in range(4):
            at = slice(h * 256, (h + 1) * 256)
            got = jnp.dot(lhs[at, :], scaled[...], preferred_element_type=F32)
            out[at, :] = got.astype(out.dtype)


def cut_kernel(pos, *refs):
    parts, outs = refs[:4], refs[4:8]
    x, y, c, t = pos[0], pos[2], pos[3], pos[4]
    for k in range(4):
        xx, yy = (x + k) & 3, (y + k) & 3
        for j in range(4):
            left = ((xx >> 1) ^ t) * 512 + (xx & 1) * PART + j * CHIP
            row = pl.multiple_of(jnp.where(c == 0, left, j * PART + yy * CHIP), CHIP)
            total = parts[0][pl.ds(row, CHIP), :]
            for part in parts[1:]:
                total = total + part[pl.ds(row, CHIP), :].astype(F32)
            outs[k][j * CHIP : (j + 1) * CHIP, :] = total.astype(outs[k].dtype)


def cut_last_kernel(pos, *refs):
    parts, outs, tmp = refs[:4], refs[4:8], refs[8]
    z = pos[1]
    total = parts[0][...]
    for part in parts[1:]:
        total = total + part[...].astype(F32)
    tmp[...] = total
    for k in range(4):
        row = pl.multiple_of(((z + k) & 3) * CHIP, CHIP)
        outs[k][...] = tmp[pl.ds(row, CHIP), :].astype(outs[k].dtype)


def proj_kernel(pos, *refs):
    mine, other, weight, keep, send = refs[:4], refs[4:8], refs[8], refs[9], refs[10]
    t = pos[4]
    for out, grads in ((send, other), (keep, mine)):
        for cols in (slice(0, 256), slice(256, 512)):
            total = 0.0
            for n in range(4):
                half = t if n < 2 else 1 - t
                rows = pl.ds(pl.multiple_of((2 * half + n % 2) * CHUNK, CHUNK), CHUNK)
                total = total + lax.dot_general(
                    grads[n][...], weight[rows, cols], (((0,), (0,)), ((), ())), preferred_element_type=F32
                )
            out[:, cols] = total


def match_kernel(info, info_o, attn, attn_o, keep, send, out):
    for n, (i, a, p) in enumerate(((info, attn, keep), (info_o, attn_o, send))):
        columns = [jnp.sum(a[:ROWS, :].astype(F32) * p[...], axis=1, keepdims=True)]
        for slots in ((0, 1), (2,)):
            parts = []
            for b in range(NB):
                value = sum(chosen(i, j, b) * slot(a, j) for j in slots)
                parts.append(jnp.sum(value * p[b * BLOCK : (b + 1) * BLOCK, :], axis=1, keepdims=True))
            columns.append(jnp.concatenate(parts, axis=0))
        out[:, n * ROWS : (n + 1) * ROWS] = to_rows(columns)


def slope_kernel(pos, info, info_o, attn, attn_o, gates, sums, by_t, by_c, by_ct, hidden, weight, out, vector):
    heads = 0.0
    for n, (i, a) in enumerate(((info, attn), (info_o, attn_o))):
        cols = slice(n * ROWS, (n + 1) * ROWS)
        both = quad_sum(n, sums, by_t, by_c, by_ct)
        match0, match1, match2 = both[0:1], both[1:2], both[2:3]
        g = gates[:, cols]
        gate0, gate1, gate2, along0, along1 = g[0:1], g[1:2], g[2:3], g[3:4], g[4:5]
        slope2 = mask_row(i, (2,)) * match2 * gate2 * (1.0 - gate2)
        slope1 = mask_row(i, (0, 1)) * (match1 + slope2 * along1) * gate1 * (1.0 - gate1)
        later0 = slope1 + slope2
        slope0 = (match0 + later0 * along0) * gate0 * (1.0 - gate0)
        total = later0 + slope0
        rows = jnp.concatenate(
            [gate0, gate1, gate2, later0, slope2, total, later0 * gate0, gate1 * slope2], axis=0
        )
        columns = to_columns(rows)
        heads = heads + jnp.sum(columns[:, 6:7] * a[:ROWS, :].astype(F32), axis=0, keepdims=True)
        for j in range(2):
            w = sum(chosen(i, j, b) * columns[b * BLOCK : (b + 1) * BLOCK, 7:8] for b in range(NB))
            heads = heads + jnp.sum(w * slot(a, j), axis=0, keepdims=True)
        if n == 0:
            out[...] = rows
            hid = jnp.sum(columns[:, 5:6] * hidden[...].astype(F32), axis=0, keepdims=True)
    vector[:, :HALF] = heads
    got = lax.dot_general(split3(heads), weight[...], (((1,), (1,)), ((), ())), preferred_element_type=F32)
    term = jnp.sum(got, axis=0, keepdims=True)
    for n in range(2):
        part = term[:, n * WIDTH : (n + 1) * WIDTH] + jnp.where(pos[4] == n, hid, 0.0)
        vector[:, HALF + n * WIDTH : HALF + (n + 1) * WIDTH] = part


def split3(v):
    a = v.astype(BF16)
    rest = v - a.astype(F32)
    b = rest.astype(BF16)
    d = (rest - b.astype(F32)).astype(BF16)
    return jnp.concatenate([a, b, d, jnp.zeros((13, v.shape[1]), BF16)], axis=0)


def block_kernel(pos, own, ahead, far, behind, block, later):
    z = pos[1]
    for k, part in enumerate((own, ahead, far, behind)):
        block[pl.ds(pl.multiple_of(((z + k) & 3) * CHIP, CHIP), CHIP), :] = part[...]
    for k in range(8):
        later[k] = pos[k]


def attn_kernel(pos, first, second, third, hidden, router, attn, give, base):
    base[...] = to_rows([jnp.sum(hidden[...].astype(F32) * router[...], axis=1, keepdims=True)])
    c = pos[3]
    for out, half in ((attn, c), (give, 1 - c)):
        cols = pl.ds(pl.multiple_of(half * HALF, HALF), HALF)
        out[:ROWS, :] = first[:, cols]
        out[ROWS : ROWS + 2 * BLOCK, :] = second[:, cols]
        out[ROWS + 2 * BLOCK :, :] = third[:, cols]


def plane_kernel(own, ahead, far, behind, out):
    for k, part in enumerate((own, ahead, far, behind)):
        out[k * PART : (k + 1) * PART, :] = part[...]


def final_kernel(pos, own, ahead, far, behind, router, heads, mine, other):
    total = own[...] + (ahead[...].astype(F32) + far[...].astype(F32) + behind[...].astype(F32))
    scale = float(ROWS * NF) ** (-0.5)
    total = (total + router[...] * heads[...]) * scale
    low, high = total[:SPAN].astype(BF16), total[SPAN:].astype(BF16)
    mine[...] = jnp.where(pos[3] == 0, low, high)
    other[...] = jnp.where(pos[3] == 0, high, low)


def grads_kernel(pos, kept2, kept3, rows, keep, sent, heads, heads_o, grad, router, gin, g1, g2, g3, proj, line):
    columns = to_columns(rows[...])
    gin[...] = (grad[...].astype(F32) + columns[:, 5:6] * router[...]).astype(BF16)
    c = pos[3]
    for half, part, head in ((c, keep, heads), (1 - c, sent, heads_o)):
        at = pl.ds(pl.multiple_of(half * HALF, HALF), HALF)
        proj[:, at] = part[...]
        line[:, at] = head[...]
    r = line[...]
    g1[...] = (columns[:, 0:1] * (proj[...] + columns[:, 3:4] * r)).astype(BF16)

    def at_slot(kept, j):
        safe = jnp.maximum(kept[0, j], 0)
        live = (kept[0, j] >= 0).astype(F32)
        col = jnp.zeros((BLOCK, 128), F32)
        for b in range(NB):
            col = jnp.where(safe == b, columns[b * BLOCK : (b + 1) * BLOCK], col)
        return proj[pl.ds(pl.multiple_of(safe * BLOCK, BLOCK), BLOCK), :], col, live

    for j in range(2):
        p, col, live = at_slot(kept2, j)
        v = live * col[:, 1:2] * (p + col[:, 4:5] * r)
        g2[j * BLOCK : (j + 1) * BLOCK, :] = v.astype(BF16)
    p, col, live = at_slot(kept3, 0)
    g3[...] = (live * col[:, 2:3] * p).astype(BF16)


def local(
    hidden_in,
    attn_first,
    attn_second,
    attn_third,
    out_weight,
    router,
    kept_second,
    kept_third,
    grad_out,
):
    x, z, y, c, t = (lax.axis_index(a) for a in "xzyct")
    f = ((x * NZ + z) * NY + y) * NC + c
    pos = jnp.stack([x, z, y, c, t, t, t, t]).astype(jnp.int32)
    router_part = lax.dynamic_slice_in_dim(router, t * WIDTH, WIDTH, 0).reshape(1, WIDTH)

    router_chip = lax.dynamic_slice_in_dim(router, f // NC * CHIP, CHIP, 0).reshape(CHIP, 1)

    own_half, other_half, info = call(
        halves_kernel, [((SPAN, HALF), BF16)] * 2 + [((8, 2 * ROWS), F32)], [],
        pos, kept_second, kept_third, out_weight,
    )
    own = call(chip_kernel, ((CHIP, HALF), BF16), [], pos, own_half, shifted(other_half, "c", 1))
    zs = [shifted(own, "z", k) for k in (1, 2, 3)]
    low, high = call(split_kernel, [((CHUNK, ROWS), BF16)] * 2, [], grad_out)
    info = lax.psum(info, "c")
    zs, info, low, high = tie(zs, info, low, high)
    low_t = swap_tp(low)
    block, later = call(block_kernel, [((PART, HALF), BF16), ((8,), jnp.int32)], [], pos, own, *zs)

    blocks = [crossed(block, "xy", k) for k in (1, 3, 2)]
    attn, give, base = call(
        attn_kernel, [((2 * ROWS, HALF), BF16)] * 2 + [((8, ROWS), F32)], [],
        later, attn_first, attn_second, attn_third, hidden_in, router_part,
    )
    low_o = shifted(low, "c", 1)
    blocks, attn, give, low_o, high = tie(blocks, attn, give, low_o, high)
    plane = call(plane_kernel, ((CHUNK, HALF), BF16), [], block, blocks[0], blocks[2], blocks[1])
    info_o = jnp.where(c == 0, info[:, ROWS:], info[:, :ROWS])
    info = jnp.where(c == 0, info[:, :ROWS], info[:, ROWS:])

    planes = [crossed(plane, "yx", k) for k in (1, 3, 2)]
    low_t, high = tie(low_t, high)
    high_t = swap_tp(high)
    low_to, high_o, attn_o = shifted(low_t, "c", 1), shifted(high, "c", 1), shifted(give, "c", 1)
    high_to = shifted(high_t, "c", 1)
    weight = call(near_kernel, ((2 * WIDTH, HALF), BF16), [], pos, plane, planes[0], planes[1])
    planes, weight, attn_o, high_t, low_to, high_o, high_to = tie(
        planes, weight, attn_o, high_t, low_to, high_o, high_to
    )
    side = (info, info_o, attn, attn_o)
    grads = (low, high, low_t, high_t, low_o, high_o, low_to, high_to)

    weight, heads, sums = call(
        along_kernel, [((2 * WIDTH, HALF), BF16), ((1, HALF), F32), ((8, 2 * ROWS), F32)], [],
        pos, *side, base, router.reshape(1, 2 * WIDTH), planes[2], weight, alias={8: 0},
    )
    others, heads_o = quad(sums), shifted(heads, "c", 1)
    keep, send = call(proj_kernel, [((ROWS, HALF), F32)] * 2, [], pos, *grads, weight)
    others, heads_o, keep, send = tie(others, heads_o, keep, send)
    gates, scaled = call(
        scaled_kernel, [((8, 2 * ROWS), F32), ((2 * ROWS, HALF), BF16)], [], *side, sums, *others
    )
    sums = call(match_kernel, ((8, 2 * ROWS), F32), [], *side, keep, send)
    sums, scaled = tie(sums, scaled)
    others = quad(sums)

    kinds = [F32, BF16, BF16, BF16]
    *terms, later = call(
        term_kernel, [((CHUNK, HALF), BF16)] * 3 + [((8,), jnp.int32)],
        [((CHUNK, 2 * ROWS), BF16)], pos, *grads, scaled,
    )
    sent = shifted(send, "c", 1)
    terms, others, sent, later = tie(terms, others, sent, later)
    got = [crossed(terms[n], "yx", -k) for n, k in enumerate((1, 3, 2))]
    rows, vector = call(
        slope_kernel, [((8, ROWS), F32), ((1, HALF + 2 * WIDTH), F32)], [],
        later, *side, gates, sums, *others, hidden_in, weight,
    )
    term, _ = call(
        term_kernel, [((CHUNK, HALF), F32), ((8,), jnp.int32)],
        [((CHUNK, 2 * ROWS), BF16)], later, *grads, scaled,
    )
    vector = fly_step(fly_step(fly_step(vector.reshape(-1), "x", 1), "x", 2), "y", 1)
    got, vector, term = tie(got, vector, term)
    cuts = call(
        cut_kernel, [((PART, HALF), k) for k in kinds], [], pos, term, *got
    )
    got = [crossed(cuts[k], "xy", -k) for k in (1, 3, 2)]
    vector = fly_step(fly_step(vector, "y", 2), "z", 1)
    got, vector, rows = tie(got, vector, rows)
    cuts = call(
        cut_last_kernel, [((CHIP, HALF), k) for k in kinds], [((PART, HALF), F32)], pos, cuts[0], *got
    )
    cuts, vector, rows = tie(cuts, vector, rows)
    got = [shifted(cuts[k], "z", -k) for k in (1, 2, 3)]
    grads = call(
        grads_kernel,
        [((ROWS, WIDTH), BF16), ((ROWS, HEADS), BF16), ((2 * BLOCK, HEADS), BF16), ((BLOCK, HEADS), BF16)],
        [((ROWS, HEADS), F32), ((1, HEADS), F32)],
        pos, kept_second, kept_third, rows, keep, sent, heads, heads_o, grad_out, router_part,
    )
    vector = fly_step(vector, "z", 2)
    got, grads, vector = tie(got, grads, vector)
    heads_total, vector = vector[:HALF].reshape(1, HALF), vector[HALF:]
    mine, other = call(
        final_kernel, [((SPAN, HALF), BF16)] * 2, [], pos, cuts[0], *got, router_chip, heads_total
    )
    other = shifted(other, "c", 1)
    weight_grad = jnp.where(
        c == 0, jnp.concatenate([mine, other], axis=1), jnp.concatenate([other, mine], axis=1)
    )
    by_t, by_c, by_ct = quad(vector)
    router_grad = ((vector + by_t) + (by_c + by_ct)) * float(ROWS * NF) ** (-0.5)
    return (*grads, weight_grad, router_grad)


def solution(mesh):
    fine = jax.sharding.Mesh(mesh.devices.reshape(NX, NZ, NY, NC, 2), ("x", "z", "y", "c", "t"))
    rows = ("x", "z", "y", "c")
    both, lists = P(rows, "t"), P(rows, None)
    return jax.shard_map(
        local,
        mesh=fine,
        in_specs=(both, both, both, both, both, P(), lists, lists, both),
        out_specs=(both, both, both, both, both, P()),
        check_vma=False,
    )
```

```python
import jax
import jax.numpy as jnp
from jax import lax
from jax.experimental import pallas as pl
from jax.experimental.pallas import tpu as pltpu
from jax.sharding import PartitionSpec as P

NB = 3
NX, NZ, NY, NC = 4, 4, 4, 2
NF = NX * NZ * NY * NC
F32, BF16 = jnp.float32, jnp.bfloat16
ROWS, WIDTH, HEADS = 384, 2048, 1024
BLOCK = ROWS // NB
DEPTH = WIDTH // 2
HALF = HEADS // 2
SPAN = 32
CHIP = 2 * SPAN
PART = 4 * CHIP
CHUNK = 4 * PART
SIZES = {"x": NX, "z": NZ, "y": NY, "c": NC, "t": 2}
VMEM = pl.BlockSpec(memory_space=pltpu.VMEM)
SMEM = pl.BlockSpec(memory_space=pltpu.SMEM)


def shifted(v, axis, step):
    n = SIZES[axis]
    return lax.ppermute(v, axis, [((i + step) % n, i) for i in range(n)])


def paired(v, axis, bit):
    return lax.ppermute(v, axis, [(i ^ bit, i) for i in range(SIZES[axis])])


def crossed(v, axes, step):
    pairs = []
    for i in range(NX * NY * NC):
        at = {"x": i // (NY * NC), "y": i // NC % NY, "c": i % NC}
        axis = axes[at["c"]]
        at[axis] = (at[axis] + step) % 4
        pairs.append(((at["x"] * NY + at["y"]) * NC + at["c"], i))
    return lax.ppermute(v, ("x", "y", "c"), pairs)


def swap_tp(v):
    return shifted(v, "t", 1)


def tie(*groups):
    return lax.optimization_barrier(groups)


def fly_step(v, axis, bit):
    return v + paired(v, axis, bit)


def quad(v):
    return swap_tp(v), shifted(v, "c", 1), lax.ppermute(v, ("c", "t"), [(3 - i, i) for i in range(4)])


def call(kernel, outs, scratch, *args, alias=None):
    def spec(dtype):
        return SMEM if dtype == jnp.int32 else VMEM

    single = not isinstance(outs, list)
    shapes = [jax.ShapeDtypeStruct(s, d) for s, d in ([outs] if single else outs)]
    got = pl.pallas_call(
        kernel,
        out_shape=shapes,
        in_specs=[spec(a.dtype) for a in args],
        out_specs=[spec(s.dtype) for s in shapes],
        scratch_shapes=[pltpu.VMEM(s, d) for s, d in scratch],
        input_output_aliases=alias or {},
        compiler_params=pltpu.CompilerParams(vmem_limit_bytes=12 * 2**20),
        cost_estimate=pl.CostEstimate(flops=1, bytes_accessed=1, transcendentals=0),
    )(*args)
    return got[0] if single else got


def halves_kernel(pos, kept2, kept3, weight, mine, other, info):
    c = pos[3]
    mine[...] = weight[:, pl.ds(pl.multiple_of(c * HALF, HALF), HALF)]
    other[...] = weight[:, pl.ds(pl.multiple_of((1 - c) * HALF, HALF), HALF)]
    rows = jnp.zeros((8, ROWS), F32)
    at = lax.broadcasted_iota(jnp.int32, (8, ROWS), 0)
    for k, value in enumerate((kept2[0, 0], kept2[0, 1], kept3[0, 0])):
        rows = jnp.where(at == k + 1, value.astype(F32), rows)
    info[:, :ROWS] = jnp.where(c == 0, rows, 0.0)
    info[:, ROWS:] = jnp.where(c == 0, 0.0, rows)


def chip_kernel(pos, mine, other, out):
    c = pos[3]
    out[pl.ds(pl.multiple_of(c * SPAN, SPAN), SPAN), :] = mine[...]
    out[pl.ds(pl.multiple_of((1 - c) * SPAN, SPAN), SPAN), :] = other[...]


def split_kernel(grad, low, high):
    row = lax.broadcasted_iota(jnp.int32, (256, 256), 0)
    col = lax.broadcasted_iota(jnp.int32, (256, 256), 1)
    same = (row == col).astype(F32).astype(BF16)
    for k in range(WIDTH // 256):
        piece = grad[:, k * 256 : (k + 1) * 256]
        got = lax.dot_general(same, piece, (((1,), (1,)), ((), ())), preferred_element_type=F32)
        out = low if k < 4 else high
        out[(k % 4) * 256 : (k % 4 + 1) * 256, :] = got.astype(BF16)


def to_rows(columns):
    lane = lax.broadcasted_iota(jnp.int32, (ROWS, 128), 1)
    wide = jnp.zeros((ROWS, 128), F32)
    for k, column in enumerate(columns):
        wide = jnp.where(lane == k, column, wide)
    return wide.T[:8]


def to_columns(rows):
    wide = jnp.concatenate([rows, jnp.zeros((128 - rows.shape[0], ROWS), F32)], axis=0)
    return wide.T


def chosen(info, j, b):
    return (info[j + 1 : j + 2, 0:1] == float(b)).astype(F32)


def mask_row(info, slots):
    b = (lax.broadcasted_iota(jnp.int32, (1, ROWS), 1) >> 7).astype(F32)
    mask = jnp.zeros((1, ROWS), F32)
    for j in slots:
        mask = jnp.where(info[j + 1 : j + 2, :] == b, 1.0, mask)
    return mask


def slot(attn, j):
    return attn[ROWS + j * BLOCK : ROWS + (j + 1) * BLOCK, :].astype(F32)


def put_pieces(pos, pieces, which, weight):
    x, y, c = pos[0], pos[2], pos[3]
    for piece, k in zip(pieces, which):
        for i in range(4):
            xx = (x + jnp.where(c == 0, i, k)) & 3
            yy = (y + jnp.where(c == 0, k, i)) & 3
            for j in range(4):
                row = pl.multiple_of((xx * 4 + j) * PART + yy * CHIP, CHIP)
                at = (i * 4 + j) * CHIP
                weight[pl.ds(row, CHIP), :] = piece[at : at + CHIP, :]


def near_kernel(pos, own, ahead, behind, weight):
    put_pieces(pos, (own, ahead, behind), (0, 1, 3), weight)


def along_kernel(pos, info, info_o, attn, attn_o, base, router, far, weight_in, weight, heads, out):
    put_pieces(pos, (far,), (2,), weight)
    r = jnp.sum(jnp.dot(split3(router[...]), weight[...], preferred_element_type=F32), axis=0, keepdims=True)
    heads[...] = r
    for n, (i, a) in enumerate(((info, attn), (info_o, attn_o))):
        along0 = jnp.sum(a[:ROWS, :].astype(F32) * r, axis=1, keepdims=True)
        parts = [jnp.sum(slot(a, j) * r, axis=1, keepdims=True) for j in range(2)]
        along1 = jnp.concatenate(
            [chosen(i, 0, b) * parts[0] + chosen(i, 1, b) * parts[1] for b in range(NB)], axis=0
        )
        rows = to_rows([along0, along1])
        if n == 0:
            first = jnp.concatenate([jnp.zeros((2, ROWS), F32), base[0:1, :], jnp.zeros((5, ROWS), F32)], axis=0)
            rows = rows + first
        out[:, n * ROWS : (n + 1) * ROWS] = rows


def quad_sum(n, sums, by_t, by_c, by_ct):
    cols = slice(n * ROWS, (n + 1) * ROWS)
    swapped = slice((1 - n) * ROWS, (2 - n) * ROWS)
    return (sums[:, cols] + by_t[:, cols]) + (by_c[:, swapped] + by_ct[:, swapped])


def scaled_kernel(info, info_o, attn, attn_o, sums, by_t, by_c, by_ct, gates, scaled):
    for n, (i, a) in enumerate(((info, attn), (info_o, attn_o))):
        cols = slice(n * ROWS, (n + 1) * ROWS)
        both = quad_sum(n, sums, by_t, by_c, by_ct)
        along0, along1, base = both[0:1], both[1:2], both[2:3]
        gate0 = jax.nn.sigmoid(base)
        logit1 = base + gate0 * along0
        gate1 = jax.nn.sigmoid(logit1)
        gate2 = jax.nn.sigmoid(logit1 + mask_row(i, (0, 1)) * gate1 * along1)
        rows = jnp.concatenate([gate0, gate1, gate2, along0, along1, jnp.zeros((3, ROWS), F32)], axis=0)
        gates[:, cols] = rows
        columns = to_columns(rows)
        for b in range(NB):
            at = slice(b * BLOCK, (b + 1) * BLOCK)
            g = columns[at]
            total = (g[:, 0:1] * a[at, :].astype(F32)).astype(BF16).astype(F32)
            for j in range(3):
                w = g[:, 1:2] if j < 2 else g[:, 2:3]
                total = total + chosen(i, j, b) * (w * slot(a, j)).astype(BF16).astype(F32)
            scaled[n * ROWS + b * BLOCK : n * ROWS + (b + 1) * BLOCK, :] = total.astype(BF16)


def term_kernel(pos, *refs):
    mine, other, scaled, outs, later, lhs = refs[:4], refs[4:8], refs[8], refs[9:-2], refs[-2], refs[-1]
    x, y, c, t = pos[0], pos[2], pos[3], pos[4]
    for k in range(8):
        later[k] = pos[k]
    for out, k in zip(outs, (1, 3, 2) if len(outs) == 3 else (0,)):
        xx = (x + k) & 3
        for n in range(4):
            half = t if n < 2 else 1 - t

            @pl.when(c == 0)
            def _():
                for g in range(4):
                    row = pl.multiple_of(g * PART + ((y + k) & 3) * CHIP, CHIP)
                    at = slice(n * PART + g * CHIP, n * PART + (g + 1) * CHIP)
                    lhs[at, :ROWS] = mine[n][pl.ds(row, CHIP), :]
                    lhs[at, ROWS:] = other[n][pl.ds(row, CHIP), :]

            @pl.when((c == 1) & (xx == 2 * half + n % 2))
            def _():
                lhs[:, :ROWS] = mine[n][...]
                lhs[:, ROWS:] = other[n][...]

        for h in range(4):
            at = slice(h * 256, (h + 1) * 256)
            got = jnp.dot(lhs[at, :], scaled[...], preferred_element_type=F32)
            out[at, :] = got.astype(out.dtype)


def cut_kernel(pos, *refs):
    parts, outs = refs[:4], refs[4:8]
    x, y, c, t = pos[0], pos[2], pos[3], pos[4]
    for k in range(4):
        xx, yy = (x + k) & 3, (y + k) & 3
        for j in range(4):
            left = ((xx >> 1) ^ t) * 512 + (xx & 1) * PART + j * CHIP
            row = pl.multiple_of(jnp.where(c == 0, left, j * PART + yy * CHIP), CHIP)
            total = parts[0][pl.ds(row, CHIP), :]
            for part in parts[1:]:
                total = total + part[pl.ds(row, CHIP), :].astype(F32)
            outs[k][j * CHIP : (j + 1) * CHIP, :] = total.astype(outs[k].dtype)


def cut_last_kernel(pos, *refs):
    parts, outs, tmp = refs[:4], refs[4:8], refs[8]
    z = pos[1]
    total = parts[0][...]
    for part in parts[1:]:
        total = total + part[...].astype(F32)
    tmp[...] = total
    for k in range(4):
        row = pl.multiple_of(((z + k) & 3) * CHIP, CHIP)
        outs[k][...] = tmp[pl.ds(row, CHIP), :].astype(outs[k].dtype)


def proj_kernel(pos, *refs):
    mine, other, weight, keep, send = refs[:4], refs[4:8], refs[8], refs[9], refs[10]
    t = pos[4]
    for out, grads in ((send, other), (keep, mine)):
        for cols in (slice(0, 256), slice(256, 512)):
            total = 0.0
            for n in range(4):
                half = t if n < 2 else 1 - t
                rows = pl.ds(pl.multiple_of((2 * half + n % 2) * CHUNK, CHUNK), CHUNK)
                total = total + lax.dot_general(
                    grads[n][...], weight[rows, cols], (((0,), (0,)), ((), ())), preferred_element_type=F32
                )
            out[:, cols] = total


def match_kernel(info, info_o, attn, attn_o, keep, send, out):
    for n, (i, a, p) in enumerate(((info, attn, keep), (info_o, attn_o, send))):
        columns = [jnp.sum(a[:ROWS, :].astype(F32) * p[...], axis=1, keepdims=True)]
        for slots in ((0, 1), (2,)):
            parts = []
            for b in range(NB):
                value = sum(chosen(i, j, b) * slot(a, j) for j in slots)
                parts.append(jnp.sum(value * p[b * BLOCK : (b + 1) * BLOCK, :], axis=1, keepdims=True))
            columns.append(jnp.concatenate(parts, axis=0))
        out[:, n * ROWS : (n + 1) * ROWS] = to_rows(columns)


def slope_kernel(pos, info, info_o, attn, attn_o, gates, sums, by_t, by_c, by_ct, hidden, weight, out, vector):
    heads = 0.0
    for n, (i, a) in enumerate(((info, attn), (info_o, attn_o))):
        cols = slice(n * ROWS, (n + 1) * ROWS)
        both = quad_sum(n, sums, by_t, by_c, by_ct)
        match0, match1, match2 = both[0:1], both[1:2], both[2:3]
        g = gates[:, cols]
        gate0, gate1, gate2, along0, along1 = g[0:1], g[1:2], g[2:3], g[3:4], g[4:5]
        slope2 = mask_row(i, (2,)) * match2 * gate2 * (1.0 - gate2)
        slope1 = mask_row(i, (0, 1)) * (match1 + slope2 * along1) * gate1 * (1.0 - gate1)
        later0 = slope1 + slope2
        slope0 = (match0 + later0 * along0) * gate0 * (1.0 - gate0)
        total = later0 + slope0
        rows = jnp.concatenate(
            [gate0, gate1, gate2, later0, slope2, total, later0 * gate0, gate1 * slope2], axis=0
        )
        columns = to_columns(rows)
        heads = heads + jnp.sum(columns[:, 6:7] * a[:ROWS, :].astype(F32), axis=0, keepdims=True)
        for j in range(2):
            w = sum(chosen(i, j, b) * columns[b * BLOCK : (b + 1) * BLOCK, 7:8] for b in range(NB))
            heads = heads + jnp.sum(w * slot(a, j), axis=0, keepdims=True)
        if n == 0:
            out[...] = rows
            hid = jnp.sum(columns[:, 5:6] * hidden[...].astype(F32), axis=0, keepdims=True)
    vector[:, :HALF] = heads
    got = lax.dot_general(split3(heads), weight[...], (((1,), (1,)), ((), ())), preferred_element_type=F32)
    term = jnp.sum(got, axis=0, keepdims=True)
    for n in range(2):
        part = term[:, n * WIDTH : (n + 1) * WIDTH] + jnp.where(pos[4] == n, hid, 0.0)
        vector[:, HALF + n * WIDTH : HALF + (n + 1) * WIDTH] = part


def split3(v):
    a = v.astype(BF16)
    rest = v - a.astype(F32)
    b = rest.astype(BF16)
    d = (rest - b.astype(F32)).astype(BF16)
    return jnp.concatenate([a, b, d, jnp.zeros((13, v.shape[1]), BF16)], axis=0)


def block_kernel(pos, own, ahead, far, behind, block, later):
    z = pos[1]
    for k, part in enumerate((own, ahead, far, behind)):
        block[pl.ds(pl.multiple_of(((z + k) & 3) * CHIP, CHIP), CHIP), :] = part[...]
    for k in range(8):
        later[k] = pos[k]


def attn_kernel(pos, first, second, third, hidden, router, attn, give, base):
    base[...] = to_rows([jnp.sum(hidden[...].astype(F32) * router[...], axis=1, keepdims=True)])
    c = pos[3]
    for out, half in ((attn, c), (give, 1 - c)):
        cols = pl.ds(pl.multiple_of(half * HALF, HALF), HALF)
        out[:ROWS, :] = first[:, cols]
        out[ROWS : ROWS + 2 * BLOCK, :] = second[:, cols]
        out[ROWS + 2 * BLOCK :, :] = third[:, cols]


def plane_kernel(own, ahead, far, behind, out):
    for k, part in enumerate((own, ahead, far, behind)):
        out[k * PART : (k + 1) * PART, :] = part[...]


def final_kernel(pos, own, ahead, far, behind, router, heads, mine, other):
    total = own[...] + (ahead[...].astype(F32) + far[...].astype(F32) + behind[...].astype(F32))
    scale = float(ROWS * NF) ** (-0.5)
    total = (total + router[...] * heads[...]) * scale
    low, high = total[:SPAN].astype(BF16), total[SPAN:].astype(BF16)
    mine[...] = jnp.where(pos[3] == 0, low, high)
    other[...] = jnp.where(pos[3] == 0, high, low)


def grads_kernel(pos, kept2, kept3, rows, keep, sent, heads, heads_o, grad, router, gin, g1, g2, g3, proj, line):
    columns = to_columns(rows[...])
    gin[...] = (grad[...].astype(F32) + columns[:, 5:6] * router[...]).astype(BF16)
    c = pos[3]
    for half, part, head in ((c, keep, heads), (1 - c, sent, heads_o)):
        at = pl.ds(pl.multiple_of(half * HALF, HALF), HALF)
        proj[:, at] = part[...]
        line[:, at] = head[...]
    r = line[...]
    g1[...] = (columns[:, 0:1] * (proj[...] + columns[:, 3:4] * r)).astype(BF16)

    def at_slot(kept, j):
        safe = jnp.maximum(kept[0, j], 0)
        live = (kept[0, j] >= 0).astype(F32)
        col = jnp.zeros((BLOCK, 128), F32)
        for b in range(NB):
            col = jnp.where(safe == b, columns[b * BLOCK : (b + 1) * BLOCK], col)
        return proj[pl.ds(pl.multiple_of(safe * BLOCK, BLOCK), BLOCK), :], col, live

    for j in range(2):
        p, col, live = at_slot(kept2, j)
        v = live * col[:, 1:2] * (p + col[:, 4:5] * r)
        g2[j * BLOCK : (j + 1) * BLOCK, :] = v.astype(BF16)
    p, col, live = at_slot(kept3, 0)
    g3[...] = (live * col[:, 2:3] * p).astype(BF16)


def local(
    hidden_in,
    attn_first,
    attn_second,
    attn_third,
    out_weight,
    router,
    kept_second,
    kept_third,
    grad_out,
):
    x, z, y, c, t = (lax.axis_index(a) for a in "xzyct")
    f = ((x * NZ + z) * NY + y) * NC + c
    pos = jnp.stack([x, z, y, c, t, t, t, t]).astype(jnp.int32)
    router_part = lax.dynamic_slice_in_dim(router, t * WIDTH, WIDTH, 0).reshape(1, WIDTH)

    router_chip = lax.dynamic_slice_in_dim(router, f // NC * CHIP, CHIP, 0).reshape(CHIP, 1)

    own_half, other_half, info = call(
        halves_kernel, [((SPAN, HALF), BF16)] * 2 + [((8, 2 * ROWS), F32)], [],
        pos, kept_second, kept_third, out_weight,
    )
    own = call(chip_kernel, ((CHIP, HALF), BF16), [], pos, own_half, shifted(other_half, "c", 1))
    zs = [shifted(own, "z", k) for k in (1, 2, 3)]
    low, high = call(split_kernel, [((CHUNK, ROWS), BF16)] * 2, [], grad_out)
    info = lax.psum(info, "c")
    zs, info, low, high = tie(zs, info, low, high)
    low_t = swap_tp(low)
    block, later = call(block_kernel, [((PART, HALF), BF16), ((8,), jnp.int32)], [], pos, own, *zs)

    blocks = [crossed(block, "xy", k) for k in (1, 3, 2)]
    attn, give, base = call(
        attn_kernel, [((2 * ROWS, HALF), BF16)] * 2 + [((8, ROWS), F32)], [],
        later, attn_first, attn_second, attn_third, hidden_in, router_part,
    )
    low_o = shifted(low, "c", 1)
    blocks, attn, give, low_o, high = tie(blocks, attn, give, low_o, high)
    plane = call(plane_kernel, ((CHUNK, HALF), BF16), [], block, blocks[0], blocks[2], blocks[1])
    info_o = jnp.where(c == 0, info[:, ROWS:], info[:, :ROWS])
    info = jnp.where(c == 0, info[:, :ROWS], info[:, ROWS:])

    planes = [crossed(plane, "yx", k) for k in (1, 3, 2)]
    low_t, high = tie(low_t, high)
    high_t = swap_tp(high)
    low_to, high_o, attn_o = shifted(low_t, "c", 1), shifted(high, "c", 1), shifted(give, "c", 1)
    high_to = shifted(high_t, "c", 1)
    weight = call(near_kernel, ((2 * WIDTH, HALF), BF16), [], pos, plane, planes[0], planes[1])
    planes, weight, attn_o, high_t, low_to, high_o, high_to = tie(
        planes, weight, attn_o, high_t, low_to, high_o, high_to
    )
    side = (info, info_o, attn, attn_o)
    grads = (low, high, low_t, high_t, low_o, high_o, low_to, high_to)

    weight, heads, sums = call(
        along_kernel, [((2 * WIDTH, HALF), BF16), ((1, HALF), F32), ((8, 2 * ROWS), F32)], [],
        pos, *side, base, router.reshape(1, 2 * WIDTH), planes[2], weight, alias={8: 0},
    )
    others, heads_o = quad(sums), shifted(heads, "c", 1)
    keep, send = call(proj_kernel, [((ROWS, HALF), F32)] * 2, [], pos, *grads, weight)
    others, heads_o, keep, send = tie(others, heads_o, keep, send)
    gates, scaled = call(
        scaled_kernel, [((8, 2 * ROWS), F32), ((2 * ROWS, HALF), BF16)], [], *side, sums, *others
    )
    sums = call(match_kernel, ((8, 2 * ROWS), F32), [], *side, keep, send)
    sums, scaled = tie(sums, scaled)
    others = quad(sums)

    kinds = [F32, BF16, BF16, BF16]
    *terms, later = call(
        term_kernel, [((CHUNK, HALF), BF16)] * 3 + [((8,), jnp.int32)],
        [((CHUNK, 2 * ROWS), BF16)], pos, *grads, scaled,
    )
    sent = shifted(send, "c", 1)
    terms, others, sent, later = tie(terms, others, sent, later)
    got = [crossed(terms[n], "yx", -k) for n, k in enumerate((1, 3, 2))]
    rows, vector = call(
        slope_kernel, [((8, ROWS), F32), ((1, HALF + 2 * WIDTH), F32)], [],
        later, *side, gates, sums, *others, hidden_in, weight,
    )
    term, _ = call(
        term_kernel, [((CHUNK, HALF), F32), ((8,), jnp.int32)],
        [((CHUNK, 2 * ROWS), BF16)], later, *grads, scaled,
    )
    vector = fly_step(fly_step(fly_step(vector.reshape(-1), "x", 1), "x", 2), "y", 1)
    got, vector, term = tie(got, vector, term)
    cuts = call(
        cut_kernel, [((PART, HALF), k) for k in kinds], [], pos, term, *got
    )
    got = [crossed(cuts[k], "xy", -k) for k in (1, 3, 2)]
    vector = fly_step(fly_step(fly_step(vector, "y", 2), "z", 1), "z", 2)
    got, vector, rows = tie(got, vector, rows)
    cuts = call(
        cut_last_kernel, [((CHIP, HALF), k) for k in kinds], [((PART, HALF), F32)], pos, cuts[0], *got
    )
    cuts, vector, rows = tie(cuts, vector, rows)
    got = [shifted(cuts[k], "z", -k) for k in (1, 2, 3)]
    grads = call(
        grads_kernel,
        [((ROWS, WIDTH), BF16), ((ROWS, HEADS), BF16), ((2 * BLOCK, HEADS), BF16), ((BLOCK, HEADS), BF16)],
        [((ROWS, HEADS), F32), ((1, HEADS), F32)],
        pos, kept_second, kept_third, rows, keep, sent, heads, heads_o, grad_out, router_part,
    )
    heads_total, vector = vector[:HALF].reshape(1, HALF), vector[HALF:]
    vector = vector + swap_tp(vector)
    router_grad = (vector + shifted(vector, "c", 1)) * float(ROWS * NF) ** (-0.5)
    got, grads, router_grad = tie(got, grads, router_grad)
    mine, other = call(
        final_kernel, [((SPAN, HALF), BF16)] * 2, [], pos, cuts[0], *got, router_chip, heads_total
    )
    other = shifted(other, "c", 1)
    weight_grad = jnp.where(
        c == 0, jnp.concatenate([mine, other], axis=1), jnp.concatenate([other, mine], axis=1)
    )
    return (*grads, weight_grad, router_grad)


def solution(mesh):
    fine = jax.sharding.Mesh(mesh.devices.reshape(NX, NZ, NY, NC, 2), ("x", "z", "y", "c", "t"))
    rows = ("x", "z", "y", "c")
    both, lists = P(rows, "t"), P(rows, None)
    return jax.shard_map(
        local,
        mesh=fine,
        in_specs=(both, both, both, both, both, P(), lists, lists, both),
        out_specs=(both, both, both, both, both, P()),
        check_vma=False,
    )
```
